32 devices in a mesh: dp: 16 (over z, x, core), fsdp: 2 (over y).
Axes of the slice: x: 2, y: 2, z: 4, core: 2. Of those that a mesh axis runs over, the one named last changes fastest.
Arguments:
- tokens: bfloat16 [16, 1024, 1536], P('dp', 'fsdp'), may hold values from -6 to 6
- caption: bfloat16 [16, 256, 4096], P('dp', None, 'fsdp'), may hold values from -6 to 6
- modulation: bfloat16 [16, 6, 1536], P('dp', None, 'fsdp'), may hold values from -4 to 4
- caption_mask: int32 [16, 256], P('dp'), may hold values from 0 to 1, as said below
- positions: int32 [16, 2, 1024], P('dp', None, 'fsdp'), may hold values from 0 to 63, as said below
- w_qkv: bfloat16 [1536, 4608], P('fsdp'), may hold values from -0.15625 to 0.15625
- w_out: bfloat16 [1536, 1536], P('fsdp'), may hold values from -0.15625 to 0.15625
- w_caption_kv: bfloat16 [4096, 3072], P('fsdp'), may hold values from -0.09375 to 0.09375
- w_gate_up: bfloat16 [1536, 8192], P('fsdp'), may hold values from -0.15625 to 0.15625
- w_down: bfloat16 [4096, 1536], P('fsdp'), may hold values from -0.09375 to 0.09375
- norm_gains: bfloat16 [6, 1536], P(None, 'fsdp'), may hold values from 0.099609375 to 1.8984375
- caption_gain: bfloat16 [1536], P('fsdp'), may hold values from 0.099609375 to 1.8984375
- cross_gate: bfloat16 [24], P('fsdp'), may hold values from -1.5 to 1.5
- cotangent: bfloat16 [16, 1024, 1536], P('dp', 'fsdp'), may hold values from -6 to 6
Outputs:
- block_out: bfloat16 [16, 1024, 1536], P('dp', 'fsdp')
- grad_tokens: bfloat16 [16, 1024, 1536], P('dp', 'fsdp')
- grad_caption: bfloat16 [16, 256, 4096], P('dp', None, 'fsdp')
- grad_modulation: float32 [16, 6, 1536], P('dp', None, 'fsdp')
- grad_w_qkv: float32 [1536, 4608], P('fsdp', 'dp')
- grad_w_out: float32 [1536, 1536], P('fsdp', 'dp')
- grad_w_caption_kv: float32 [4096, 3072], P('fsdp', 'dp')
- grad_w_gate_up: float32 [1536, 8192], P('fsdp', 'dp')
- grad_w_down: float32 [4096, 1536], P('fsdp', 'dp')
- grad_norm_gains: float32 [6, 1536], P(None, 'fsdp')
- grad_caption_gain: float32 [1536], P('fsdp')
- grad_cross_gate: float32 [24], P('fsdp')
The draws below stay inside these ranges and needn't reach their ends.
Inputs may be any that keep to these rules, and one draw needn't show every extreme that they name: `caption_mask`: each image's row holds ones for its first n slots and zeros after them, with 8 <= n <= 256; some image has n = 256 and some has n = 8. Image i lies on a grid of W_i columns, W_i one of 16, 32, 64: positions[i,0,t] = t // W_i and positions[i,1,t] = t % W_i; both 16 and 64 occur.
All inputs are finite; a program needn't handle non-finite values.
Results may differ from the reference program's by a relative error of at most 0.029.
Values may be sent and summed in bfloat16 or wider, within the bound.
No kernel may reach another device: no remote copies, remote signals or barrier semaphores. Data moves between devices by JAX's collectives and lax.ppermute only.
A program may use at most 512 MiB of HBM per device.

```python
import jax
import jax.numpy as jnp
from jax import lax

D = 1536
HEADS = 24
HEAD_DIM = 64
CAP_D = 4096
FF = 4096
SEQ = 1024
TEXT = 256
IMAGES = 16


def draw_caption_mask(key, part):
    lengths = jax.random.randint(key, (IMAGES,), 8, TEXT + 1)
    lengths = lengths.at[0].set(TEXT).at[1].set(8)
    slots = jnp.arange(TEXT, dtype=jnp.int32)
    return (slots[None, :] < lengths[:, None]).astype(jnp.int32)


def draw_positions(key, part):
    powers = jax.random.randint(key, (IMAGES,), 4, 7)
    powers = powers.at[0].set(4).at[1].set(6)
    widths = jnp.left_shift(jnp.ones_like(powers), powers)
    places = jnp.arange(SEQ, dtype=jnp.int32)
    row_index = places[None, :] // widths[:, None]
    col_index = places[None, :] % widths[:, None]
    return jnp.stack([row_index, col_index], axis=1).astype(jnp.int32)


def level_of(key, shape, pieces, least, top_value):
    def one(axis_at, blocks):
        steps = jax.random.uniform(jax.random.fold_in(jax.random.fold_in(key, 6), axis_at), (blocks,), jnp.float32, least / len(pieces), top_value / len(pieces))
        return jnp.repeat(jnp.exp(steps), shape[axis_at] // blocks).reshape((-1,) + (1,) * (len(shape) - axis_at - 1))

    loudness = one(*pieces[0])
    for cut in pieces[1:]:
        loudness = loudness * one(*cut)
    return loudness


def scatter_about(rng, extent, width, limit, split=(), kind=jnp.bfloat16):
    drawn = width * jax.random.normal(rng, extent, jnp.float32)
    if split:
        drawn = drawn * level_of(rng, extent, split, -0.22, 0.18)
    return jnp.clip(drawn, -limit, limit).astype(kind)


def setup_inputs(seed: int = 0) -> dict:
    key_list = jax.random.split(jax.random.key(seed), 15)
    tokens = scatter_about(key_list[0], (IMAGES, SEQ, D), 1.0, 6.0, ((0, 16), (1, 2)))
    caption = scatter_about(key_list[1], (IMAGES, TEXT, CAP_D), 1.0, 6.0, ((0, 16), (2, 2)))
    modulation = scatter_about(key_list[2], (IMAGES, 6, D), 0.7, 4.0, ((0, 16), (2, 2)))
    caption_mask = draw_caption_mask(jax.random.fold_in(key_list[14], 71), 0)
    positions = draw_positions(jax.random.fold_in(key_list[14], 71), 0)
    w_qkv = scatter_about(key_list[5], (D, 3 * D), D ** -0.5, 0.15625, ((0, 2),))
    w_out = scatter_about(key_list[6], (D, D), D ** -0.5, 0.15625, ((0, 2),))
    w_caption_kv = scatter_about(key_list[7], (CAP_D, 2 * D), CAP_D ** -0.5, 0.09375, ((0, 2),))
    w_gate_up = scatter_about(key_list[8], (D, 2 * FF), D ** -0.5, 0.15625, ((0, 2),))
    w_down = scatter_about(key_list[9], (FF, D), FF ** -0.5, 0.09375, ((0, 2),))
    norm_gains = jnp.clip(1.0 + 0.18 * jax.random.normal(key_list[10], (6, D), jnp.float32), 0.099609375, 1.8984375).astype(jnp.bfloat16)
    caption_gain = jnp.clip(1.0 + 0.18 * jax.random.normal(key_list[11], (D,), jnp.float32), 0.099609375, 1.8984375).astype(jnp.bfloat16)
    cross_gate = jnp.clip(jax.random.uniform(key_list[12], (HEADS,), jnp.float32, -1.5, 1.5) * level_of(key_list[12], (HEADS,), ((0, 2),), -0.4, 0.0), -1.5, 1.5).astype(jnp.bfloat16)
    cotangent = scatter_about(key_list[13], (IMAGES, SEQ, D), 1.0, 6.0, ((0, 16), (1, 2)))
    return {"tokens": tokens, "caption": caption, "modulation": modulation, "caption_mask": caption_mask, "positions": positions, "w_qkv": w_qkv, "w_out": w_out, "w_caption_kv": w_caption_kv, "w_gate_up": w_gate_up, "w_down": w_down, "norm_gains": norm_gains, "caption_gain": caption_gain, "cross_gate": cross_gate, "cotangent": cotangent}


EPS = 1e-05
HIGH = lax.Precision.HIGHEST

@jax.custom_vjp
def low(v):
    return lax.optimization_barrier(v.astype(jnp.bfloat16)).astype(jnp.float32)

@jax.custom_vjp
def low_back(v):
    return v

def low_keep(v):
    return (low(v), None)

def low_pass(kept, grad):
    return (grad,)

def back_keep(v):
    return (v, None)

def back_low(kept, grad):
    return (low(grad),)
low.defvjp(low_keep, low_pass)
low_back.defvjp(back_keep, back_low)

def rms_scale(values):
    return lax.rsqrt(lax.optimization_barrier(jnp.mean(values * values, axis=-1, keepdims=True)) + EPS)

def rope_tables(positions):
    quarter = HEAD_DIM // 4
    frequency = 10000.0 ** (-jnp.arange(quarter, dtype=jnp.float32) / quarter)
    row_angles = positions[..., 0, :].astype(jnp.float32)[..., None] * frequency
    col_angles = positions[..., 1, :].astype(jnp.float32)[..., None] * frequency
    angles = jnp.concatenate([row_angles, col_angles], axis=-1)[..., None, :]
    return (jnp.cos(angles), jnp.sin(angles))

def rotate(values, cosine, sine_table):
    quarter = HEAD_DIM // 4
    shaped = values.reshape(values.shape[:-1] + (HEADS, HEAD_DIM))
    front_part = jnp.concatenate([shaped[..., :quarter], shaped[..., 2 * quarter:3 * quarter]], axis=-1)
    back_part = jnp.concatenate([shaped[..., quarter:2 * quarter], shaped[..., 3 * quarter:]], axis=-1)
    new_front = front_part * cosine - back_part * sine_table
    new_back = front_part * sine_table + back_part * cosine
    joined = jnp.concatenate([new_front[..., :quarter], new_back[..., :quarter], new_front[..., quarter:], new_back[..., quarter:]], axis=-1)
    return joined.reshape(values.shape)

def image_layer(image_items, weights):
    inputs, caption, mods, mask_row, positions = image_items
    qkv_weight, out_weight, caption_weight, gate_up_weight, down_weight, gains, caption_gain, cross_gate = weights
    hidden = inputs * rms_scale(inputs) * gains[0]
    modulated = low(hidden * (1.0 + mods[1]) + mods[0])
    mixed = low_back(jnp.dot(modulated, qkv_weight, precision=HIGH))
    query_pre = mixed[:, :D]
    key_pre = mixed[:, D:2 * D]
    cosine, sine_table = rope_tables(positions)
    query = low(rotate(query_pre * rms_scale(query_pre) * gains[1], cosine, sine_table))
    keys = low(rotate(key_pre * rms_scale(key_pre) * gains[2], cosine, sine_table))
    values = low(mixed[:, 2 * D:])
    caption_kv = low_back(jnp.dot(caption, caption_weight, precision=HIGH))
    ckey_pre = caption_kv[:, :D]
    caption_keys = low(ckey_pre * rms_scale(ckey_pre) * caption_gain)
    caption_values = low(caption_kv[:, D:])
    scale_factor = HEAD_DIM ** (-0.5)
    query_h = query.reshape(SEQ, HEADS, HEAD_DIM)
    key_h = keys.reshape(SEQ, HEADS, HEAD_DIM)
    value_h = values.reshape(SEQ, HEADS, HEAD_DIM)
    ckey_h = caption_keys.reshape(TEXT, HEADS, HEAD_DIM)
    cvalue_h = caption_values.reshape(TEXT, HEADS, HEAD_DIM)
    scores = low_back(jnp.einsum('qhd,khd->hqk', query_h, key_h, precision=HIGH) * scale_factor)
    weights_self = low(jax.nn.softmax(scores, axis=-1))
    self_out = jnp.einsum('hqk,khd->qhd', weights_self, value_h, precision=HIGH)
    cross_scores = low_back(jnp.einsum('qhd,khd->hqk', query_h, ckey_h, precision=HIGH) * scale_factor)
    cross_scores = jnp.where(mask_row[None, None, :] > 0, cross_scores, -1e+30)
    cross_probs = low(jax.nn.softmax(cross_scores, axis=-1))
    cross_out = low_back(jnp.einsum('hqk,khd->qhd', cross_probs, cvalue_h, precision=HIGH))
    gate_tanh = jnp.tanh(cross_gate)[:, None]
    combined = low(low_back((self_out + gate_tanh * cross_out).reshape(SEQ, D)))
    projected = low_back(jnp.dot(combined, out_weight, precision=HIGH))
    normed = projected * rms_scale(projected) * gains[3]
    middle = inputs + jnp.tanh(mods[2]) * normed
    ffn_hidden = middle * rms_scale(middle) * gains[4]
    ffn_in = low(ffn_hidden * (1.0 + mods[4]) + mods[3])
    gate_up = low_back(jnp.dot(ffn_in, gate_up_weight, precision=HIGH))
    ffn_inner = low(jax.nn.silu(gate_up[:, :FF]) * gate_up[:, FF:])
    down_proj = low_back(jnp.dot(ffn_inner, down_weight, precision=HIGH))
    down_normed = down_proj * rms_scale(down_proj) * gains[5]
    return middle + jnp.tanh(mods[5]) * down_normed

def reference(tokens, caption, modulation, caption_mask, positions, w_qkv, w_out, w_caption_kv, w_gate_up, w_down, norm_gains, caption_gain, cross_gate, cotangent):

    def forward(tokens_f, caption_f, modulation_f, qkv_f, out_f, caption_kv_f, gate_up_f, down_f, gains_f, cgain_f, gate_f):
        weights = (qkv_f, out_f, caption_kv_f, gate_up_f, down_f, gains_f, cgain_f, gate_f)

        def one_image(image_items):
            return image_layer(image_items, weights)
        return lax.map(jax.checkpoint(one_image), (tokens_f, caption_f, modulation_f, caption_mask, positions))
    block_value, pullback = jax.vjp(forward, tokens.astype(jnp.float32), caption.astype(jnp.float32), modulation.astype(jnp.float32), w_qkv.astype(jnp.float32), w_out.astype(jnp.float32), w_caption_kv.astype(jnp.float32), w_gate_up.astype(jnp.float32), w_down.astype(jnp.float32), norm_gains.astype(jnp.float32), caption_gain.astype(jnp.float32), cross_gate.astype(jnp.float32))
    gradients = pullback(cotangent.astype(jnp.float32))
    return (block_value.astype(jnp.bfloat16), gradients[0].astype(jnp.bfloat16), gradients[1].astype(jnp.bfloat16), gradients[2], gradients[3], gradients[4], gradients[5], gradients[6], gradients[7], gradients[8], gradients[9], gradients[10])
```

```python
import functools

import jax
import jax.numpy as jnp
from jax import lax
from jax.experimental import pallas as pl
from jax.experimental.pallas import tpu as pltpu
from jax.sharding import PartitionSpec as P

D = 1536
HEADS = 24
HEAD_DIM = 64
FF = 4096
EPS = 1e-05


def rms_scale(values):
    return lax.rsqrt(jnp.mean(values * values, axis=-1, keepdims=True) + EPS)


def norm_back(grad_normed, values, inv_rms, gain_row):
    scaled_grad = grad_normed * gain_row
    grad_values = inv_rms * scaled_grad - values * inv_rms**3 * jnp.mean(
        scaled_grad * values, axis=-1, keepdims=True
    )
    return (grad_values, grad_normed * values * inv_rms)


def rope_tables(positions):
    lane = jnp.arange(PAIR)
    frequency = 10000.0 ** (-(lane % 16).astype(jnp.float32) / 16)
    places = positions.astype(jnp.float32)
    angles = jnp.where((lane % 64 < 32)[None], places[:, :1], places[:, 1:]) * frequency
    sign = jnp.where(lane % 32 < 16, -1.0, 1.0).astype(jnp.float32)
    return jnp.cos(angles), jnp.sin(angles) * sign


PAIR = 2 * HEAD_DIM
NT = (((1,), (1,)), ((), ()))
TN = (((0,), (0,)), ((), ()))


def head_masks(dtype):
    lane = lax.broadcasted_iota(jnp.int32, (1, PAIR), 1)
    return [(lane < HEAD_DIM).astype(dtype), (lane >= HEAD_DIM).astype(dtype)]


def attend_kernel(q_ref, k_ref, v_ref, ck_ref, cv_ref, bias_ref, gate_ref, a_ref, o_ref, oy_ref, stat_ref):
    masks = head_masks(jnp.float32)
    rows = q_ref.shape[0]
    step = min(rows, 256)
    gate = gate_ref[...]
    for start in range(0, rows, step):
        where = pl.ds(start, step)
        q = q_ref[where, :].astype(jnp.float32) * HEAD_DIM**-0.5
        own, cross, stats = [], [], []
        for mask in masks:
            qm = (q * mask).astype(jnp.bfloat16)
            for keys, values, bias, outs in (
                (k_ref, v_ref, None, own),
                (ck_ref, cv_ref, bias_ref, cross),
            ):
                s = lax.dot_general(qm, keys[...], NT, preferred_element_type=jnp.float32)
                if bias is not None:
                    s = s + bias[...]
                top = jnp.max(s, axis=1, keepdims=True)
                e = jnp.exp(s - top)
                total = jnp.sum(e, axis=1, keepdims=True)
                out = jnp.dot(e.astype(jnp.bfloat16), values[...], preferred_element_type=jnp.float32)
                outs.append(out / total * mask)
                stats.append(top + jnp.log(total))
        o = own[0] + own[1]
        oy = cross[0] + cross[1]
        a_ref[where, :] = (o + gate * oy).astype(jnp.bfloat16)
        o_ref[where, :] = o.astype(jnp.bfloat16)
        oy_ref[where, :] = oy.astype(jnp.bfloat16)
        lane = lax.broadcasted_iota(jnp.int32, (step, PAIR), 1)
        tile = jnp.where(lane == 0, stats[0], jnp.where(lane == 1, stats[1], jnp.where(lane == 2, stats[2], stats[3])))
        stat_ref[0, :, where] = tile.T[:8, :]


def attend(query, key, value, ckey, cvalue, bias_row, gate_lanes):
    rows, keys, slots = query.shape[0], key.shape[0], ckey.shape[0]
    pairs = D // PAIR
    spec = lambda n: pl.BlockSpec((n, PAIR), lambda j: (0, j))
    return pl.pallas_call(
        attend_kernel,
        grid=(pairs,),
        in_specs=[
            spec(rows), spec(keys), spec(keys), spec(slots), spec(slots),
            pl.BlockSpec((1, slots), lambda j: (0, 0)), spec(1),
        ],
        out_specs=[spec(rows)] * 3 + [pl.BlockSpec((1, 8, rows), lambda j: (j, 0, 0))],
        out_shape=[jax.ShapeDtypeStruct((rows, D), jnp.bfloat16)] * 3
        + [jax.ShapeDtypeStruct((pairs, 8, rows), jnp.float32)],
        compiler_params=pltpu.CompilerParams(vmem_limit_bytes=48 * 2**20),
        cost_estimate=cost(16 * rows * (keys + slots) * D, 20e6, HEADS * rows * (keys + slots)),
    )(query, key, value, ckey, cvalue, bias_row, gate_lanes)


def back_part(k_tile, v_tile, bias, qm, grads, deltas, lses):
    masks = head_masks(jnp.bfloat16)
    dk = dv = add = None
    for h in range(2):
        st = dot(k_tile, qm[h], NT)
        if bias is not None:
            st = st + bias
        pt = jnp.exp(st - lses[h])
        dpt = dot(v_tile, grads[h], NT)
        dst = (pt * (dpt - deltas[h])).astype(jnp.bfloat16)
        terms = (
            dot(dst, qm[h]),
            dot(pt.astype(jnp.bfloat16), grads[h]),
            dot(dst, k_tile * masks[h], TN),
        )
        dk, dv, add = terms if h == 0 else (dk + terms[0], dv + terms[1], add + terms[2])
    return dk, dv, add


def head_sums(terms):
    t = terms.T
    return [
        jnp.sum(t[:HEAD_DIM], axis=0, keepdims=True),
        jnp.sum(t[HEAD_DIM:], axis=0, keepdims=True),
    ]


def split_heads(values):
    return [(values * m).astype(jnp.bfloat16) for m in head_masks(jnp.float32)]


def cross_back_kernel(q_ref, ck_ref, cv_ref, bias_ref, gate_ref, stat_ref, da_ref, oy_ref, dq_ref, dck_ref, dcv_ref, gsum_ref):
    qm = split_heads(q_ref[...].astype(jnp.float32) * HEAD_DIM**-0.5)
    da = da_ref[...].astype(jnp.float32)
    doy = (da * gate_ref[...]).astype(jnp.bfloat16).astype(jnp.float32)
    oy = oy_ref[...].astype(jnp.float32)
    gsum_ref[...] = jnp.sum(da * oy, axis=0, keepdims=True)
    stat = stat_ref[0]
    dk, dv, dq = back_part(
        ck_ref[...], cv_ref[...], bias_ref[...], qm, split_heads(doy), head_sums(doy * oy), [stat[1:2], stat[3:4]]
    )
    dck_ref[...] = dk.astype(dck_ref.dtype)
    dcv_ref[...] = dv.astype(dcv_ref.dtype)
    dq_ref[...] = (dq * HEAD_DIM**-0.5).astype(dq_ref.dtype)


def self_back_kernel(q_ref, k_ref, v_ref, stat_ref, da_ref, o_ref, dqc_ref, dq_ref, dk_ref, dv_ref):
    keys = k_ref.shape[0]
    step = min(keys, 256)
    qm = split_heads(q_ref[...].astype(jnp.float32) * HEAD_DIM**-0.5)
    da = da_ref[...].astype(jnp.float32)
    deltas = head_sums(da * o_ref[...].astype(jnp.float32))
    dam = split_heads(da)
    stat = stat_ref[0]
    dq = None
    for start in range(0, keys, step):
        where = pl.ds(start, step)
        dk, dv, add = back_part(k_ref[where, :], v_ref[where, :], None, qm, dam, deltas, [stat[0:1], stat[2:3]])
        dk_ref[where, :] = dk.astype(dk_ref.dtype)
        dv_ref[where, :] = dv.astype(dv_ref.dtype)
        dq = add if dq is None else dq + add
    dq = dq * HEAD_DIM**-0.5 + dqc_ref[...].astype(jnp.float32)
    dq_ref[...] = dq.astype(dq_ref.dtype)


def cross_back(query, ckey, cvalue, bias_col, gate_lanes, stats, grad_a, o_cross):
    rows, slots = query.shape[0], ckey.shape[0]
    pairs = D // PAIR
    spec = lambda n: pl.BlockSpec((n, PAIR), lambda j: (0, j))
    return pl.pallas_call(
        cross_back_kernel,
        grid=(pairs,),
        in_specs=[
            spec(rows), spec(slots), spec(slots),
            pl.BlockSpec((slots, 1), lambda j: (0, 0)), spec(1),
            pl.BlockSpec((1, 8, rows), lambda j: (j, 0, 0)),
            spec(rows), spec(rows),
        ],
        out_specs=[spec(rows), spec(slots), spec(slots), spec(1)],
        out_shape=[jax.ShapeDtypeStruct((n, D), jnp.bfloat16) for n in (rows, slots, slots)]
        + [jax.ShapeDtypeStruct((1, D), jnp.float32)],
        compiler_params=params(48),
        cost_estimate=cost(40 * rows * slots * D, 9e6, HEADS * rows * slots),
    )(query, ckey, cvalue, bias_col, gate_lanes, stats, grad_a, o_cross)


def self_back(query, key, value, stats, grad_a, o_self, dq_cross, first, count):
    rows, keys = query.shape[0], key.shape[0]
    spec = lambda n: pl.BlockSpec((n, PAIR), lambda j: (0, j + first))
    out = lambda n: pl.BlockSpec((n, PAIR), lambda j: (0, j))
    return pl.pallas_call(
        self_back_kernel,
        grid=(count,),
        in_specs=[
            spec(rows), spec(keys), spec(keys),
            pl.BlockSpec((1, 8, rows), lambda j: (j + first, 0, 0)),
            spec(rows), spec(rows), spec(rows),
        ],
        out_specs=[out(rows), out(keys), out(keys)],
        out_shape=[jax.ShapeDtypeStruct((n, count * PAIR), jnp.bfloat16) for n in (rows, keys, keys)],
        compiler_params=params(48),
        cost_estimate=cost(80 * rows * keys * count * PAIR, 1e6 * count, 2 * count * rows * keys),
    )(query, key, value, stats, grad_a, o_self, dq_cross)


NN = (((1,), (0,)), ((), ()))


def dot(a, b, dims=NN):
    return lax.dot_general(a, b, dims, preferred_element_type=jnp.float32)


def chunks(rows, step, body):
    def one(i, carry):
        body(pl.ds(pl.multiple_of(i * step, step), step))
        return carry

    lax.fori_loop(0, rows // step, one, 0)


def add_row(ref, index, terms):
    ref[index : index + 1, :] += jnp.sum(terms, axis=0, keepdims=True)


def partner(values):
    lane = lax.broadcasted_iota(jnp.int32, (values.shape[0], PAIR), 1)
    low = (lane & 31) < 16
    outs = []
    for start in range(0, values.shape[1], PAIR):
        tile = values[:, start : start + PAIR]
        outs.append(jnp.where(low, pltpu.roll(tile, PAIR - 16, 1), pltpu.roll(tile, 16, 1)))
    return jnp.concatenate(outs, axis=1)


def turn(values, cosine, sine):
    count = values.shape[1] // PAIR
    wide = lambda t: jnp.concatenate([t] * count, axis=1)
    return values * wide(cosine) + partner(values) * wide(sine)


def halves(values, which):
    mid = values.shape[1] // 2
    low, high = values[:, :mid], values[:, mid:]
    first = which == 0
    return jnp.where(first, low, high), jnp.where(first, high, low)


def small_spec(shape):
    return pl.BlockSpec(shape, lambda *_: (0,) * len(shape))


def params(mib=56):
    return pltpu.CompilerParams(vmem_limit_bytes=mib * 2**20)


def cost(flops, nbytes, trans=0):
    share = 0.05
    return pl.CostEstimate(
        flops=int(flops * share), bytes_accessed=int(nbytes * share), transcendentals=int(trans * share)
    )


def project_kernel(parts, own_rows, where_ref, tok_ref, gain_ref, mod_ref, cos_ref, sin_ref, own_ref, *refs):
    pieces = refs[:parts]
    hm_ref, full_ref, q_ref, k_ref, v_ref, qpre_ref, kpre_ref, pre_ref = refs[parts:]
    pid = pl.program_id(0)
    rows = tok_ref.shape[0]
    step = min(128, rows)
    tile = full_ref.shape[1]
    per = D // tile

    @pl.when(pid == 0)
    def hidden():
        def body(where):
            x = tok_ref[where, :].astype(jnp.float32)
            hid = x * rms_scale(x) * gain_ref[0:1]
            hm_ref[where, :] = (hid * (1.0 + mod_ref[1:2]) + mod_ref[0:1]).astype(jnp.bfloat16)

        chunks(rows, step, body)

    n = own_ref.shape[0]
    full_ref[pl.ds(pl.multiple_of(where_ref[0], n), n), :] = own_ref[...]
    for i, piece in enumerate(pieces):
        n = piece.shape[0]
        full_ref[pl.ds(pl.multiple_of(where_ref[i + 1], n), n), :] = piece[...]

    for j in range(2 * per):
        count = own_rows if j < per else rows

        @pl.when(pid == j)
        def pre(j=j, count=count):
            pre_ref[:count, (j % per) * tile : (j % per + 1) * tile] = dot(
                hm_ref[:count, :], full_ref[...]
            )

    @pl.when(pid >= 2 * per)
    def value():
        v_ref[...] = dot(hm_ref[...], full_ref[...]).astype(jnp.bfloat16)

    for last, count, out, keep, gain in (
        (per - 1, own_rows, q_ref, qpre_ref, 1),
        (2 * per - 1, rows, k_ref, kpre_ref, 2),
    ):

        @pl.when(pid == last)
        def finish(count=count, out=out, keep=keep, gain=gain):
            def body(where):
                p = pre_ref[where, :]
                n = p * rms_scale(p) * gain_ref[gain : gain + 1]
                out[where, :] = turn(n, cos_ref[where, :], sin_ref[where, :]).astype(jnp.bfloat16)
                keep[where, :] = p.astype(jnp.bfloat16)

            chunks(count, min(step, count), body)


def project(tokens_all, own_rows, gains, mods, cosine, sine, weight, tile=512):
    own, pieces, starts = weight
    rows = tokens_all.shape[0]
    n = 3 * D // tile
    vtile = 2 * D // tile
    outs = [
        ((rows, D), jnp.bfloat16, None),
        ((D, 3 * D), jnp.bfloat16, pl.BlockSpec((D, tile), lambda j, w: (0, j))),
        ((own_rows, D), jnp.bfloat16, None),
        ((rows, D), jnp.bfloat16, None),
        ((rows, D), jnp.bfloat16, pl.BlockSpec((rows, tile), lambda j, w: (0, jnp.maximum(j - vtile, 0)))),
        ((own_rows, D), jnp.bfloat16, None),
        ((rows, D), jnp.bfloat16, None),
    ]
    return pl.pallas_call(
        functools.partial(project_kernel, len(pieces), own_rows),
        grid_spec=pltpu.PrefetchScalarGridSpec(
            num_scalar_prefetch=1,
            grid=(n,),
            in_specs=[small_spec(a.shape) for a in (tokens_all, gains, mods, cosine, sine)]
            + [pl.BlockSpec((p.shape[0], tile), lambda j, w: (0, j)) for p in [own] + pieces],
            out_specs=[s if s is not None else small_spec(shape) for shape, _, s in outs],
            scratch_shapes=[pltpu.VMEM((rows, D), jnp.float32)],
        ),
        out_shape=[jax.ShapeDtypeStruct(shape, d) for shape, d, _ in outs],
        compiler_params=params(58),
        cost_estimate=cost(2 * D * D * (own_rows + 2 * rows), 60e6),
    )(jnp.stack(starts).astype(jnp.int32), tokens_all, gains, mods, cosine, sine, own, *pieces)


def output_kernel(which_ref, a_ref, w0_ref, w1_ref, x_ref, gain_ref, mod_ref, o_ref, mid_ref, hfm_ref):
    a0, a1 = halves(a_ref[...], which_ref[0])
    o = dot(a0, w0_ref[...]) + dot(a1, w1_ref[...])
    o_ref[...] = o.astype(jnp.bfloat16)
    on = o * rms_scale(o) * gain_ref[3:4]
    mid = x_ref[...].astype(jnp.float32) + jnp.tanh(mod_ref[2:3]) * on
    mid_ref[...] = mid
    hf = mid * rms_scale(mid) * gain_ref[4:5]
    hfm_ref[...] = (hf * (1.0 + mod_ref[4:5]) + mod_ref[3:4]).astype(jnp.bfloat16)


def output_step(which, combined, weight, tokens, gains, mods):
    rows = combined.shape[0]
    step = min(rows, 256)
    row_spec = pl.BlockSpec((step, D), lambda i, w: (i, 0))
    return pl.pallas_call(
        output_kernel,
        grid_spec=pltpu.PrefetchScalarGridSpec(
            num_scalar_prefetch=1,
            grid=(rows // step,),
            in_specs=[row_spec, small_spec(weight[0].shape), small_spec(weight[1].shape), row_spec]
            + [small_spec(gains.shape), small_spec(mods.shape)],
            out_specs=[row_spec] * 3,
        ),
        out_shape=[
            jax.ShapeDtypeStruct((rows, D), jnp.bfloat16),
            jax.ShapeDtypeStruct((rows, D), jnp.float32),
            jax.ShapeDtypeStruct((rows, D), jnp.bfloat16),
        ],
        compiler_params=params(),
        cost_estimate=cost(2 * rows * D * D, 15e6),
    )(which, combined, weight[0], weight[1], tokens, gains, mods)


def gate_up_kernel(which_ref, h_ref, g0_ref, g1_ref, u0_ref, u1_ref, ga_ref, up_ref, ff_ref, hs_ref):
    @pl.when(pl.program_id(0) == 0)
    def split():
        hs_ref[0], hs_ref[1] = halves(h_ref[...], which_ref[0])

    ga = dot(hs_ref[0], g0_ref[...]) + dot(hs_ref[1], g1_ref[...])
    up = dot(hs_ref[0], u0_ref[...]) + dot(hs_ref[1], u1_ref[...])
    ga_ref[...] = ga.astype(jnp.bfloat16)
    up_ref[...] = up.astype(jnp.bfloat16)
    ff_ref[...] = (ga / (1.0 + jnp.exp(-ga)) * up).astype(jnp.bfloat16)


def gate_up_step(which, hfm, weight, tile=512):
    rows = hfm.shape[0]
    n = FF // tile
    half = D // 2
    spec = lambda off: pl.BlockSpec((half, tile), lambda j, w: (0, j + off))
    out = pl.BlockSpec((rows, tile), lambda j, w: (0, j))
    return pl.pallas_call(
        gate_up_kernel,
        grid_spec=pltpu.PrefetchScalarGridSpec(
            num_scalar_prefetch=1,
            grid=(n,),
            in_specs=[small_spec(hfm.shape), spec(0), spec(0), spec(n), spec(n)],
            out_specs=[out] * 3,
            scratch_shapes=[pltpu.VMEM((2, rows, half), jnp.bfloat16)],
        ),
        out_shape=[jax.ShapeDtypeStruct((rows, FF), jnp.bfloat16)] * 3,
        compiler_params=params(),
        cost_estimate=cost(4 * rows * D * FF, 40e6, rows * FF),
    )(which, hfm, weight[0], weight[1], weight[0], weight[1])


def down_kernel(which_ref, ff_ref, w0_ref, w1_ref, mid_ref, cot_ref, gain_ref, mod_ref, out_ref, df_ref, sum_ref, f_ref, hs_ref):
    pid = pl.program_id(0)
    tile = w0_ref.shape[1]
    rows = ff_ref.shape[0]

    @pl.when(pid == 0)
    def split():
        hs_ref[0], hs_ref[1] = halves(ff_ref[...], which_ref[0])

    f_ref[pid] = dot(hs_ref[0], w0_ref[...]) + dot(hs_ref[1], w1_ref[...])

    @pl.when(pid == pl.num_programs(0) - 1)
    def finish():
        gate = jnp.tanh(mod_ref[5:6])
        sum_ref[...] = jnp.zeros_like(sum_ref)

        def body(where):
            f = jnp.concatenate([f_ref[j, where, :] for j in range(D // tile)], axis=1)
            rf = rms_scale(f)
            fn = f * rf * gain_ref[5:6]
            dy = cot_ref[where, :].astype(jnp.float32)
            out_ref[where, :] = (mid_ref[where, :] + gate * fn).astype(jnp.bfloat16)
            dfn = dy * gate
            add_row(sum_ref, 0, dy * fn)
            df, terms = norm_back(dfn, f, rf, gain_ref[5:6])
            add_row(sum_ref, 1, terms)
            df_ref[where, :] = df.astype(jnp.bfloat16)

        chunks(rows, min(64, rows), body)


def down_step(which, ffh, weight, middle, cotangent, gains, mods, tile=256):
    rows = ffh.shape[0]
    half = FF // 2
    spec = pl.BlockSpec((half, tile), lambda j, w: (0, j))
    full = small_spec((rows, D))
    return pl.pallas_call(
        down_kernel,
        grid_spec=pltpu.PrefetchScalarGridSpec(
            num_scalar_prefetch=1,
            grid=(D // tile,),
            in_specs=[small_spec(ffh.shape), spec, spec, full, full, small_spec(gains.shape), small_spec(mods.shape)],
            out_specs=[full, full, small_spec((8, D))],
            scratch_shapes=[
                pltpu.VMEM((D // tile, rows, tile), jnp.float32),
                pltpu.VMEM((2, rows, half), jnp.bfloat16),
            ],
        ),
        out_shape=[jax.ShapeDtypeStruct((rows, D), jnp.bfloat16)] * 2
        + [jax.ShapeDtypeStruct((8, D), jnp.float32)],
        compiler_params=params(),
        cost_estimate=cost(2 * rows * D * FF, 24e6),
    )(which, ffh, weight[0], weight[1], middle, cotangent, gains, mods)


def gate_up_back_kernel(which_ref, df_ref, ga_ref, up_ref, d0_ref, d1_ref, dgu_ref):
    pid = pl.program_id(0)
    n = pl.num_programs(0)

    def work(w_ref):
        dffh = dot(df_ref[...], w_ref[...], NT)
        ga = ga_ref[...].astype(jnp.float32)
        up = up_ref[...].astype(jnp.float32)
        s = 1.0 / (1.0 + jnp.exp(-ga))
        dgu_ref[0] = (dffh * up * (s * (1.0 + ga * (1.0 - s)))).astype(jnp.bfloat16)
        dgu_ref[1] = (dffh * (ga * s)).astype(jnp.bfloat16)

    @pl.when(pid < n // 2)
    def first():
        work(d0_ref)

    @pl.when(pid >= n // 2)
    def second():
        work(d1_ref)


def gate_up_back(which, df, ga, up, w_down, tile=512):
    rows = df.shape[0]
    n = FF // tile
    h = n // 2
    cols = pl.BlockSpec((rows, tile), lambda j, w: (0, (j + w[0] * h) % n))
    return pl.pallas_call(
        gate_up_back_kernel,
        grid_spec=pltpu.PrefetchScalarGridSpec(
            num_scalar_prefetch=1,
            grid=(n,),
            in_specs=[
                small_spec((rows, D)), cols, cols,
                pl.BlockSpec((tile, D), lambda j, w: (jnp.minimum(j, h - 1), 0)),
                pl.BlockSpec((tile, D), lambda j, w: (jnp.maximum(j - h, 0), 0)),
            ],
            out_specs=pl.BlockSpec((2, rows, tile), lambda j, w: (0, 0, (j + w[0] * h) % n)),
        ),
        out_shape=jax.ShapeDtypeStruct((2, rows, FF), jnp.bfloat16),
        compiler_params=params(),
        cost_estimate=cost(2 * rows * D * FF, 30e6, rows * FF),
    )(which, df, ga, up, w_down[0], w_down[1])


def ffn_back_kernel(
    which_ref, dgu_ref, g0_ref, g1_ref, u0_ref, u1_ref,
    mid_ref, cot_ref, o_ref, w0_ref, w1_ref, gain_ref, mod_ref,
    dmid_ref, do_ref, da_ref, sum_ref, acc_ref,
):
    pid = pl.program_id(0)
    n = pl.num_programs(0)
    rows = mid_ref.shape[0]
    which = which_ref[0]
    dga, dup = dgu_ref[0], dgu_ref[1]
    p0 = dot(dga, g0_ref[...], NT) + dot(dup, u0_ref[...], NT)
    p1 = dot(dga, g1_ref[...], NT) + dot(dup, u1_ref[...], NT)

    @pl.when(pid == 0)
    def clear():
        acc_ref[which] = p0
        acc_ref[1 - which] = p1

    @pl.when(pid > 0)
    def more():
        acc_ref[which] += p0
        acc_ref[1 - which] += p1

    @pl.when(pid == n - 1)
    def finish():
        sum_ref[...] = jnp.zeros_like(sum_ref)
        gate = jnp.tanh(mod_ref[2:3])

        def body(where):
            dhfm = jnp.concatenate([acc_ref[0, where, :], acc_ref[1, where, :]], axis=1)
            mid = mid_ref[where, :]
            r2 = rms_scale(mid)
            add_row(sum_ref, 0, dhfm)
            add_row(sum_ref, 1, dhfm * (mid * r2 * gain_ref[4:5]))
            dmid, terms = norm_back(dhfm * (1.0 + mod_ref[4:5]), mid, r2, gain_ref[4:5])
            add_row(sum_ref, 2, terms)
            dmid = cot_ref[where, :].astype(jnp.float32) + dmid
            dmid_ref[where, :] = dmid
            o = o_ref[where, :].astype(jnp.float32)
            ro = rms_scale(o)
            add_row(sum_ref, 3, dmid * (o * ro * gain_ref[3:4]))
            do, terms = norm_back(dmid * gate, o, ro, gain_ref[3:4])
            add_row(sum_ref, 4, terms)
            do_ref[where, :] = do.astype(jnp.bfloat16)

        chunks(rows, min(64, rows), body)
        do = do_ref[...]
        q0 = dot(do, w0_ref[...], NT).astype(jnp.bfloat16)
        q1 = dot(do, w1_ref[...], NT).astype(jnp.bfloat16)
        half = q0.shape[1]
        da_ref[:, :half] = jnp.where(which == 0, q0, q1)
        da_ref[:, half:] = jnp.where(which == 0, q1, q0)


def ffn_back(which, dgu, w_gate_up, w_out, middle, cotangent, o, gains, mods, tile=512):
    rows = middle.shape[0]
    n = FF // tile
    half = D // 2
    full = small_spec((rows, D))
    gspec = pl.BlockSpec((half, tile), lambda j, w: (0, j))
    uspec = pl.BlockSpec((half, tile), lambda j, w: (0, j + n))
    return pl.pallas_call(
        ffn_back_kernel,
        grid_spec=pltpu.PrefetchScalarGridSpec(
            num_scalar_prefetch=1,
            grid=(n,),
            in_specs=[
                pl.BlockSpec((2, rows, tile), lambda j, w: (0, 0, j)),
                gspec, gspec, uspec, uspec, full, full, full,
                small_spec(w_out[0].shape), small_spec(w_out[1].shape),
                small_spec(gains.shape), small_spec(mods.shape),
            ],
            out_specs=[full, full, full, small_spec((8, D))],
            scratch_shapes=[pltpu.VMEM((2, rows, half), jnp.float32)],
        ),
        out_shape=[jax.ShapeDtypeStruct((rows, D), jnp.float32)]
        + [jax.ShapeDtypeStruct((rows, D), jnp.bfloat16)] * 2
        + [jax.ShapeDtypeStruct((8, D), jnp.float32)],
        compiler_params=params(60),
        cost_estimate=cost(4 * rows * D * FF + 2 * rows * D * D, 55e6),
    )(
        which, dgu, w_gate_up[0], w_gate_up[1], w_gate_up[0], w_gate_up[1],
        middle, cotangent, o, w_out[0], w_out[1], gains, mods,
    )


def qk_back_kernel(own_blocks, parts, *refs):
    dq_refs, dk_refs, dv_refs = refs[:parts], refs[parts : 2 * parts], refs[2 * parts : 3 * parts]
    qpre_ref, kpre_ref, cos_ref, sin_ref, gain_ref, dqkv_ref, sum_ref = refs[3 * parts :]
    pid = pl.program_id(0)

    @pl.when(pid == 0)
    def clear():
        sum_ref[...] = jnp.zeros_like(sum_ref)

    def back(grad_refs, pre_ref, row):
        pre = pre_ref[...].astype(jnp.float32)
        grad = jnp.concatenate([g[...] for g in grad_refs], axis=1).astype(jnp.float32)
        grad = turn(grad, cos_ref[...], -sin_ref[...])
        d, terms = norm_back(grad, pre, rms_scale(pre), gain_ref[row : row + 1])
        add_row(sum_ref, row, terms)
        return d.astype(jnp.bfloat16)

    dqkv_ref[:, D : 2 * D] = back(dk_refs, kpre_ref, 2)
    width = D // parts
    for i, ref in enumerate(dv_refs):
        dqkv_ref[:, 2 * D + i * width : 2 * D + (i + 1) * width] = ref[...]

    @pl.when(pid < own_blocks)
    def with_query():
        dqkv_ref[:, :D] = back(dq_refs, qpre_ref, 1)

    @pl.when(pid >= own_blocks)
    def no_query():
        dqkv_ref[:, :D] = jnp.zeros((dqkv_ref.shape[0], D), jnp.bfloat16)


def qk_back(dq, dk, dv, qpre, kpre, cosine, sine, gains):
    own, rows = dq[0].shape[0], dk[0].shape[0]
    parts = len(dq)
    step = min(128, own)
    blocks = own // step
    row = lambda n: pl.BlockSpec((step, n), lambda i: (i, 0))
    own_row = lambda n: pl.BlockSpec((step, n), lambda i: (jnp.minimum(i, blocks - 1), 0))
    return pl.pallas_call(
        functools.partial(qk_back_kernel, blocks, parts),
        grid=(rows // step,),
        in_specs=[own_row(D // parts)] * parts + [row(D // parts)] * (2 * parts)
        + [own_row(D), row(D), row(PAIR), row(PAIR), small_spec(gains.shape)],
        out_specs=[row(3 * D), small_spec((8, D))],
        out_shape=[
            jax.ShapeDtypeStruct((rows, 3 * D), jnp.bfloat16),
            jax.ShapeDtypeStruct((8, D), jnp.float32),
        ],
        compiler_params=params(),
        cost_estimate=cost(60 * rows * D, 30e6),
    )(*dq, *dk, *dv, qpre, kpre, cosine, sine, gains)


def project_back_kernel(with_query, dqkv_ref, tok_ref, w_ref, gain_ref, mod_ref, dx_ref, sum_ref):
    @pl.when(pl.program_id(0) == 0)
    def clear():
        sum_ref[...] = jnp.zeros_like(sum_ref)

    first = 0 if with_query else D
    dhm = dot(dqkv_ref[:, first:], w_ref[:, first:], NT)
    x = tok_ref[...].astype(jnp.float32)
    r1 = rms_scale(x)
    add_row(sum_ref, 3, dhm)
    add_row(sum_ref, 4, dhm * (x * r1 * gain_ref[0:1]))
    dx, terms = norm_back(dhm * (1.0 + mod_ref[1:2]), x, r1, gain_ref[0:1])
    add_row(sum_ref, 0, terms)
    dx_ref[...] = dx.astype(jnp.bfloat16)


def project_back(dqkv, first, own, tokens_all, full_qkv, gains, mods):
    rows = dqkv.shape[0] - own if first else own
    step = min(256, own)
    skip = first // step
    row = pl.BlockSpec((step, D), lambda i: (i + skip, 0))
    return pl.pallas_call(
        functools.partial(project_back_kernel, first == 0),
        grid=(max(rows // step, 1),),
        in_specs=[pl.BlockSpec((step, 3 * D), lambda i: (i + skip, 0)), row]
        + [pl.BlockSpec(full_qkv.shape, lambda i: (0, 0), pipeline_mode=pl.Buffered(1))]
        + [small_spec(gains.shape), small_spec(mods.shape)],
        out_specs=[pl.BlockSpec((step, D), lambda i: (i, 0)), small_spec((8, D))],
        out_shape=[
            jax.ShapeDtypeStruct((rows, D), jnp.bfloat16),
            jax.ShapeDtypeStruct((8, D), jnp.float32),
        ],
        compiler_params=params(),
        cost_estimate=cost(6 * rows * D * D, 30e6),
    )(dqkv, tokens_all, full_qkv, gains, mods)


def product_kernel(where_ref, d_ref, a_ref, *refs):
    p = dot(d_ref[0], a_ref[...], TN)
    if len(refs) == 2:
        p = p + refs[0][0].astype(jnp.float32)
    refs[-1][0] = p.astype(jnp.bfloat16)


def product(dact, act, starts, lanes, received=None):
    parts, tokens, columns = dact.shape
    count = len(starts)
    width = lanes if lanes <= 512 else 512
    per = lanes // width
    tile = next(t for t in (2048, 1536, 1024, 512, 256, 128) if columns % t == 0)
    each = columns // tile
    out_spec = pl.BlockSpec((1, tile, width), lambda n, k, s: (k // per, n, k % per))
    return pl.pallas_call(
        product_kernel,
        grid_spec=pltpu.PrefetchScalarGridSpec(
            num_scalar_prefetch=1,
            grid=(parts * each, count * per),
            in_specs=[
                pl.BlockSpec((1, tokens, tile), lambda n, k, s: (n // each, 0, n % each)),
                pl.BlockSpec((tokens, width), lambda n, k, s: (0, s[k // per] * per + k % per)),
            ]
            + ([] if received is None else [out_spec]),
            out_specs=out_spec,
        ),
        out_shape=jax.ShapeDtypeStruct((count, parts * columns, lanes), jnp.bfloat16),
        compiler_params=params(),
        cost_estimate=cost(
            2 * tokens * parts * columns * lanes * count, 4 * parts * columns * lanes * count
        ),
    )(jnp.stack(starts).astype(jnp.int32), dact, act, *([] if received is None else [received]))


ORDERS = ["yxz", "xzy", "zyx"]


def bits_of(size):
    return size.bit_length() - 1


def swap(value, axis, mask, size):
    return lax.ppermute(value, axis, [(i, i ^ mask) for i in range(size)])


def after(value, *earlier):
    return lax.optimization_barrier((value,) + earlier)[0]


def special(env):
    return env[1] == 2 and bits_of(env[0]) >= 3


def gather_pieces(shard, routes, env):
    nd, nf, me, mine = env
    if not special(env):
        full = lax.all_gather(shard, "fsdp", axis=0, tiled=True)
        half = full.shape[0] // 2
        return (full[:half], [full[half:]], [jnp.int32(0), jnp.int32(half)]), shard
    rows = shard.shape[0]
    chunk = rows // len(routes)
    pieces, starts, firsts = [], [], []
    for r, route in enumerate(routes):
        piece_rows = chunk >> len(route)
        index = sum(((me >> b) & 1) << i for i, b in enumerate(route))
        base = r * chunk + (mine ^ 1) * rows
        part = lax.dynamic_slice_in_dim(shard, r * chunk + index * piece_rows, piece_rows, 0)
        held = [(0, swap(part, "fsdp", 1, nf))]
        firsts.append(held[0][1])
        for i, b in enumerate(route):
            held = held + [(rel | (1 << i), swap(p, "dp", 1 << b, nd)) for rel, p in held]
        for rel, p in held:
            pieces.append(p)
            starts.append(base + (index ^ rel) * piece_rows)
    return (shard, pieces, [mine * rows] + starts), firsts


def gather_half(shard, env, hold, late):
    nd, nf, me, mine = env
    if not special(env):
        full = lax.all_gather(shard, "fsdp", axis=0, tiled=True)
        half = full.shape[0] // 2
        return (full[:half], full[half:]), shard
    rows = shard.shape[0] // 8
    part = after(lax.dynamic_slice_in_dim(shard, (me & 7) * rows, rows, 0), *hold)
    got = swap(part, "fsdp", 1, nf)
    groups = [list(range(i, i + 8)) for i in range(0, nd, 8)]
    if late:
        got = after(got, *late)
    other = lax.all_gather(got, "dp", axis=0, tiled=True, axis_index_groups=groups)
    return (shard, other), got


def gather_relative(value, env):
    nf = env[1]
    blocks = [value]
    for b in range(bits_of(nf)):
        blocks = blocks + [swap(p, "fsdp", 1 << b, nf) for p in blocks]
    return jnp.concatenate(blocks, axis=0)


def reduce_relative(value, env):
    nf = env[1]
    total = None
    for b in reversed(range(bits_of(nf))):
        half = value.shape[0] // 2
        got = swap(value[half:], "fsdp", 1 << b, nf)
        total = value[:half].astype(jnp.float32) + got.astype(jnp.float32)
        value = total.astype(jnp.bfloat16)
    return value.astype(jnp.float32) if total is None else total


def sum_fsdp(value, env, anchor=None):
    nf = env[1]
    for b in range(bits_of(nf)):
        got = swap(value.astype(jnp.bfloat16), "fsdp", 1 << b, nf)
        if anchor is not None:
            got = after(got, anchor)
        value = value + got.astype(jnp.float32)
    return value


def gather_small(pack, env):
    nf, mine = env[1], env[3]
    if nf != 2:
        return lax.all_gather(pack, "fsdp", axis=1, tiled=True)
    got = swap(pack, "fsdp", 1, nf)
    return jnp.concatenate(
        [jnp.where(mine == 0, pack, got), jnp.where(mine == 0, got, pack)], axis=1
    )


def sum_wide(value, axes, env):
    for axis in axes:
        size = env[0] if axis == "dp" else env[1]
        for b in range(bits_of(size)):
            value = value + swap(value, axis, 1 << b, size)
    return value


def stages_of(order, env):
    kinds = {
        "y": [("f", b) for b in range(bits_of(env[1]))],
        "x": [("d", 1)],
        "z": [("d", 2)] if bits_of(env[0]) > 2 else [],
    }
    return [stage for letter in order for stage in kinds[letter]]


def ladder_step(cur, alive, stage, env, anchor):
    nd, nf, me, mine = env
    kind, b = stage
    if kind == "f":
        pairs = cur.reshape((cur.shape[0] // 2, 2) + cur.shape[1:])
        keep, got = pairs[:, 0], swap(pairs[:, 1], "fsdp", 1 << b, nf)
    else:
        axis = 1 + alive.index(b)
        bit = (me >> b) & 1
        keep = lax.dynamic_index_in_dim(cur, bit, axis, keepdims=False)
        got = swap(lax.dynamic_index_in_dim(cur, bit ^ 1, axis, keepdims=False), "dp", 1 << b, nd)
        alive = [d for d in alive if d != b]
    return keep, got, alive


def add_low(keep, got):
    return (keep.astype(jnp.float32) + got.astype(jnp.float32)).astype(jnp.bfloat16)


def finish_rows(done, env):
    nd, nf, me, mine = env
    core = me & 1
    sent = lax.dynamic_index_in_dim(done, core ^ 1, 0, keepdims=False)
    kept = lax.dynamic_index_in_dim(done, core, 0, keepdims=False)
    got = swap(sent, "dp", 1, nd)
    both = jnp.where(
        core == 0,
        jnp.concatenate([kept, got], axis=1),
        jnp.concatenate([got, kept], axis=1),
    )
    return both.T.astype(jnp.float32)


def core_product(dact, act, core, env, rows_only, received=None):
    nd, nf, me, mine = env
    count = 1 if rows_only else nf
    lanes = act.shape[1] // (2 * count)
    blocks = [core] if rows_only else [2 * (mine ^ r) + core for r in range(nf)]
    if lanes % 128 == 0:
        return product(dact, act, blocks, lanes, received)
    wide = jnp.concatenate(list(dact), axis=1)
    parts = [lax.dynamic_slice_in_dim(act, b * lanes, lanes, 1) for b in blocks]
    out = jnp.stack([dot(wide, p, TN) for p in parts])
    if received is not None:
        out = out + received.astype(jnp.float32)
    return out.astype(jnp.bfloat16)


class Reduction:
    def __init__(self, dact, act, portions, env, rows_only=False):
        self.env, self.dact, self.act = env, dact, act
        self.portions, self.rows_only = portions, rows_only
        nd, core = env[0], env[2] & 1
        self.partial = core_product(dact, act, core ^ 1, env, rows_only)
        self.sent = swap(self.partial, "dp", 1, nd)
        self.tie = [self.partial]
        self.flight = None
        self.done = False

    def launch(self):
        if not any(stages for _, _, stages in self.ladders):
            if len(self.ladders) > 1:
                alive = self.ladders[0][1]
                self.ladders = [
                    (jnp.concatenate([cur for cur, _, _ in self.ladders], axis=-1), alive, [])
                ]
            cur, alive, _ = self.ladders[0]
            if not alive:
                self.done = True
                return
            self.ladders = [(cur, alive, [("d", alive[-1])])]
        self.flight = [
            ladder_step(cur, alive, stages[0], self.env, None) + (stages[1:],)
            for cur, alive, stages in self.ladders
        ]

    def step(self, anchor):
        if self.done:
            return
        nd, bits = self.env[0], bits_of(self.env[0])
        if self.flight is None:
            core = self.env[2] & 1
            sent = after(self.sent, anchor)
            total = core_product(self.dact, self.act, core, self.env, self.rows_only, sent)
            total = total.reshape(
                (total.shape[0],) + (2,) * bits + (total.shape[1] // nd, total.shape[2])
            )
            alive = list(range(bits - 1, 0, -1))
            self.ladders, start = [], 0
            for width, order in self.portions:
                stages = stages_of(order, self.env)
                self.ladders.append((total[..., start : start + width], alive, stages))
                start += width
            self.tie = [total]
        else:
            self.ladders = []
            for keep, got, alive, stages in self.flight:
                self.ladders.append((add_low(keep, after(got, anchor)), alive, stages))
            self.tie = [cur for cur, _, _ in self.ladders]
        self.launch()

    def finish(self, anchor):
        while not self.done:
            self.step(anchor)
            anchor = self.tie[0]
        return finish_rows(self.ladders[0][0][0], self.env)


def then(value, anchor, *reductions):
    ties = [anchor]
    for r in reductions:
        if not r.done:
            r.step(anchor)
            ties += r.tie
    return after(value, *ties)


def portion_list(lanes, names):
    units = lanes // 128
    if lanes % 128 or units < len(names):
        return [(lanes, names[-1])]
    cuts = [units * i // len(names) * 128 for i in range(len(names) + 1)]
    return [(b - a, n) for a, b, n in zip(cuts, cuts[1:], names)]


def per_device(
    tokens,
    caption,
    modulation,
    caption_mask,
    positions,
    w_qkv,
    w_out,
    w_caption_kv,
    w_gate_up,
    w_down,
    norm_gains,
    caption_gain,
    cross_gate,
    cotangent,
):
    nd, nf = lax.axis_size("dp"), lax.axis_size("fsdp")
    me, mine = lax.axis_index("dp"), lax.axis_index("fsdp")
    env = (nd, nf, me, mine)
    own_rows = tokens.shape[1]
    heads = cross_gate.shape[0]
    which = (mine if special(env) else jnp.int32(0)).astype(jnp.int32)[None]
    pack = jnp.concatenate(
        [
            norm_gains,
            modulation[0],
            caption_gain[None],
            jnp.pad(cross_gate, (0, caption_gain.shape[0] - heads))[None],
        ]
    )
    pack = gather_small(pack, env)
    places = gather_relative(positions[0].T, env)
    gath_qkv, firsts = gather_pieces(w_qkv, [(1, 2, 0), (2, 1, 0)], env)
    tokens_all = gather_relative(after(tokens[0], *firsts), env)
    partial_kv = dot(caption[0], w_caption_kv)
    tokens_all = after(tokens_all, partial_kv)
    late = tuple(gath_qkv[1]) + (tokens_all, pack, places)
    full_gate_up, got = gather_half(w_gate_up, env, firsts, late)
    full_out, _ = gather_half(w_out, env, (got,), late)
    pack = pack.astype(jnp.float32)
    gains, mods, cap_gain = pack[:6], pack[6:12], pack[12]
    gate_heads = jnp.tanh(pack[13].reshape(nf, -1)[:, :heads].reshape(HEADS))
    gate_tanh = jnp.repeat(gate_heads, HEAD_DIM)[None]
    cosine, sine = rope_tables(places)
    hm, full_qkv, query_b, key_b, value_b, query_pre, key_pre = project(
        tokens_all, own_rows, gains, mods, cosine, sine, gath_qkv
    )
    cap_rows = sum_fsdp(after(partial_kv, tokens_all), env, hm)
    ckey_pre = cap_rows[:, :D]
    ckey_scale = rms_scale(ckey_pre)
    ckey_b = (ckey_pre * ckey_scale * cap_gain).astype(jnp.bfloat16)
    cvalue_b = cap_rows[:, D:].astype(jnp.bfloat16)
    bias = jnp.where(caption_mask[0] > 0, 0.0, -1e30).astype(jnp.float32)
    combined, self_out, cross_out, stats = attend(
        query_b, key_b, value_b, ckey_b, cvalue_b, bias[None], gate_tanh
    )
    full_down, _ = gather_half(w_down, env, (cvalue_b,), (stats,))
    projected, middle, ffn_in = output_step(which, combined, full_out, tokens[0], gains, mods)
    gate_part, up_part, ffn_inner = gate_up_step(which, ffn_in, full_gate_up)
    block_out, grad_down, down_sums = down_step(
        which, ffn_inner, full_down, middle, cotangent[0], gains, mods
    )
    lanes_d, lanes_f = D // (2 * nf), FF // (2 * nf)
    red_down = Reduction(grad_down[None], ffn_inner, portion_list(lanes_f, ORDERS), env)
    grad_down = after(grad_down, red_down.partial)
    grad_gate_up = gate_up_back(which, grad_down, gate_part, up_part, full_down)
    dgu = then(grad_gate_up, grad_gate_up, red_down)
    red_gate_up = Reduction(dgu, ffn_in, portion_list(lanes_d, ORDERS), env)
    dgu = after(dgu, red_gate_up.partial)
    grad_mid, grad_proj, grad_comb, ffn_sums = ffn_back(
        which, dgu, full_gate_up, full_out, middle, cotangent[0], projected, gains, mods
    )
    grad_comb = then(grad_comb, ffn_sums, red_down)
    dq_cross, grad_ckey, grad_cvalue, gate_sums = cross_back(
        query_b, ckey_b, cvalue_b, bias[:, None], gate_tanh, stats, grad_comb, cross_out
    )
    gate_terms = gate_sums[0].reshape(HEADS, HEAD_DIM).sum(axis=-1) * (1.0 - gate_heads**2)
    grad_ckey_pre, cap_gain_terms = norm_back(
        grad_ckey.astype(jnp.float32), ckey_pre, ckey_scale, cap_gain
    )
    grad_cap_kv = jnp.concatenate([grad_ckey_pre, grad_cvalue.astype(jnp.float32)], axis=-1)
    grad_cap_kv = grad_cap_kv.astype(jnp.bfloat16)
    tied = then(gate_sums, grad_cap_kv, red_down)
    grad_comb = then(grad_comb, tied, red_gate_up)
    red_out = Reduction(
        after(grad_proj, grad_comb)[None], combined, portion_list(lanes_d, ORDERS[2:]), env
    )
    grad_comb = then(grad_comb, red_out.partial, red_down)
    pairs = D // PAIR
    each = pairs // 4
    parts = []

    def attention_part(grads):
        parts.append(
            self_back(query_b, key_b, value_b, stats, grads, self_out, dq_cross, len(parts) * each, each)
        )
        return parts[-1][0]

    done = attention_part(grad_comb)
    grad_comb = then(grad_comb, done, red_down, red_out)
    done = attention_part(grad_comb)
    grad_cap_kv = sum_fsdp(grad_cap_kv.astype(jnp.float32), env, done).astype(jnp.bfloat16)
    red_caption = Reduction(
        grad_cap_kv[None], caption[0], portion_list(caption.shape[2] // 2, ["xz", "zx"]), env, True
    )
    grad_comb = after(grad_comb, red_caption.partial)
    done = attention_part(grad_comb)
    grad_comb = then(grad_comb, done, red_gate_up, red_out)
    done = then(grad_comb, done, red_caption)
    done = attention_part(done)
    grad_query, grad_key, grad_value = zip(*parts)
    grad_query = (then(grad_query[0], done, red_out),) + grad_query[1:]
    grad_mixed, qk_sums = qk_back(
        grad_query, grad_key, grad_value, query_pre, key_pre, cosine, sine, gains
    )
    grad_mixed = then(grad_mixed, qk_sums, red_gate_up)
    red_qkv = Reduction(grad_mixed[None], hm, portion_list(lanes_d, ORDERS), env)
    grad_mixed = then(grad_mixed, red_qkv.partial, red_gate_up, red_out)
    dx_other, other_sums = project_back(
        grad_mixed, own_rows, own_rows, tokens_all, full_qkv, gains, mods
    )
    grad_mixed = then(grad_mixed, other_sums, red_caption, red_qkv)
    dx_own, own_sums = project_back(grad_mixed, 0, own_rows, tokens_all, full_qkv, gains, mods)
    grad_cap_kv = then(grad_cap_kv, own_sums, red_caption, red_gate_up, red_out)
    grad_caption = dot(grad_cap_kv, w_caption_kv, NT).astype(jnp.bfloat16)
    anchor = grad_caption
    red_qkv.step(anchor)
    project_sums = own_sums + other_sums if nf > 1 else own_sums
    grad_inputs = jnp.concatenate([dx_own, dx_other]) if nf > 1 else dx_own
    grad_tokens = (grad_mid + reduce_relative(grad_inputs, env)).astype(jnp.bfloat16)
    small = jnp.concatenate(
        [
            project_sums[:1],
            qk_sums[1:3],
            jnp.stack(
                [
                    ffn_sums[4],
                    ffn_sums[2],
                    down_sums[1],
                    jnp.sum(cap_gain_terms, axis=0),
                    jnp.pad(gate_terms, (0, D - HEADS)),
                ]
            ),
        ]
    )
    small = sum_wide(small, ("fsdp", "dp"), env)
    mod_grads = jnp.stack(
        [
            project_sums[3],
            project_sums[4],
            ffn_sums[3] * (1.0 - jnp.tanh(mods[2]) ** 2),
            ffn_sums[0],
            ffn_sums[1],
            down_sums[0] * (1.0 - jnp.tanh(mods[5]) ** 2),
        ]
    )
    mod_grads = sum_wide(mod_grads, ("fsdp",), env)
    outs = []
    for r in (red_down, red_gate_up, red_out, red_caption, red_qkv):
        outs.append(r.finish(anchor))
    out_down, out_gate_up, out_out, out_caption, out_qkv = outs
    width = D // nf
    return (
        block_out[None],
        grad_tokens[None],
        grad_caption[None],
        lax.dynamic_slice_in_dim(mod_grads, mine * width, width, 1)[None],
        out_qkv,
        out_out,
        out_caption,
        out_gate_up,
        out_down,
        lax.dynamic_slice_in_dim(small[:6], mine * width, width, 1),
        lax.dynamic_slice_in_dim(small[6], mine * width, width, 0),
        lax.dynamic_slice_in_dim(small[7], mine * heads, heads, 0),
    )


def solution(mesh):
    placed = (
        P("dp", "fsdp", None),
        P("dp", None, "fsdp"),
        P("dp", None, "fsdp"),
        P("dp", None),
        P("dp", None, "fsdp"),
        P("fsdp", None),
        P("fsdp", None),
        P("fsdp", None),
        P("fsdp", None),
        P("fsdp", None),
        P(None, "fsdp"),
        P("fsdp"),
        P("fsdp"),
        P("dp", "fsdp", None),
    )
    return jax.shard_map(
        per_device,
        mesh=mesh,
        in_specs=placed,
        out_specs=(
            P("dp", "fsdp", None),
            P("dp", "fsdp", None),
            P("dp", None, "fsdp"),
            P("dp", None, "fsdp"),
            P("fsdp", "dp"),
            P("fsdp", "dp"),
            P("fsdp", "dp"),
            P("fsdp", "dp"),
            P("fsdp", "dp"),
            P(None, "fsdp"),
            P("fsdp"),
            P("fsdp"),
        ),
        check_vma=False,
    )
```

```python
import functools

import jax
import jax.numpy as jnp
from jax import lax
from jax.experimental import pallas as pl
from jax.experimental.pallas import tpu as pltpu
from jax.sharding import PartitionSpec as P

D = 1536
HEADS = 24
HEAD_DIM = 64
FF = 4096
EPS = 1e-05


def rms_scale(values):
    return lax.rsqrt(jnp.mean(values * values, axis=-1, keepdims=True) + EPS)


def norm_back(grad_normed, values, inv_rms, gain_row):
    scaled_grad = grad_normed * gain_row
    grad_values = inv_rms * scaled_grad - values * inv_rms**3 * jnp.mean(
        scaled_grad * values, axis=-1, keepdims=True
    )
    return (grad_values, grad_normed * values * inv_rms)


def rope_tables(positions):
    lane = jnp.arange(PAIR)
    frequency = 10000.0 ** (-(lane % 16).astype(jnp.float32) / 16)
    places = positions.astype(jnp.float32)
    angles = jnp.where((lane % 64 < 32)[None], places[:, :1], places[:, 1:]) * frequency
    sign = jnp.where(lane % 32 < 16, -1.0, 1.0).astype(jnp.float32)
    return jnp.cos(angles), jnp.sin(angles) * sign


PAIR = 2 * HEAD_DIM
NT = (((1,), (1,)), ((), ()))
TN = (((0,), (0,)), ((), ()))


def head_masks(dtype):
    lane = lax.broadcasted_iota(jnp.int32, (1, PAIR), 1)
    return [(lane < HEAD_DIM).astype(dtype), (lane >= HEAD_DIM).astype(dtype)]


def attend_kernel(q_ref, k_ref, v_ref, ck_ref, cv_ref, bias_ref, gate_ref, a_ref, o_ref, oy_ref, stat_ref):
    masks = head_masks(jnp.float32)
    rows = q_ref.shape[0]
    step = min(rows, 256)
    gate = gate_ref[...]
    for start in range(0, rows, step):
        where = pl.ds(start, step)
        q = q_ref[where, :].astype(jnp.float32) * HEAD_DIM**-0.5
        own, cross, stats = [], [], []
        for mask in masks:
            qm = (q * mask).astype(jnp.bfloat16)
            for keys, values, bias, outs in (
                (k_ref, v_ref, None, own),
                (ck_ref, cv_ref, bias_ref, cross),
            ):
                s = lax.dot_general(qm, keys[...], NT, preferred_element_type=jnp.float32)
                if bias is not None:
                    s = s + bias[...]
                top = jnp.max(s, axis=1, keepdims=True)
                e = jnp.exp(s - top)
                total = jnp.sum(e, axis=1, keepdims=True)
                out = jnp.dot(e.astype(jnp.bfloat16), values[...], preferred_element_type=jnp.float32)
                outs.append(out / total * mask)
                stats.append(top + jnp.log(total))
        o = own[0] + own[1]
        oy = cross[0] + cross[1]
        a_ref[where, :] = (o + gate * oy).astype(jnp.bfloat16)
        o_ref[where, :] = o.astype(jnp.bfloat16)
        oy_ref[where, :] = oy.astype(jnp.bfloat16)
        lane = lax.broadcasted_iota(jnp.int32, (step, PAIR), 1)
        tile = jnp.where(lane == 0, stats[0], jnp.where(lane == 1, stats[1], jnp.where(lane == 2, stats[2], stats[3])))
        stat_ref[0, :, where] = tile.T[:8, :]


def attend(query, key, value, ckey, cvalue, bias_row, gate_lanes):
    rows, keys, slots = query.shape[0], key.shape[0], ckey.shape[0]
    pairs = D // PAIR
    spec = lambda n: pl.BlockSpec((n, PAIR), lambda j: (0, j))
    return pl.pallas_call(
        attend_kernel,
        grid=(pairs,),
        in_specs=[
            spec(rows), spec(keys), spec(keys), spec(slots), spec(slots),
            pl.BlockSpec((1, slots), lambda j: (0, 0)), spec(1),
        ],
        out_specs=[spec(rows)] * 3 + [pl.BlockSpec((1, 8, rows), lambda j: (j, 0, 0))],
        out_shape=[jax.ShapeDtypeStruct((rows, D), jnp.bfloat16)] * 3
        + [jax.ShapeDtypeStruct((pairs, 8, rows), jnp.float32)],
        compiler_params=pltpu.CompilerParams(vmem_limit_bytes=48 * 2**20),
        cost_estimate=cost(16 * rows * (keys + slots) * D, 20e6, HEADS * rows * (keys + slots)),
    )(query, key, value, ckey, cvalue, bias_row, gate_lanes)


def back_part(k_tile, v_tile, bias, qm, grads, deltas, lses):
    masks = head_masks(jnp.bfloat16)
    dk = dv = add = None
    for h in range(2):
        st = dot(k_tile, qm[h], NT)
        if bias is not None:
            st = st + bias
        pt = jnp.exp(st - lses[h])
        dpt = dot(v_tile, grads[h], NT)
        dst = (pt * (dpt - deltas[h])).astype(jnp.bfloat16)
        terms = (
            dot(dst, qm[h]),
            dot(pt.astype(jnp.bfloat16), grads[h]),
            dot(dst, k_tile * masks[h], TN),
        )
        dk, dv, add = terms if h == 0 else (dk + terms[0], dv + terms[1], add + terms[2])
    return dk, dv, add


def head_sums(terms):
    t = terms.T
    return [
        jnp.sum(t[:HEAD_DIM], axis=0, keepdims=True),
        jnp.sum(t[HEAD_DIM:], axis=0, keepdims=True),
    ]


def split_heads(values):
    return [(values * m).astype(jnp.bfloat16) for m in head_masks(jnp.float32)]


def cross_back_kernel(q_ref, ck_ref, cv_ref, bias_ref, gate_ref, stat_ref, da_ref, oy_ref, dq_ref, dck_ref, dcv_ref, gsum_ref):
    qm = split_heads(q_ref[...].astype(jnp.float32) * HEAD_DIM**-0.5)
    da = da_ref[...].astype(jnp.float32)
    doy = (da * gate_ref[...]).astype(jnp.bfloat16).astype(jnp.float32)
    oy = oy_ref[...].astype(jnp.float32)
    gsum_ref[...] = jnp.sum(da * oy, axis=0, keepdims=True)
    stat = stat_ref[0]
    dk, dv, dq = back_part(
        ck_ref[...], cv_ref[...], bias_ref[...], qm, split_heads(doy), head_sums(doy * oy), [stat[1:2], stat[3:4]]
    )
    dck_ref[...] = dk.astype(dck_ref.dtype)
    dcv_ref[...] = dv.astype(dcv_ref.dtype)
    dq_ref[...] = (dq * HEAD_DIM**-0.5).astype(dq_ref.dtype)


def self_back_kernel(q_ref, k_ref, v_ref, stat_ref, da_ref, o_ref, dqc_ref, dq_ref, dk_ref, dv_ref):
    keys = k_ref.shape[0]
    step = min(keys, 256)
    qm = split_heads(q_ref[...].astype(jnp.float32) * HEAD_DIM**-0.5)
    da = da_ref[...].astype(jnp.float32)
    deltas = head_sums(da * o_ref[...].astype(jnp.float32))
    dam = split_heads(da)
    stat = stat_ref[0]
    dq = None
    for start in range(0, keys, step):
        where = pl.ds(start, step)
        dk, dv, add = back_part(k_ref[where, :], v_ref[where, :], None, qm, dam, deltas, [stat[0:1], stat[2:3]])
        dk_ref[where, :] = dk.astype(dk_ref.dtype)
        dv_ref[where, :] = dv.astype(dv_ref.dtype)
        dq = add if dq is None else dq + add
    dq = dq * HEAD_DIM**-0.5 + dqc_ref[...].astype(jnp.float32)
    dq_ref[...] = dq.astype(dq_ref.dtype)


def cross_back(query, ckey, cvalue, bias_col, gate_lanes, stats, grad_a, o_cross):
    rows, slots = query.shape[0], ckey.shape[0]
    pairs = D // PAIR
    spec = lambda n: pl.BlockSpec((n, PAIR), lambda j: (0, j))
    return pl.pallas_call(
        cross_back_kernel,
        grid=(pairs,),
        in_specs=[
            spec(rows), spec(slots), spec(slots),
            pl.BlockSpec((slots, 1), lambda j: (0, 0)), spec(1),
            pl.BlockSpec((1, 8, rows), lambda j: (j, 0, 0)),
            spec(rows), spec(rows),
        ],
        out_specs=[spec(rows), spec(slots), spec(slots), spec(1)],
        out_shape=[jax.ShapeDtypeStruct((n, D), jnp.bfloat16) for n in (rows, slots, slots)]
        + [jax.ShapeDtypeStruct((1, D), jnp.float32)],
        compiler_params=params(48),
        cost_estimate=cost(40 * rows * slots * D, 9e6, HEADS * rows * slots),
    )(query, ckey, cvalue, bias_col, gate_lanes, stats, grad_a, o_cross)


def self_back(query, key, value, stats, grad_a, o_self, dq_cross, first, count):
    rows, keys = query.shape[0], key.shape[0]
    spec = lambda n: pl.BlockSpec((n, PAIR), lambda j: (0, j + first))
    out = lambda n: pl.BlockSpec((n, PAIR), lambda j: (0, j))
    return pl.pallas_call(
        self_back_kernel,
        grid=(count,),
        in_specs=[
            spec(rows), spec(keys), spec(keys),
            pl.BlockSpec((1, 8, rows), lambda j: (j + first, 0, 0)),
            spec(rows), spec(rows), spec(rows),
        ],
        out_specs=[out(rows), out(keys), out(keys)],
        out_shape=[jax.ShapeDtypeStruct((n, count * PAIR), jnp.bfloat16) for n in (rows, keys, keys)],
        compiler_params=params(48),
        cost_estimate=cost(80 * rows * keys * count * PAIR, 1e6 * count, 2 * count * rows * keys),
    )(query, key, value, stats, grad_a, o_self, dq_cross)


NN = (((1,), (0,)), ((), ()))


def dot(a, b, dims=NN):
    return lax.dot_general(a, b, dims, preferred_element_type=jnp.float32)


def chunks(rows, step, body):
    def one(i, carry):
        body(pl.ds(pl.multiple_of(i * step, step), step))
        return carry

    lax.fori_loop(0, rows // step, one, 0)


def add_row(ref, index, terms):
    ref[index : index + 1, :] += jnp.sum(terms, axis=0, keepdims=True)


def partner(values):
    lane = lax.broadcasted_iota(jnp.int32, (values.shape[0], PAIR), 1)
    low = (lane & 31) < 16
    outs = []
    for start in range(0, values.shape[1], PAIR):
        tile = values[:, start : start + PAIR]
        outs.append(jnp.where(low, pltpu.roll(tile, PAIR - 16, 1), pltpu.roll(tile, 16, 1)))
    return jnp.concatenate(outs, axis=1)


def turn(values, cosine, sine):
    count = values.shape[1] // PAIR
    wide = lambda t: jnp.concatenate([t] * count, axis=1)
    return values * wide(cosine) + partner(values) * wide(sine)


def halves(values, which):
    mid = values.shape[1] // 2
    low, high = values[:, :mid], values[:, mid:]
    first = which == 0
    return jnp.where(first, low, high), jnp.where(first, high, low)


def small_spec(shape):
    return pl.BlockSpec(shape, lambda *_: (0,) * len(shape))


def params(mib=56):
    return pltpu.CompilerParams(vmem_limit_bytes=mib * 2**20)


def cost(flops, nbytes, trans=0):
    share = 0.05
    return pl.CostEstimate(
        flops=int(flops * share), bytes_accessed=int(nbytes * share), transcendentals=int(trans * share)
    )


def project_kernel(parts, own_rows, where_ref, tok_ref, gain_ref, mod_ref, cos_ref, sin_ref, own_ref, *refs):
    pieces = refs[:parts]
    hm_ref, full_ref, q_ref, k_ref, v_ref, qpre_ref, kpre_ref, pre_ref = refs[parts:]
    pid = pl.program_id(0)
    rows = tok_ref.shape[0]
    step = min(128, rows)
    tile = full_ref.shape[1]
    per = D // tile

    @pl.when(pid == 0)
    def hidden():
        def body(where):
            x = tok_ref[where, :].astype(jnp.float32)
            hid = x * rms_scale(x) * gain_ref[0:1]
            hm_ref[where, :] = (hid * (1.0 + mod_ref[1:2]) + mod_ref[0:1]).astype(jnp.bfloat16)

        chunks(rows, step, body)

    n = own_ref.shape[0]
    full_ref[pl.ds(pl.multiple_of(where_ref[0], n), n), :] = own_ref[...]
    for i, piece in enumerate(pieces):
        n = piece.shape[0]
        full_ref[pl.ds(pl.multiple_of(where_ref[i + 1], n), n), :] = piece[...]

    for j in range(2 * per):
        count = own_rows if j < per else rows

        @pl.when(pid == j)
        def pre(j=j, count=count):
            pre_ref[:count, (j % per) * tile : (j % per + 1) * tile] = dot(
                hm_ref[:count, :], full_ref[...]
            )

    @pl.when(pid >= 2 * per)
    def value():
        v_ref[...] = dot(hm_ref[...], full_ref[...]).astype(jnp.bfloat16)

    for last, count, out, keep, gain in (
        (per - 1, own_rows, q_ref, qpre_ref, 1),
        (2 * per - 1, rows, k_ref, kpre_ref, 2),
    ):

        @pl.when(pid == last)
        def finish(count=count, out=out, keep=keep, gain=gain):
            def body(where):
                p = pre_ref[where, :]
                n = p * rms_scale(p) * gain_ref[gain : gain + 1]
                out[where, :] = turn(n, cos_ref[where, :], sin_ref[where, :]).astype(jnp.bfloat16)
                keep[where, :] = p.astype(jnp.bfloat16)

            chunks(count, min(step, count), body)


def project(tokens_all, own_rows, gains, mods, cosine, sine, weight, tile=512):
    own, pieces, starts = weight
    rows = tokens_all.shape[0]
    n = 3 * D // tile
    vtile = 2 * D // tile
    outs = [
        ((rows, D), jnp.bfloat16, None),
        ((D, 3 * D), jnp.bfloat16, pl.BlockSpec((D, tile), lambda j, w: (0, j))),
        ((own_rows, D), jnp.bfloat16, None),
        ((rows, D), jnp.bfloat16, None),
        ((rows, D), jnp.bfloat16, pl.BlockSpec((rows, tile), lambda j, w: (0, jnp.maximum(j - vtile, 0)))),
        ((own_rows, D), jnp.bfloat16, None),
        ((rows, D), jnp.bfloat16, None),
    ]
    return pl.pallas_call(
        functools.partial(project_kernel, len(pieces), own_rows),
        grid_spec=pltpu.PrefetchScalarGridSpec(
            num_scalar_prefetch=1,
            grid=(n,),
            in_specs=[small_spec(a.shape) for a in (tokens_all, gains, mods, cosine, sine)]
            + [pl.BlockSpec((p.shape[0], tile), lambda j, w: (0, j)) for p in [own] + pieces],
            out_specs=[s if s is not None else small_spec(shape) for shape, _, s in outs],
            scratch_shapes=[pltpu.VMEM((rows, D), jnp.float32)],
        ),
        out_shape=[jax.ShapeDtypeStruct(shape, d) for shape, d, _ in outs],
        compiler_params=params(58),
        cost_estimate=cost(2 * D * D * (own_rows + 2 * rows), 60e6),
    )(jnp.stack(starts).astype(jnp.int32), tokens_all, gains, mods, cosine, sine, own, *pieces)


def output_kernel(which_ref, a_ref, w0_ref, w1_ref, x_ref, gain_ref, mod_ref, o_ref, mid_ref, hfm_ref):
    a0, a1 = halves(a_ref[...], which_ref[0])
    o = dot(a0, w0_ref[...]) + dot(a1, w1_ref[...])
    o_ref[...] = o.astype(jnp.bfloat16)
    on = o * rms_scale(o) * gain_ref[3:4]
    mid = x_ref[...].astype(jnp.float32) + jnp.tanh(mod_ref[2:3]) * on
    mid_ref[...] = mid
    hf = mid * rms_scale(mid) * gain_ref[4:5]
    hfm_ref[...] = (hf * (1.0 + mod_ref[4:5]) + mod_ref[3:4]).astype(jnp.bfloat16)


def output_step(which, combined, weight, tokens, gains, mods):
    rows = combined.shape[0]
    step = min(rows, 256)
    row_spec = pl.BlockSpec((step, D), lambda i, w: (i, 0))
    return pl.pallas_call(
        output_kernel,
        grid_spec=pltpu.PrefetchScalarGridSpec(
            num_scalar_prefetch=1,
            grid=(rows // step,),
            in_specs=[row_spec, small_spec(weight[0].shape), small_spec(weight[1].shape), row_spec]
            + [small_spec(gains.shape), small_spec(mods.shape)],
            out_specs=[row_spec] * 3,
        ),
        out_shape=[
            jax.ShapeDtypeStruct((rows, D), jnp.bfloat16),
            jax.ShapeDtypeStruct((rows, D), jnp.float32),
            jax.ShapeDtypeStruct((rows, D), jnp.bfloat16),
        ],
        compiler_params=params(),
        cost_estimate=cost(2 * rows * D * D, 15e6),
    )(which, combined, weight[0], weight[1], tokens, gains, mods)


def gate_up_kernel(which_ref, h_ref, g0_ref, g1_ref, u0_ref, u1_ref, ga_ref, up_ref, ff_ref, hs_ref):
    @pl.when(pl.program_id(0) == 0)
    def split():
        hs_ref[0], hs_ref[1] = halves(h_ref[...], which_ref[0])

    ga = dot(hs_ref[0], g0_ref[...]) + dot(hs_ref[1], g1_ref[...])
    up = dot(hs_ref[0], u0_ref[...]) + dot(hs_ref[1], u1_ref[...])
    ga_ref[...] = ga.astype(jnp.bfloat16)
    up_ref[...] = up.astype(jnp.bfloat16)
    ff_ref[...] = (ga / (1.0 + jnp.exp(-ga)) * up).astype(jnp.bfloat16)


def gate_up_step(which, hfm, weight, tile=512):
    rows = hfm.shape[0]
    n = FF // tile
    half = D // 2
    spec = lambda off: pl.BlockSpec((half, tile), lambda j, w: (0, j + off))
    out = pl.BlockSpec((rows, tile), lambda j, w: (0, j))
    return pl.pallas_call(
        gate_up_kernel,
        grid_spec=pltpu.PrefetchScalarGridSpec(
            num_scalar_prefetch=1,
            grid=(n,),
            in_specs=[small_spec(hfm.shape), spec(0), spec(0), spec(n), spec(n)],
            out_specs=[out] * 3,
            scratch_shapes=[pltpu.VMEM((2, rows, half), jnp.bfloat16)],
        ),
        out_shape=[jax.ShapeDtypeStruct((rows, FF), jnp.bfloat16)] * 3,
        compiler_params=params(),
        cost_estimate=cost(4 * rows * D * FF, 40e6, rows * FF),
    )(which, hfm, weight[0], weight[1], weight[0], weight[1])


def down_kernel(which_ref, ff_ref, w0_ref, w1_ref, mid_ref, cot_ref, gain_ref, mod_ref, out_ref, df_ref, sum_ref, f_ref, hs_ref):
    pid = pl.program_id(0)
    tile = w0_ref.shape[1]
    rows = ff_ref.shape[0]

    @pl.when(pid == 0)
    def split():
        hs_ref[0], hs_ref[1] = halves(ff_ref[...], which_ref[0])

    f_ref[pid] = dot(hs_ref[0], w0_ref[...]) + dot(hs_ref[1], w1_ref[...])

    @pl.when(pid == pl.num_programs(0) - 1)
    def finish():
        gate = jnp.tanh(mod_ref[5:6])
        sum_ref[...] = jnp.zeros_like(sum_ref)

        def body(where):
            f = jnp.concatenate([f_ref[j, where, :] for j in range(D // tile)], axis=1)
            rf = rms_scale(f)
            fn = f * rf * gain_ref[5:6]
            dy = cot_ref[where, :].astype(jnp.float32)
            out_ref[where, :] = (mid_ref[where, :] + gate * fn).astype(jnp.bfloat16)
            dfn = dy * gate
            add_row(sum_ref, 0, dy * fn)
            df, terms = norm_back(dfn, f, rf, gain_ref[5:6])
            add_row(sum_ref, 1, terms)
            df_ref[where, :] = df.astype(jnp.bfloat16)

        chunks(rows, min(64, rows), body)


def down_step(which, ffh, weight, middle, cotangent, gains, mods, tile=256):
    rows = ffh.shape[0]
    half = FF // 2
    spec = pl.BlockSpec((half, tile), lambda j, w: (0, j))
    full = small_spec((rows, D))
    return pl.pallas_call(
        down_kernel,
        grid_spec=pltpu.PrefetchScalarGridSpec(
            num_scalar_prefetch=1,
            grid=(D // tile,),
            in_specs=[small_spec(ffh.shape), spec, spec, full, full, small_spec(gains.shape), small_spec(mods.shape)],
            out_specs=[full, full, small_spec((8, D))],
            scratch_shapes=[
                pltpu.VMEM((D // tile, rows, tile), jnp.float32),
                pltpu.VMEM((2, rows, half), jnp.bfloat16),
            ],
        ),
        out_shape=[jax.ShapeDtypeStruct((rows, D), jnp.bfloat16)] * 2
        + [jax.ShapeDtypeStruct((8, D), jnp.float32)],
        compiler_params=params(),
        cost_estimate=cost(2 * rows * D * FF, 24e6),
    )(which, ffh, weight[0], weight[1], middle, cotangent, gains, mods)


def gate_up_back_kernel(which_ref, df_ref, ga_ref, up_ref, d0_ref, d1_ref, dgu_ref):
    pid = pl.program_id(0)
    n = pl.num_programs(0)

    def work(w_ref):
        dffh = dot(df_ref[...], w_ref[...], NT)
        ga = ga_ref[...].astype(jnp.float32)
        up = up_ref[...].astype(jnp.float32)
        s = 1.0 / (1.0 + jnp.exp(-ga))
        dgu_ref[0] = (dffh * up * (s * (1.0 + ga * (1.0 - s)))).astype(jnp.bfloat16)
        dgu_ref[1] = (dffh * (ga * s)).astype(jnp.bfloat16)

    @pl.when(pid < n // 2)
    def first():
        work(d0_ref)

    @pl.when(pid >= n // 2)
    def second():
        work(d1_ref)


def gate_up_back(which, df, ga, up, w_down, tile=512):
    rows = df.shape[0]
    n = FF // tile
    h = n // 2
    cols = pl.BlockSpec((rows, tile), lambda j, w: (0, (j + w[0] * h) % n))
    return pl.pallas_call(
        gate_up_back_kernel,
        grid_spec=pltpu.PrefetchScalarGridSpec(
            num_scalar_prefetch=1,
            grid=(n,),
            in_specs=[
                small_spec((rows, D)), cols, cols,
                pl.BlockSpec((tile, D), lambda j, w: (jnp.minimum(j, h - 1), 0)),
                pl.BlockSpec((tile, D), lambda j, w: (jnp.maximum(j - h, 0), 0)),
            ],
            out_specs=pl.BlockSpec((2, rows, tile), lambda j, w: (0, 0, (j + w[0] * h) % n)),
        ),
        out_shape=jax.ShapeDtypeStruct((2, rows, FF), jnp.bfloat16),
        compiler_params=params(),
        cost_estimate=cost(2 * rows * D * FF, 30e6, rows * FF),
    )(which, df, ga, up, w_down[0], w_down[1])


def ffn_back_kernel(
    which_ref, dgu_ref, g0_ref, g1_ref, u0_ref, u1_ref,
    mid_ref, cot_ref, o_ref, w0_ref, w1_ref, gain_ref, mod_ref,
    dmid_ref, do_ref, da_ref, sum_ref, acc_ref,
):
    pid = pl.program_id(0)
    n = pl.num_programs(0)
    rows = mid_ref.shape[0]
    which = which_ref[0]
    dga, dup = dgu_ref[0], dgu_ref[1]
    p0 = dot(dga, g0_ref[...], NT) + dot(dup, u0_ref[...], NT)
    p1 = dot(dga, g1_ref[...], NT) + dot(dup, u1_ref[...], NT)

    @pl.when(pid == 0)
    def clear():
        acc_ref[which] = p0
        acc_ref[1 - which] = p1

    @pl.when(pid > 0)
    def more():
        acc_ref[which] += p0
        acc_ref[1 - which] += p1

    @pl.when(pid == n - 1)
    def finish():
        sum_ref[...] = jnp.zeros_like(sum_ref)
        gate = jnp.tanh(mod_ref[2:3])

        def body(where):
            dhfm = jnp.concatenate([acc_ref[0, where, :], acc_ref[1, where, :]], axis=1)
            mid = mid_ref[where, :]
            r2 = rms_scale(mid)
            add_row(sum_ref, 0, dhfm)
            add_row(sum_ref, 1, dhfm * (mid * r2 * gain_ref[4:5]))
            dmid, terms = norm_back(dhfm * (1.0 + mod_ref[4:5]), mid, r2, gain_ref[4:5])
            add_row(sum_ref, 2, terms)
            dmid = cot_ref[where, :].astype(jnp.float32) + dmid
            dmid_ref[where, :] = dmid
            o = o_ref[where, :].astype(jnp.float32)
            ro = rms_scale(o)
            add_row(sum_ref, 3, dmid * (o * ro * gain_ref[3:4]))
            do, terms = norm_back(dmid * gate, o, ro, gain_ref[3:4])
            add_row(sum_ref, 4, terms)
            do_ref[where, :] = do.astype(jnp.bfloat16)

        chunks(rows, min(64, rows), body)
        do = do_ref[...]
        q0 = dot(do, w0_ref[...], NT).astype(jnp.bfloat16)
        q1 = dot(do, w1_ref[...], NT).astype(jnp.bfloat16)
        half = q0.shape[1]
        da_ref[:, :half] = jnp.where(which == 0, q0, q1)
        da_ref[:, half:] = jnp.where(which == 0, q1, q0)


def ffn_back(which, dgu, w_gate_up, w_out, middle, cotangent, o, gains, mods, tile=512):
    rows = middle.shape[0]
    n = FF // tile
    half = D // 2
    full = small_spec((rows, D))
    gspec = pl.BlockSpec((half, tile), lambda j, w: (0, j))
    uspec = pl.BlockSpec((half, tile), lambda j, w: (0, j + n))
    return pl.pallas_call(
        ffn_back_kernel,
        grid_spec=pltpu.PrefetchScalarGridSpec(
            num_scalar_prefetch=1,
            grid=(n,),
            in_specs=[
                pl.BlockSpec((2, rows, tile), lambda j, w: (0, 0, j)),
                gspec, gspec, uspec, uspec, full, full, full,
                small_spec(w_out[0].shape), small_spec(w_out[1].shape),
                small_spec(gains.shape), small_spec(mods.shape),
            ],
            out_specs=[full, full, full, small_spec((8, D))],
            scratch_shapes=[pltpu.VMEM((2, rows, half), jnp.float32)],
        ),
        out_shape=[jax.ShapeDtypeStruct((rows, D), jnp.float32)]
        + [jax.ShapeDtypeStruct((rows, D), jnp.bfloat16)] * 2
        + [jax.ShapeDtypeStruct((8, D), jnp.float32)],
        compiler_params=params(60),
        cost_estimate=cost(4 * rows * D * FF + 2 * rows * D * D, 55e6),
    )(
        which, dgu, w_gate_up[0], w_gate_up[1], w_gate_up[0], w_gate_up[1],
        middle, cotangent, o, w_out[0], w_out[1], gains, mods,
    )


def qk_back_kernel(own_blocks, parts, *refs):
    dq_refs, dk_refs, dv_refs = refs[:parts], refs[parts : 2 * parts], refs[2 * parts : 3 * parts]
    qpre_ref, kpre_ref, cos_ref, sin_ref, gain_ref, dqkv_ref, sum_ref = refs[3 * parts :]
    pid = pl.program_id(0)

    @pl.when(pid == 0)
    def clear():
        sum_ref[...] = jnp.zeros_like(sum_ref)

    def back(grad_refs, pre_ref, row):
        pre = pre_ref[...].astype(jnp.float32)
        grad = jnp.concatenate([g[...] for g in grad_refs], axis=1).astype(jnp.float32)
        grad = turn(grad, cos_ref[...], -sin_ref[...])
        d, terms = norm_back(grad, pre, rms_scale(pre), gain_ref[row : row + 1])
        add_row(sum_ref, row, terms)
        return d.astype(jnp.bfloat16)

    dqkv_ref[:, D : 2 * D] = back(dk_refs, kpre_ref, 2)
    width = D // parts
    for i, ref in enumerate(dv_refs):
        dqkv_ref[:, 2 * D + i * width : 2 * D + (i + 1) * width] = ref[...]

    @pl.when(pid < own_blocks)
    def with_query():
        dqkv_ref[:, :D] = back(dq_refs, qpre_ref, 1)

    @pl.when(pid >= own_blocks)
    def no_query():
        dqkv_ref[:, :D] = jnp.zeros((dqkv_ref.shape[0], D), jnp.bfloat16)


def qk_back(dq, dk, dv, qpre, kpre, cosine, sine, gains):
    own, rows = dq[0].shape[0], dk[0].shape[0]
    parts = len(dq)
    step = min(128, own)
    blocks = own // step
    row = lambda n: pl.BlockSpec((step, n), lambda i: (i, 0))
    own_row = lambda n: pl.BlockSpec((step, n), lambda i: (jnp.minimum(i, blocks - 1), 0))
    return pl.pallas_call(
        functools.partial(qk_back_kernel, blocks, parts),
        grid=(rows // step,),
        in_specs=[own_row(D // parts)] * parts + [row(D // parts)] * (2 * parts)
        + [own_row(D), row(D), row(PAIR), row(PAIR), small_spec(gains.shape)],
        out_specs=[row(3 * D), small_spec((8, D))],
        out_shape=[
            jax.ShapeDtypeStruct((rows, 3 * D), jnp.bfloat16),
            jax.ShapeDtypeStruct((8, D), jnp.float32),
        ],
        compiler_params=params(),
        cost_estimate=cost(60 * rows * D, 30e6),
    )(*dq, *dk, *dv, qpre, kpre, cosine, sine, gains)


def project_back_kernel(with_query, dqkv_ref, tok_ref, w_ref, gain_ref, mod_ref, dx_ref, sum_ref):
    @pl.when(pl.program_id(0) == 0)
    def clear():
        sum_ref[...] = jnp.zeros_like(sum_ref)

    first = 0 if with_query else D
    dhm = dot(dqkv_ref[:, first:], w_ref[:, first:], NT)
    x = tok_ref[...].astype(jnp.float32)
    r1 = rms_scale(x)
    add_row(sum_ref, 3, dhm)
    add_row(sum_ref, 4, dhm * (x * r1 * gain_ref[0:1]))
    dx, terms = norm_back(dhm * (1.0 + mod_ref[1:2]), x, r1, gain_ref[0:1])
    add_row(sum_ref, 0, terms)
    dx_ref[...] = dx.astype(jnp.bfloat16)


def project_back(dqkv, first, own, tokens_all, full_qkv, gains, mods):
    rows = dqkv.shape[0] - own if first else own
    step = min(256, own)
    skip = first // step
    row = pl.BlockSpec((step, D), lambda i: (i + skip, 0))
    return pl.pallas_call(
        functools.partial(project_back_kernel, first == 0),
        grid=(max(rows // step, 1),),
        in_specs=[pl.BlockSpec((step, 3 * D), lambda i: (i + skip, 0)), row]
        + [pl.BlockSpec(full_qkv.shape, lambda i: (0, 0), pipeline_mode=pl.Buffered(1))]
        + [small_spec(gains.shape), small_spec(mods.shape)],
        out_specs=[pl.BlockSpec((step, D), lambda i: (i, 0)), small_spec((8, D))],
        out_shape=[
            jax.ShapeDtypeStruct((rows, D), jnp.bfloat16),
            jax.ShapeDtypeStruct((8, D), jnp.float32),
        ],
        compiler_params=params(),
        cost_estimate=cost(6 * rows * D * D, 30e6),
    )(dqkv, tokens_all, full_qkv, gains, mods)


def product_kernel(widths, has_received, where_ref, d_ref, a_ref, *refs):
    p = dot(d_ref[0], a_ref[...], TN)
    outs = refs[1:] if has_received else refs
    if has_received:
        p = p + refs[0][0].astype(jnp.float32)
    p = p.astype(jnp.bfloat16)
    start = 0
    for out, width in zip(outs, widths):
        out[0] = p[:, start : start + width]
        start += width


def product(dact, act, starts, lanes, received=None, widths=None):
    parts, tokens, columns = dact.shape
    count = len(starts)
    widths = list(widths or [lanes])
    tile = next(
        t for t in (2048, 1536, 1024, 512, 256, 128) if columns % t == 0 and t * lanes <= 2048 * 512
    )
    each = columns // tile
    spec = lambda w: pl.BlockSpec((1, tile, w), lambda n, k, s: (k, n, 0))
    return pl.pallas_call(
        functools.partial(product_kernel, widths, received is not None),
        grid_spec=pltpu.PrefetchScalarGridSpec(
            num_scalar_prefetch=1,
            grid=(parts * each, count),
            in_specs=[
                pl.BlockSpec((1, tokens, tile), lambda n, k, s: (n // each, 0, n % each)),
                pl.BlockSpec((tokens, lanes), lambda n, k, s: (0, s[k])),
            ]
            + ([] if received is None else [spec(lanes)]),
            out_specs=[spec(w) for w in widths],
        ),
        out_shape=[
            jax.ShapeDtypeStruct((count, parts * columns, w), jnp.bfloat16) for w in widths
        ],
        compiler_params=params(),
        cost_estimate=cost(
            2 * tokens * parts * columns * lanes * count, 4 * parts * columns * lanes * count
        ),
    )(jnp.stack(starts).astype(jnp.int32), dact, act, *([] if received is None else [received]))


def split_product_kernel(portions, count, where_ref, d_ref, *refs):
    acts, received, outs = refs[:count], refs[count], refs[count + 1 :]
    prods = [
        (dot(d_ref[0], acts[f][...], TN) + received[f].astype(jnp.float32)).astype(jnp.bfloat16)
        for f in range(count)
    ]
    half = prods[0].shape[0] // 2
    start = 0
    for i, (width, letter) in enumerate(portions):
        keep, send = outs[2 * i], outs[2 * i + 1]
        lanes = slice(start, start + width)
        start += width
        if letter == "y":
            keep[...] = prods[0][:, lanes]
            send[...] = prods[1][:, lanes]
        elif letter == "x":
            low = where_ref[count] == 0
            for f in range(count):
                a, b = prods[f][:half, lanes], prods[f][half:, lanes]
                keep[f] = jnp.where(low, a, b)
                send[f] = jnp.where(low, b, a)
        else:
            mine = pl.program_id(0) % 2 == where_ref[count + 1]

            @pl.when(mine)
            def to_keep(keep=keep, lanes=lanes):
                for f in range(count):
                    keep[f] = prods[f][:, lanes]

            @pl.when(jnp.logical_not(mine))
            def to_send(send=send, lanes=lanes):
                for f in range(count):
                    send[f] = prods[f][:, lanes]


def split_product(dact, act, starts, lanes, received, portions, bits, nd):
    parts, tokens, columns = dact.shape
    count = len(starts)
    total = parts * columns
    tile = 4 * (total // nd)
    each = columns // tile
    specs, shapes = [], []
    for width, letter in portions:
        if letter == "y":
            spec, shape = pl.BlockSpec((tile, width), lambda n, s: (n, 0)), (total, width)
        elif letter == "x":
            spec = pl.BlockSpec((count, tile // 2, width), lambda n, s: (0, n, 0))
            shape = (count, total // 2, width)
        else:
            spec = pl.BlockSpec((count, tile, width), lambda n, s: (0, n // 2, 0))
            shape = (count, total // 2, width)
        specs += [spec] * 2
        shapes += [jax.ShapeDtypeStruct(shape, jnp.bfloat16)] * 2
    act_spec = lambda f: pl.BlockSpec((tokens, lanes), lambda n, s: (0, s[f]))
    outs = pl.pallas_call(
        functools.partial(split_product_kernel, portions, count),
        grid_spec=pltpu.PrefetchScalarGridSpec(
            num_scalar_prefetch=1,
            grid=(total // tile,),
            in_specs=[pl.BlockSpec((1, tokens, tile), lambda n, s: (n // each, 0, n % each))]
            + [act_spec(f) for f in range(count)]
            + [pl.BlockSpec((count, tile, lanes), lambda n, s: (0, n, 0))],
            out_specs=specs,
        ),
        out_shape=shapes,
        compiler_params=params(),
        cost_estimate=cost(2 * tokens * total * lanes * count, 4 * total * lanes * count),
    )(jnp.stack(list(starts) + list(bits)).astype(jnp.int32), dact, *([act] * count), received)
    return list(zip(outs[::2], outs[1::2]))


ORDERS = ["yxz", "xzy", "zyx"]


def bits_of(size):
    return size.bit_length() - 1


def swap(value, axis, mask, size):
    return lax.ppermute(value, axis, [(i, i ^ mask) for i in range(size)])


def after(value, *earlier):
    return lax.optimization_barrier((value,) + earlier)[0]


def special(env):
    return env[1] == 2 and bits_of(env[0]) >= 3


def gather_pieces(shard, routes, env):
    nd, nf, me, mine = env
    if not special(env):
        full = lax.all_gather(shard, "fsdp", axis=0, tiled=True)
        half = full.shape[0] // 2
        return (full[:half], [full[half:]], [jnp.int32(0), jnp.int32(half)]), shard
    rows = shard.shape[0]
    chunk = rows // len(routes)
    pieces, starts, firsts = [], [], []
    for r, route in enumerate(routes):
        piece_rows = chunk >> len(route)
        index = sum(((me >> b) & 1) << i for i, b in enumerate(route))
        base = r * chunk + (mine ^ 1) * rows
        part = lax.dynamic_slice_in_dim(shard, r * chunk + index * piece_rows, piece_rows, 0)
        held = [(0, swap(part, "fsdp", 1, nf))]
        firsts.append(held[0][1])
        for i, b in enumerate(route):
            held = held + [(rel | (1 << i), swap(p, "dp", 1 << b, nd)) for rel, p in held]
        for rel, p in held:
            pieces.append(p)
            starts.append(base + (index ^ rel) * piece_rows)
    return (shard, pieces, [mine * rows] + starts), firsts


def gather_half(shard, env, hold, late):
    nd, nf, me, mine = env
    if not special(env):
        full = lax.all_gather(shard, "fsdp", axis=0, tiled=True)
        half = full.shape[0] // 2
        return (full[:half], full[half:]), shard
    rows = shard.shape[0] // 8
    part = after(lax.dynamic_slice_in_dim(shard, (me & 7) * rows, rows, 0), *hold)
    got = swap(part, "fsdp", 1, nf)
    groups = [list(range(i, i + 8)) for i in range(0, nd, 8)]
    if late:
        got = after(got, *late)
    other = lax.all_gather(got, "dp", axis=0, tiled=True, axis_index_groups=groups)
    return (shard, other), got


def gather_relative(value, env):
    nf = env[1]
    blocks = [value]
    for b in range(bits_of(nf)):
        blocks = blocks + [swap(p, "fsdp", 1 << b, nf) for p in blocks]
    return jnp.concatenate(blocks, axis=0)


def reduce_relative(value, env):
    nf = env[1]
    total = None
    for b in reversed(range(bits_of(nf))):
        half = value.shape[0] // 2
        got = swap(value[half:], "fsdp", 1 << b, nf)
        total = value[:half].astype(jnp.float32) + got.astype(jnp.float32)
        value = total.astype(jnp.bfloat16)
    return value.astype(jnp.float32) if total is None else total


def sum_fsdp(value, env, anchor=None):
    nf = env[1]
    for b in range(bits_of(nf)):
        got = swap(value.astype(jnp.bfloat16), "fsdp", 1 << b, nf)
        if anchor is not None:
            got = after(got, anchor)
        value = value + got.astype(jnp.float32)
    return value


def gather_small(pack, env):
    nf, mine = env[1], env[3]
    if nf != 2:
        return lax.all_gather(pack, "fsdp", axis=1, tiled=True)
    got = swap(pack, "fsdp", 1, nf)
    return jnp.concatenate(
        [jnp.where(mine == 0, pack, got), jnp.where(mine == 0, got, pack)], axis=1
    )


def stages_of(order, env):
    kinds = {
        "y": [("fsdp", b) for b in range(bits_of(env[1]))],
        "x": [("dp", 1)],
        "z": [("dp", 2)] if bits_of(env[0]) > 2 else [],
    }
    return [stage for letter in order for stage in kinds[letter]]


def add_low(terms):
    total = terms[0].astype(jnp.float32)
    for term in terms[1:]:
        total = total + term.astype(jnp.float32)
    return total.astype(jnp.bfloat16)


class Flow:
    most = 5

    def __init__(self, env):
        self.env, self.pending, self.flying = env, [], []

    def send(self, operand, axis, mask, land, rank):
        self.pending.append((operand, axis, mask, land, rank))

    def turn(self, outs, ins):
        nd, nf = self.env[:2]
        flying, self.flying = self.flying, []
        if flying:
            tied = lax.optimization_barrier(tuple(got for got, _ in flying) + tuple(outs))
            for got, (_, land) in zip(tied, flying):
                land(got)
        pending = sorted(self.pending, key=lambda p: p[4])
        pending, self.pending = pending[: self.most], pending[self.most :]
        sends = tuple(p[0] for p in pending)
        tied = lax.optimization_barrier(sends + tuple(ins) + tuple(outs))
        for operand, (_, axis, mask, land, _) in zip(tied, pending):
            size = nd if axis == "dp" else nf
            self.flying.append((swap(operand, axis, mask, size), land))
        return tied[len(sends) : len(sends) + len(ins)]

    def drain(self, outs):
        while self.flying or self.pending:
            self.turn(outs, ())
            outs = ()


class Ladder:
    def __init__(self, current, alive, stages, env):
        self.current, self.alive, self.stages, self.env = current, alive, stages, env
        self.sent = None

    def split(self, axis, b):
        t = self.current
        if axis == "fsdp":
            pairs = t.reshape((t.shape[0] // 2, 2) + t.shape[1:])
            return pairs[:, 0], pairs[:, 1]
        place = 1 + self.alive.index(b)
        bit = (self.env[2] >> b) & 1
        self.alive = [d for d in self.alive if d != b]
        before, after_dims = t.shape[:place], t.shape[place + 1 :]
        rows = 1
        for n in after_dims[:-1]:
            rows *= n
        count = 1
        for n in before:
            count *= n
        flat = t.reshape(count, 2, rows, t.shape[-1])
        pick = lambda i: lax.dynamic_index_in_dim(flat, i, 1, keepdims=False).reshape(
            before + after_dims
        )
        return pick(bit), pick(bit ^ 1)

    def launch(self, flow, landed, rank):
        axis, b = self.stages.pop(0)
        if self.sent is None:
            kept, send = self.split(axis, b)
        else:
            kept, send, self.sent = self.current, self.sent, None

        def land(got):
            self.current = add_low([kept, got.reshape(kept.shape)])
            landed()

        flow.send(send, axis, 1 << b, land, rank)


def join_rows(kept, got, env):
    core = env[2] & 1
    both = jnp.where(
        core == 0,
        jnp.concatenate([kept, got], axis=1),
        jnp.concatenate([got, kept], axis=1),
    )
    return both.T.astype(jnp.float32)


def core_product(dact, act, core, env, rows_only, received=None, widths=None):
    nd, nf, me, mine = env
    count = 1 if rows_only else nf
    lanes = act.shape[1] // (2 * count)
    blocks = [core] if rows_only else [2 * (mine ^ r) + core for r in range(nf)]
    if lanes % 128 == 0:
        outs = product(dact, act, blocks, lanes, received, widths)
        return outs if widths else outs[0]
    wide = jnp.concatenate(list(dact), axis=1)
    parts = [lax.dynamic_slice_in_dim(act, b * lanes, lanes, 1) for b in blocks]
    out = jnp.stack([dot(wide, p, TN) for p in parts])
    if received is not None:
        out = out + received.astype(jnp.float32)
    out = out.astype(jnp.bfloat16)
    if widths is None:
        return out
    cuts = [sum(widths[:i]) for i in range(len(widths))]
    return [out[:, :, a : a + w] for a, w in zip(cuts, widths)]


class Reduction:
    def __init__(self, dact, act, portions, flow, rank, rows_only=False):
        self.flow, self.env, self.act, self.rank = flow, flow.env, act, rank
        self.portions, self.rows_only = portions, rows_only
        core = self.env[2] & 1
        self.partial = core_product(dact, act, core ^ 1, self.env, rows_only)
        flow.send(self.partial, "dp", 1, self.receive, 0)

    def receive(self, got):
        self.sent = got

    def keep(self, dact):
        nd, nf, me, mine = self.env
        core, bits = me & 1, bits_of(nd)
        alive = list(range(bits - 1, 0, -1))
        tail = (2, self.sent.shape[1] // nd)
        self.ladders = []
        if special(self.env):
            count = 1 if self.rows_only else nf
            blocks = [core] if self.rows_only else [2 * (mine ^ r) + core for r in range(nf)]
            pairs = split_product(
                dact, self.act, blocks, self.act.shape[1] // (2 * count), self.sent,
                [(w, order[0]) for w, order in self.portions], [(me >> 1) & 1, (me >> 2) & 1], nd,
            )
            for (kept, sent), (_, order) in zip(pairs, self.portions):
                stages = stages_of(order, self.env)
                axis, b = stages[0]
                left = [d for d in alive if axis != "dp" or d != b]
                lead = 1 if axis == "fsdp" else count
                shape = (lead,) + (2,) * len(left) + tail + (kept.shape[-1],)
                ladder = Ladder(kept.reshape(shape), left, stages, self.env)
                ladder.sent = sent
                self.ladders.append(ladder)
            first = pairs[0][0]
        else:
            widths = [w for w, _ in self.portions]
            totals = core_product(dact, self.act, core, self.env, self.rows_only, self.sent, widths)
            for total, (_, order) in zip(totals, self.portions):
                shape = (total.shape[0],) + (2,) * (bits - 1) + tail + (total.shape[2],)
                stages = stages_of(order, self.env)
                self.ladders.append(Ladder(total.reshape(shape), alive, stages, self.env))
            first = totals[0]
        self.launch()
        return first

    def launch(self):
        ladders = self.ladders
        if ladders[0].stages:
            self.waiting = len(ladders)
            for ladder in ladders:
                ladder.launch(self.flow, self.landed, self.rank)
            return
        if len(ladders) > 1:
            joined = jnp.concatenate([r.current for r in ladders], axis=-1)
            self.ladders = ladders = [Ladder(joined, ladders[0].alive, [], self.env)]
        if ladders[0].alive:
            ladders[0].stages = [("dp", ladders[0].alive[-1])]
            self.launch()
            return
        core = self.env[2] & 1
        rows = ladders[0].current[0]
        kept = lax.dynamic_index_in_dim(rows, core, 0, keepdims=False)

        def land(got):
            self.result = join_rows(kept, got, self.env)

        sent = lax.dynamic_index_in_dim(rows, core ^ 1, 0, keepdims=False)
        self.flow.send(sent, "dp", 1, land, 3)

    def landed(self):
        self.waiting -= 1
        if not self.waiting:
            self.launch()


class WideSum:
    def __init__(self, value, axes, flow, rank):
        env = flow.env
        self.rank = rank
        self.value, self.flow = value, flow
        self.hops = [
            (axis, 1 << b)
            for axis in axes
            for b in range(bits_of(env[0] if axis == "dp" else env[1]))
        ]
        self.launch()

    def launch(self):
        if self.hops:
            axis, mask = self.hops.pop(0)
            self.flow.send(self.value, axis, mask, self.land, self.rank)

    def land(self, got):
        self.value = self.value.astype(jnp.float32) + got.astype(jnp.float32)
        if got.dtype == jnp.bfloat16:
            self.value = self.value.astype(jnp.bfloat16)
        self.launch()


def portion_list(lanes, names):
    units = lanes // 128
    if lanes % 128 or units < len(names):
        return [(lanes, names[-1])]
    cuts = [units * i // len(names) * 128 for i in range(len(names) + 1)]
    return [(b - a, n) for a, b, n in zip(cuts, cuts[1:], names)]


def per_device(
    tokens,
    caption,
    modulation,
    caption_mask,
    positions,
    w_qkv,
    w_out,
    w_caption_kv,
    w_gate_up,
    w_down,
    norm_gains,
    caption_gain,
    cross_gate,
    cotangent,
):
    nd, nf = lax.axis_size("dp"), lax.axis_size("fsdp")
    me, mine = lax.axis_index("dp"), lax.axis_index("fsdp")
    env = (nd, nf, me, mine)
    own_rows = tokens.shape[1]
    heads = cross_gate.shape[0]
    which = (mine if special(env) else jnp.int32(0)).astype(jnp.int32)[None]
    pack = jnp.concatenate(
        [
            norm_gains,
            modulation[0],
            caption_gain[None],
            jnp.pad(cross_gate, (0, caption_gain.shape[0] - heads))[None],
        ]
    )
    pack = gather_small(pack, env)
    places = gather_relative(positions[0].T, env)
    gath_qkv, firsts = gather_pieces(w_qkv, [(1, 2, 0), (2, 1, 0)], env)
    tokens_all = gather_relative(after(tokens[0], *firsts), env)
    partial_kv = dot(caption[0], w_caption_kv)
    tokens_all = after(tokens_all, partial_kv)
    late = tuple(gath_qkv[1]) + (tokens_all, pack, places)
    full_gate_up, got = gather_half(w_gate_up, env, firsts, late)
    full_out, _ = gather_half(w_out, env, (got,), late)
    pack = pack.astype(jnp.float32)
    gains, mods, cap_gain = pack[:6], pack[6:12], pack[12]
    gate_heads = jnp.tanh(pack[13].reshape(nf, -1)[:, :heads].reshape(HEADS))
    gate_tanh = jnp.repeat(gate_heads, HEAD_DIM)[None]
    cosine, sine = rope_tables(places)
    hm, full_qkv, query_b, key_b, value_b, query_pre, key_pre = project(
        tokens_all, own_rows, gains, mods, cosine, sine, gath_qkv
    )
    cap_rows = sum_fsdp(after(partial_kv, tokens_all), env, hm)
    ckey_pre = cap_rows[:, :D]
    ckey_scale = rms_scale(ckey_pre)
    ckey_b = (ckey_pre * ckey_scale * cap_gain).astype(jnp.bfloat16)
    cvalue_b = cap_rows[:, D:].astype(jnp.bfloat16)
    bias = jnp.where(caption_mask[0] > 0, 0.0, -1e30).astype(jnp.float32)
    combined, self_out, cross_out, stats = attend(
        query_b, key_b, value_b, ckey_b, cvalue_b, bias[None], gate_tanh
    )
    full_down, _ = gather_half(w_down, env, (cvalue_b,), (stats,))
    projected, middle, ffn_in = output_step(which, combined, full_out, tokens[0], gains, mods)
    gate_part, up_part, ffn_inner = gate_up_step(which, ffn_in, full_gate_up)
    block_out, grad_down, down_sums = down_step(
        which, ffn_inner, full_down, middle, cotangent[0], gains, mods
    )
    lanes_d, lanes_f = D // (2 * nf), FF // (2 * nf)
    flow = Flow(env)
    red_down = Reduction(grad_down[None], ffn_inner, portion_list(lanes_f, ORDERS), flow, 1)
    (grad_down_b,) = flow.turn((red_down.partial,), (grad_down,))
    dgu = gate_up_back(which, grad_down_b, gate_part, up_part, full_down)
    (grad_down_b,) = flow.turn((dgu,), (grad_down_b,))
    done = red_down.keep(grad_down_b[None])
    (dgu,) = flow.turn((done,), (dgu,))
    red_gate_up = Reduction(dgu, ffn_in, portion_list(lanes_d, ORDERS), flow, 1)
    (dgu_b,) = flow.turn((red_gate_up.partial,), (dgu,))
    grad_mid, grad_proj, grad_comb, ffn_sums = ffn_back(
        which, dgu_b, full_gate_up, full_out, middle, cotangent[0], projected, gains, mods
    )
    grad_comb, grad_proj = flow.turn((ffn_sums,), (grad_comb, grad_proj))
    dq_cross, grad_ckey, grad_cvalue, gate_sums = cross_back(
        query_b, ckey_b, cvalue_b, bias[:, None], gate_tanh, stats, grad_comb, cross_out
    )
    gate_terms = gate_sums[0].reshape(HEADS, HEAD_DIM).sum(axis=-1) * (1.0 - gate_heads**2)
    grad_ckey_pre, cap_gain_terms = norm_back(
        grad_ckey.astype(jnp.float32), ckey_pre, ckey_scale, cap_gain
    )
    grad_cap_kv = jnp.concatenate([grad_ckey_pre, grad_cvalue.astype(jnp.float32)], axis=-1)
    cap_sum = WideSum(grad_cap_kv.astype(jnp.bfloat16), ("fsdp",), flow, 0)
    red_out = Reduction(grad_proj[None], combined, portion_list(lanes_d, ORDERS[2:]), flow, 1.5)
    dgu_b, grad_comb = flow.turn((gate_sums, red_out.partial), (dgu_b, grad_comb))
    done = red_gate_up.keep(dgu_b)
    pairs = D // PAIR
    each = pairs // 4
    parts = []

    def attention_part(grads):
        parts.append(
            self_back(query_b, key_b, value_b, stats, grads, self_out, dq_cross, len(parts) * each, each)
        )
        return parts[-1][0]

    first = attention_part(grad_comb)
    while nf > 2 and cap_sum.hops:
        flow.turn((done,), ())
    grad_comb, grad_proj = flow.turn((done, first), (grad_comb, grad_proj))
    grad_cap_kv = cap_sum.value
    red_caption = Reduction(
        grad_cap_kv[None], caption[0], portion_list(caption.shape[2] // 2, ["xz", "zx"]), flow, 1.2, True
    )
    out_done = red_out.keep(grad_proj[None])
    dones = [attention_part(grad_comb) for _ in range(3)]
    grad_query, grad_key, grad_value = zip(*parts)
    (dq0,) = flow.turn([red_caption.partial, out_done] + dones, (grad_query[0],))
    grad_query = (dq0,) + grad_query[1:]
    grad_mixed, qk_sums = qk_back(
        grad_query, grad_key, grad_value, query_pre, key_pre, cosine, sine, gains
    )
    red_qkv = Reduction(grad_mixed[None], hm, portion_list(lanes_d, ORDERS), flow, 0.5)
    grad_mixed, grad_cap_kv = flow.turn((red_qkv.partial,), (grad_mixed, grad_cap_kv))
    done = red_caption.keep(grad_cap_kv[None])
    dx_other, other_sums = project_back(
        grad_mixed, own_rows, own_rows, tokens_all, full_qkv, gains, mods
    )
    dx_got = []
    if nf == 2:
        flow.send(dx_other, "fsdp", 1, dx_got.append, 0)
    (grad_mixed,) = flow.turn((done, other_sums), (grad_mixed,))
    done = red_qkv.keep(grad_mixed[None])
    dx_own, own_sums = project_back(grad_mixed, 0, own_rows, tokens_all, full_qkv, gains, mods)
    project_sums = own_sums + other_sums if nf > 1 else own_sums
    small = jnp.concatenate(
        [
            project_sums[:1],
            qk_sums[1:3],
            jnp.stack(
                [
                    ffn_sums[4],
                    ffn_sums[2],
                    down_sums[1],
                    jnp.sum(cap_gain_terms, axis=0),
                    jnp.pad(gate_terms, (0, D - HEADS)),
                ]
            ),
        ]
    )
    small_sum = WideSum(small, ("fsdp", "dp"), flow, 2)
    mod_grads = jnp.stack(
        [
            project_sums[3],
            project_sums[4],
            ffn_sums[3] * (1.0 - jnp.tanh(mods[2]) ** 2),
            ffn_sums[0],
            ffn_sums[1],
            down_sums[0] * (1.0 - jnp.tanh(mods[5]) ** 2),
        ]
    )
    mod_sum = WideSum(mod_grads, ("fsdp",), flow, 4)
    (grad_cap_kv,) = flow.turn((done, own_sums), (grad_cap_kv,))
    if nf == 2:
        dx = dx_own.astype(jnp.float32) + dx_got[0].astype(jnp.float32)
    else:
        dx = reduce_relative(jnp.concatenate([dx_own, dx_other]) if nf > 1 else dx_own, env)
    grad_tokens = (grad_mid + dx).astype(jnp.bfloat16)
    grad_caption = dot(grad_cap_kv, w_caption_kv, NT).astype(jnp.bfloat16)
    flow.drain((grad_caption, grad_tokens))
    small, mod_grads = small_sum.value, mod_sum.value
    out_down, out_gate_up, out_out, out_caption, out_qkv = (
        r.result for r in (red_down, red_gate_up, red_out, red_caption, red_qkv)
    )
    width = D // nf
    return (
        block_out[None],
        grad_tokens[None],
        grad_caption[None],
        lax.dynamic_slice_in_dim(mod_grads, mine * width, width, 1)[None],
        out_qkv,
        out_out,
        out_caption,
        out_gate_up,
        out_down,
        lax.dynamic_slice_in_dim(small[:6], mine * width, width, 1),
        lax.dynamic_slice_in_dim(small[6], mine * width, width, 0),
        lax.dynamic_slice_in_dim(small[7], mine * heads, heads, 0),
    )


def solution(mesh):
    placed = (
        P("dp", "fsdp", None),
        P("dp", None, "fsdp"),
        P("dp", None, "fsdp"),
        P("dp", None),
        P("dp", None, "fsdp"),
        P("fsdp", None),
        P("fsdp", None),
        P("fsdp", None),
        P("fsdp", None),
        P("fsdp", None),
        P(None, "fsdp"),
        P("fsdp"),
        P("fsdp"),
        P("dp", "fsdp", None),
    )
    return jax.shard_map(
        per_device,
        mesh=mesh,
        in_specs=placed,
        out_specs=(
            P("dp", "fsdp", None),
            P("dp", "fsdp", None),
            P("dp", None, "fsdp"),
            P("dp", None, "fsdp"),
            P("fsdp", "dp"),
            P("fsdp", "dp"),
            P("fsdp", "dp"),
            P("fsdp", "dp"),
            P("fsdp", "dp"),
            P(None, "fsdp"),
            P("fsdp"),
            P("fsdp"),
        ),
        check_vma=False,
    )
```

```python
import functools

import jax
import jax.numpy as jnp
from jax import lax
from jax.experimental import pallas as pl
from jax.experimental.pallas import tpu as pltpu
from jax.sharding import PartitionSpec as P

D = 1536
HEADS = 24
HEAD_DIM = 64
FF = 4096
EPS = 1e-05


def rms_scale(values):
    return lax.rsqrt(jnp.mean(values * values, axis=-1, keepdims=True) + EPS)


def norm_back(grad_normed, values, inv_rms, gain_row):
    scaled_grad = grad_normed * gain_row
    grad_values = inv_rms * scaled_grad - values * inv_rms**3 * jnp.mean(
        scaled_grad * values, axis=-1, keepdims=True
    )
    return (grad_values, grad_normed * values * inv_rms)


def rope_tables(positions):
    lane = jnp.arange(PAIR)
    frequency = 10000.0 ** (-(lane % 16).astype(jnp.float32) / 16)
    places = positions.astype(jnp.float32)
    angles = jnp.where((lane % 64 < 32)[None], places[:, :1], places[:, 1:]) * frequency
    sign = jnp.where(lane % 32 < 16, -1.0, 1.0).astype(jnp.float32)
    return jnp.cos(angles), jnp.sin(angles) * sign


PAIR = 2 * HEAD_DIM
NT = (((1,), (1,)), ((), ()))
TN = (((0,), (0,)), ((), ()))


def head_masks(dtype):
    lane = lax.broadcasted_iota(jnp.int32, (1, PAIR), 1)
    return [(lane < HEAD_DIM).astype(dtype), (lane >= HEAD_DIM).astype(dtype)]


def attend_kernel(q_ref, k_ref, v_ref, ck_ref, cv_ref, bias_ref, gate_ref, a_ref, o_ref, oy_ref, stat_ref):
    masks = head_masks(jnp.float32)
    rows = q_ref.shape[0]
    step = min(rows, 256)
    gate = gate_ref[...]
    for start in range(0, rows, step):
        where = pl.ds(start, step)
        q = q_ref[where, :].astype(jnp.float32) * HEAD_DIM**-0.5
        own, cross, stats = [], [], []
        for mask in masks:
            qm = (q * mask).astype(jnp.bfloat16)
            for keys, values, bias, outs in (
                (k_ref, v_ref, None, own),
                (ck_ref, cv_ref, bias_ref, cross),
            ):
                s = lax.dot_general(qm, keys[...], NT, preferred_element_type=jnp.float32)
                if bias is not None:
                    s = s + bias[...]
                top = jnp.max(s, axis=1, keepdims=True)
                e = jnp.exp(s - top)
                total = jnp.sum(e, axis=1, keepdims=True)
                out = jnp.dot(e.astype(jnp.bfloat16), values[...], preferred_element_type=jnp.float32)
                outs.append(out / total * mask)
                stats.append(top + jnp.log(total))
        o = own[0] + own[1]
        oy = cross[0] + cross[1]
        a_ref[where, :] = (o + gate * oy).astype(jnp.bfloat16)
        o_ref[where, :] = o.astype(jnp.bfloat16)
        oy_ref[where, :] = oy.astype(jnp.bfloat16)
        lane = lax.broadcasted_iota(jnp.int32, (step, PAIR), 1)
        tile = jnp.where(lane == 0, stats[0], jnp.where(lane == 1, stats[1], jnp.where(lane == 2, stats[2], stats[3])))
        stat_ref[0, :, where] = tile.T[:8, :]


def attend(query, key, value, ckey, cvalue, bias_row, gate_lanes):
    rows, keys, slots = query.shape[0], key.shape[0], ckey.shape[0]
    pairs = D // PAIR
    spec = lambda n: pl.BlockSpec((n, PAIR), lambda j: (0, j))
    return pl.pallas_call(
        attend_kernel,
        grid=(pairs,),
        in_specs=[
            spec(rows), spec(keys), spec(keys), spec(slots), spec(slots),
            pl.BlockSpec((1, slots), lambda j: (0, 0)), spec(1),
        ],
        out_specs=[spec(rows)] * 3 + [pl.BlockSpec((1, 8, rows), lambda j: (j, 0, 0))],
        out_shape=[jax.ShapeDtypeStruct((rows, D), jnp.bfloat16)] * 3
        + [jax.ShapeDtypeStruct((pairs, 8, rows), jnp.float32)],
        compiler_params=pltpu.CompilerParams(vmem_limit_bytes=48 * 2**20),
        cost_estimate=cost(16 * rows * (keys + slots) * D, 20e6, HEADS * rows * (keys + slots)),
    )(query, key, value, ckey, cvalue, bias_row, gate_lanes)


def back_part(k_tile, v_tile, bias, qm, grads, deltas, lses):
    masks = head_masks(jnp.bfloat16)
    dk = dv = add = None
    for h in range(2):
        st = dot(k_tile, qm[h], NT)
        if bias is not None:
            st = st + bias
        pt = jnp.exp(st - lses[h])
        dpt = dot(v_tile, grads[h], NT)
        dst = (pt * (dpt - deltas[h])).astype(jnp.bfloat16)
        terms = (
            dot(dst, qm[h]),
            dot(pt.astype(jnp.bfloat16), grads[h]),
            dot(dst, k_tile * masks[h], TN),
        )
        dk, dv, add = terms if h == 0 else (dk + terms[0], dv + terms[1], add + terms[2])
    return dk, dv, add


def head_sums(terms):
    t = terms.T
    return [
        jnp.sum(t[:HEAD_DIM], axis=0, keepdims=True),
        jnp.sum(t[HEAD_DIM:], axis=0, keepdims=True),
    ]


def split_heads(values):
    return [(values * m).astype(jnp.bfloat16) for m in head_masks(jnp.float32)]


def cross_back_kernel(q_ref, ck_ref, cv_ref, bias_ref, gate_ref, stat_ref, da_ref, oy_ref, dq_ref, dck_ref, dcv_ref, gsum_ref):
    qm = split_heads(q_ref[...].astype(jnp.float32) * HEAD_DIM**-0.5)
    da = da_ref[...].astype(jnp.float32)
    doy = (da * gate_ref[...]).astype(jnp.bfloat16).astype(jnp.float32)
    oy = oy_ref[...].astype(jnp.float32)
    gsum_ref[...] = jnp.sum(da * oy, axis=0, keepdims=True)
    stat = stat_ref[0]
    dk, dv, dq = back_part(
        ck_ref[...], cv_ref[...], bias_ref[...], qm, split_heads(doy), head_sums(doy * oy), [stat[1:2], stat[3:4]]
    )
    dck_ref[...] = dk.astype(dck_ref.dtype)
    dcv_ref[...] = dv.astype(dcv_ref.dtype)
    dq_ref[...] = (dq * HEAD_DIM**-0.5).astype(dq_ref.dtype)


def self_back_kernel(q_ref, k_ref, v_ref, stat_ref, da_ref, o_ref, dqc_ref, dq_ref, dk_ref, dv_ref):
    keys = k_ref.shape[0]
    step = min(keys, 256)
    qm = split_heads(q_ref[...].astype(jnp.float32) * HEAD_DIM**-0.5)
    da = da_ref[...].astype(jnp.float32)
    deltas = head_sums(da * o_ref[...].astype(jnp.float32))
    dam = split_heads(da)
    stat = stat_ref[0]
    dq = None
    for start in range(0, keys, step):
        where = pl.ds(start, step)
        dk, dv, add = back_part(k_ref[where, :], v_ref[where, :], None, qm, dam, deltas, [stat[0:1], stat[2:3]])
        dk_ref[where, :] = dk.astype(dk_ref.dtype)
        dv_ref[where, :] = dv.astype(dv_ref.dtype)
        dq = add if dq is None else dq + add
    dq = dq * HEAD_DIM**-0.5 + dqc_ref[...].astype(jnp.float32)
    dq_ref[...] = dq.astype(dq_ref.dtype)


def cross_back(query, ckey, cvalue, bias_col, gate_lanes, stats, grad_a, o_cross):
    rows, slots = query.shape[0], ckey.shape[0]
    pairs = D // PAIR
    spec = lambda n: pl.BlockSpec((n, PAIR), lambda j: (0, j))
    return pl.pallas_call(
        cross_back_kernel,
        grid=(pairs,),
        in_specs=[
            spec(rows), spec(slots), spec(slots),
            pl.BlockSpec((slots, 1), lambda j: (0, 0)), spec(1),
            pl.BlockSpec((1, 8, rows), lambda j: (j, 0, 0)),
            spec(rows), spec(rows),
        ],
        out_specs=[spec(rows), spec(slots), spec(slots), spec(1)],
        out_shape=[jax.ShapeDtypeStruct((n, D), jnp.bfloat16) for n in (rows, slots, slots)]
        + [jax.ShapeDtypeStruct((1, D), jnp.float32)],
        compiler_params=params(48),
        cost_estimate=cost(40 * rows * slots * D, 9e6, HEADS * rows * slots),
    )(query, ckey, cvalue, bias_col, gate_lanes, stats, grad_a, o_cross)


def self_back(query, key, value, stats, grad_a, o_self, dq_cross, first, count):
    rows, keys = query.shape[0], key.shape[0]
    spec = lambda n: pl.BlockSpec((n, PAIR), lambda j: (0, j + first))
    out = lambda n: pl.BlockSpec((n, PAIR), lambda j: (0, j))
    return pl.pallas_call(
        self_back_kernel,
        grid=(count,),
        in_specs=[
            spec(rows), spec(keys), spec(keys),
            pl.BlockSpec((1, 8, rows), lambda j: (j + first, 0, 0)),
            spec(rows), spec(rows), spec(rows),
        ],
        out_specs=[out(rows), out(keys), out(keys)],
        out_shape=[jax.ShapeDtypeStruct((n, count * PAIR), jnp.bfloat16) for n in (rows, keys, keys)],
        compiler_params=params(48),
        cost_estimate=cost(80 * rows * keys * count * PAIR, 1e6 * count, 2 * count * rows * keys),
    )(query, key, value, stats, grad_a, o_self, dq_cross)


NN = (((1,), (0,)), ((), ()))


def dot(a, b, dims=NN):
    return lax.dot_general(a, b, dims, preferred_element_type=jnp.float32)


def chunks(rows, step, body):
    def one(i, carry):
        body(pl.ds(pl.multiple_of(i * step, step), step))
        return carry

    lax.fori_loop(0, rows // step, one, 0)


def add_row(ref, index, terms):
    ref[index : index + 1, :] += jnp.sum(terms, axis=0, keepdims=True)


def partner(values):
    lane = lax.broadcasted_iota(jnp.int32, (values.shape[0], PAIR), 1)
    low = (lane & 31) < 16
    outs = []
    for start in range(0, values.shape[1], PAIR):
        tile = values[:, start : start + PAIR]
        outs.append(jnp.where(low, pltpu.roll(tile, PAIR - 16, 1), pltpu.roll(tile, 16, 1)))
    return jnp.concatenate(outs, axis=1)


def turn(values, cosine, sine):
    count = values.shape[1] // PAIR
    wide = lambda t: jnp.concatenate([t] * count, axis=1)
    return values * wide(cosine) + partner(values) * wide(sine)


def halves(values, which):
    mid = values.shape[1] // 2
    low, high = values[:, :mid], values[:, mid:]
    first = which == 0
    return jnp.where(first, low, high), jnp.where(first, high, low)


def small_spec(shape):
    return pl.BlockSpec(shape, lambda *_: (0,) * len(shape))


def params(mib=56):
    return pltpu.CompilerParams(vmem_limit_bytes=mib * 2**20)


def cost(flops, nbytes, trans=0):
    share = 0.05
    return pl.CostEstimate(
        flops=int(flops * share), bytes_accessed=int(nbytes * share), transcendentals=int(trans * share)
    )


def project_kernel(parts, own_rows, where_ref, tok_ref, other_ref, gain_ref, mod_ref, cos_ref, sin_ref, own_ref, *refs):
    pieces = refs[:parts]
    hm_ref, full_ref, q_ref, k_ref, v_ref, qpre_ref, kpre_ref, pre_ref = refs[parts:]
    pid = pl.program_id(0)
    rows = own_rows + other_ref.shape[0]
    step = min(128, own_rows)
    tile = full_ref.shape[1]
    per = D // tile

    @pl.when(pid == 0)
    def hidden():
        for source, first in ((tok_ref, 0), (other_ref, own_rows)):

            def body(i, carry, source=source, first=first):
                x = source[pl.ds(pl.multiple_of(i * step, step), step), :].astype(jnp.float32)
                hid = x * rms_scale(x) * gain_ref[0:1]
                hid = (hid * (1.0 + mod_ref[1:2]) + mod_ref[0:1]).astype(jnp.bfloat16)
                hm_ref[pl.ds(pl.multiple_of(first + i * step, step), step), :] = hid
                return carry

            lax.fori_loop(0, source.shape[0] // step, body, 0)

    n = own_ref.shape[0]
    full_ref[pl.ds(pl.multiple_of(where_ref[0], n), n), :] = own_ref[...]
    i = 1
    for piece in pieces:
        n = piece.shape[1]
        for k in range(piece.shape[0]):
            full_ref[pl.ds(pl.multiple_of(where_ref[i], n), n), :] = piece[k]
            i += 1

    for j in range(2 * per):
        count = own_rows if j < per else rows

        @pl.when(pid == j)
        def pre(j=j, count=count):
            pre_ref[:count, (j % per) * tile : (j % per + 1) * tile] = dot(
                hm_ref[:count, :], full_ref[...]
            )

    @pl.when(pid >= 2 * per)
    def value():
        v_ref[...] = dot(hm_ref[...], full_ref[...]).astype(jnp.bfloat16)

    for last, count, out, keep, gain in (
        (per - 1, own_rows, q_ref, qpre_ref, 1),
        (2 * per - 1, rows, k_ref, kpre_ref, 2),
    ):

        @pl.when(pid == last)
        def finish(count=count, out=out, keep=keep, gain=gain):
            def body(where):
                p = pre_ref[where, :]
                n = p * rms_scale(p) * gain_ref[gain : gain + 1]
                out[where, :] = turn(n, cos_ref[where, :], sin_ref[where, :]).astype(jnp.bfloat16)
                keep[where, :] = p.astype(jnp.bfloat16)

            chunks(count, min(step, count), body)


def project(tokens, others, gains, mods, cosine, sine, weight, tile=512):
    own, pieces, starts = weight
    own_rows = tokens.shape[0]
    rows = own_rows + others.shape[0]
    n = 3 * D // tile
    vtile = 2 * D // tile
    outs = [
        ((rows, D), jnp.bfloat16, None),
        ((D, 3 * D), jnp.bfloat16, pl.BlockSpec((D, tile), lambda j, w: (0, j))),
        ((own_rows, D), jnp.bfloat16, None),
        ((rows, D), jnp.bfloat16, None),
        ((rows, D), jnp.bfloat16, pl.BlockSpec((rows, tile), lambda j, w: (0, jnp.maximum(j - vtile, 0)))),
        ((own_rows, D), jnp.bfloat16, None),
        ((rows, D), jnp.bfloat16, None),
    ]
    return pl.pallas_call(
        functools.partial(project_kernel, len(pieces), own_rows),
        grid_spec=pltpu.PrefetchScalarGridSpec(
            num_scalar_prefetch=1,
            grid=(n,),
            in_specs=[small_spec(a.shape) for a in (tokens, others, gains, mods, cosine, sine)]
            + [pl.BlockSpec((own.shape[0], tile), lambda j, w: (0, j))]
            + [pl.BlockSpec(p.shape[:2] + (tile,), lambda j, w: (0, 0, j)) for p in pieces],
            out_specs=[s if s is not None else small_spec(shape) for shape, _, s in outs],
            scratch_shapes=[pltpu.VMEM((rows, D), jnp.float32)],
        ),
        out_shape=[jax.ShapeDtypeStruct(shape, d) for shape, d, _ in outs],
        compiler_params=params(58),
        cost_estimate=cost(2 * D * D * (own_rows + 2 * rows), 60e6),
    )(jnp.stack(starts).astype(jnp.int32), tokens, others, gains, mods, cosine, sine, own, *pieces)


def output_kernel(which_ref, a_ref, w0_ref, w1_ref, x_ref, gain_ref, mod_ref, o_ref, mid_ref, hfm_ref):
    a0, a1 = halves(a_ref[...], which_ref[0])
    o = dot(a0, w0_ref[...]) + dot(a1, w1_ref[...])
    o_ref[...] = o.astype(jnp.bfloat16)
    on = o * rms_scale(o) * gain_ref[3:4]
    mid = x_ref[...].astype(jnp.float32) + jnp.tanh(mod_ref[2:3]) * on
    mid_ref[...] = mid
    hf = mid * rms_scale(mid) * gain_ref[4:5]
    hfm_ref[...] = (hf * (1.0 + mod_ref[4:5]) + mod_ref[3:4]).astype(jnp.bfloat16)


def output_step(which, combined, weight, tokens, gains, mods):
    rows = combined.shape[0]
    step = min(rows, 256)
    row_spec = pl.BlockSpec((step, D), lambda i, w: (i, 0))
    return pl.pallas_call(
        output_kernel,
        grid_spec=pltpu.PrefetchScalarGridSpec(
            num_scalar_prefetch=1,
            grid=(rows // step,),
            in_specs=[row_spec, small_spec(weight[0].shape), small_spec(weight[1].shape), row_spec]
            + [small_spec(gains.shape), small_spec(mods.shape)],
            out_specs=[row_spec] * 3,
        ),
        out_shape=[
            jax.ShapeDtypeStruct((rows, D), jnp.bfloat16),
            jax.ShapeDtypeStruct((rows, D), jnp.float32),
            jax.ShapeDtypeStruct((rows, D), jnp.bfloat16),
        ],
        compiler_params=params(),
        cost_estimate=cost(2 * rows * D * D, 15e6),
    )(which, combined, weight[0], weight[1], tokens, gains, mods)


def gate_up_kernel(which_ref, h_ref, g0_ref, g1_ref, u0_ref, u1_ref, ga_ref, up_ref, ff_ref, hs_ref):
    @pl.when(pl.program_id(0) == 0)
    def split():
        hs_ref[0], hs_ref[1] = halves(h_ref[...], which_ref[0])

    ga = dot(hs_ref[0], g0_ref[...]) + dot(hs_ref[1], g1_ref[...])
    up = dot(hs_ref[0], u0_ref[...]) + dot(hs_ref[1], u1_ref[...])
    ga_ref[...] = ga.astype(jnp.bfloat16)
    up_ref[...] = up.astype(jnp.bfloat16)
    ff_ref[...] = (ga / (1.0 + jnp.exp(-ga)) * up).astype(jnp.bfloat16)


def gate_up_step(which, hfm, weight, tile=512):
    rows = hfm.shape[0]
    n = FF // tile
    half = D // 2
    spec = lambda off: pl.BlockSpec((half, tile), lambda j, w: (0, j + off))
    out = pl.BlockSpec((rows, tile), lambda j, w: (0, j))
    return pl.pallas_call(
        gate_up_kernel,
        grid_spec=pltpu.PrefetchScalarGridSpec(
            num_scalar_prefetch=1,
            grid=(n,),
            in_specs=[small_spec(hfm.shape), spec(0), spec(0), spec(n), spec(n)],
            out_specs=[out] * 3,
            scratch_shapes=[pltpu.VMEM((2, rows, half), jnp.bfloat16)],
        ),
        out_shape=[jax.ShapeDtypeStruct((rows, FF), jnp.bfloat16)] * 3,
        compiler_params=params(),
        cost_estimate=cost(4 * rows * D * FF, 40e6, rows * FF),
    )(which, hfm, weight[0], weight[1], weight[0], weight[1])


def down_kernel(which_ref, ff_ref, w0_ref, w1_ref, mid_ref, cot_ref, gain_ref, mod_ref, out_ref, df_ref, sum_ref, f_ref, hs_ref):
    pid = pl.program_id(0)
    tile = w0_ref.shape[1]
    rows = ff_ref.shape[0]

    @pl.when(pid == 0)
    def split():
        hs_ref[0], hs_ref[1] = halves(ff_ref[...], which_ref[0])

    f_ref[pid] = dot(hs_ref[0], w0_ref[...]) + dot(hs_ref[1], w1_ref[...])

    @pl.when(pid == pl.num_programs(0) - 1)
    def finish():
        gate = jnp.tanh(mod_ref[5:6])
        sum_ref[...] = jnp.zeros_like(sum_ref)

        def body(where):
            f = jnp.concatenate([f_ref[j, where, :] for j in range(D // tile)], axis=1)
            rf = rms_scale(f)
            fn = f * rf * gain_ref[5:6]
            dy = cot_ref[where, :].astype(jnp.float32)
            out_ref[where, :] = (mid_ref[where, :] + gate * fn).astype(jnp.bfloat16)
            dfn = dy * gate
            add_row(sum_ref, 0, dy * fn)
            df, terms = norm_back(dfn, f, rf, gain_ref[5:6])
            add_row(sum_ref, 1, terms)
            df_ref[where, :] = df.astype(jnp.bfloat16)

        chunks(rows, min(64, rows), body)


def down_step(which, ffh, weight, middle, cotangent, gains, mods, tile=256):
    rows = ffh.shape[0]
    half = FF // 2
    spec = pl.BlockSpec((half, tile), lambda j, w: (0, j))
    full = small_spec((rows, D))
    return pl.pallas_call(
        down_kernel,
        grid_spec=pltpu.PrefetchScalarGridSpec(
            num_scalar_prefetch=1,
            grid=(D // tile,),
            in_specs=[small_spec(ffh.shape), spec, spec, full, full, small_spec(gains.shape), small_spec(mods.shape)],
            out_specs=[full, full, small_spec((8, D))],
            scratch_shapes=[
                pltpu.VMEM((D // tile, rows, tile), jnp.float32),
                pltpu.VMEM((2, rows, half), jnp.bfloat16),
            ],
        ),
        out_shape=[jax.ShapeDtypeStruct((rows, D), jnp.bfloat16)] * 2
        + [jax.ShapeDtypeStruct((8, D), jnp.float32)],
        compiler_params=params(),
        cost_estimate=cost(2 * rows * D * FF, 24e6),
    )(which, ffh, weight[0], weight[1], middle, cotangent, gains, mods)


def gate_up_back_kernel(which_ref, df_ref, ga_ref, up_ref, d0_ref, d1_ref, dgu_ref):
    pid = pl.program_id(0)
    n = pl.num_programs(0)

    def work(w_ref):
        dffh = dot(df_ref[...], w_ref[...], NT)
        ga = ga_ref[...].astype(jnp.float32)
        up = up_ref[...].astype(jnp.float32)
        s = 1.0 / (1.0 + jnp.exp(-ga))
        dgu_ref[0] = (dffh * up * (s * (1.0 + ga * (1.0 - s)))).astype(jnp.bfloat16)
        dgu_ref[1] = (dffh * (ga * s)).astype(jnp.bfloat16)

    @pl.when(pid < n // 2)
    def first():
        work(d0_ref)

    @pl.when(pid >= n // 2)
    def second():
        work(d1_ref)


def gate_up_back(which, df, ga, up, w_down, tile=512):
    rows = df.shape[0]
    n = FF // tile
    h = n // 2
    cols = pl.BlockSpec((rows, tile), lambda j, w: (0, (j + w[0] * h) % n))
    return pl.pallas_call(
        gate_up_back_kernel,
        grid_spec=pltpu.PrefetchScalarGridSpec(
            num_scalar_prefetch=1,
            grid=(n,),
            in_specs=[
                small_spec((rows, D)), cols, cols,
                pl.BlockSpec((tile, D), lambda j, w: (jnp.minimum(j, h - 1), 0)),
                pl.BlockSpec((tile, D), lambda j, w: (jnp.maximum(j - h, 0), 0)),
            ],
            out_specs=pl.BlockSpec((2, rows, tile), lambda j, w: (0, 0, (j + w[0] * h) % n)),
        ),
        out_shape=jax.ShapeDtypeStruct((2, rows, FF), jnp.bfloat16),
        compiler_params=params(),
        cost_estimate=cost(2 * rows * D * FF, 30e6, rows * FF),
    )(which, df, ga, up, w_down[0], w_down[1])


def ffn_back_kernel(
    which_ref, dgu_ref, g0_ref, g1_ref, u0_ref, u1_ref,
    mid_ref, cot_ref, o_ref, w0_ref, w1_ref, gain_ref, mod_ref,
    dmid_ref, do_ref, da_ref, sum_ref, acc_ref,
):
    pid = pl.program_id(0)
    n = pl.num_programs(0)
    rows = mid_ref.shape[0]
    which = which_ref[0]
    dga, dup = dgu_ref[0], dgu_ref[1]
    p0 = dot(dga, g0_ref[...], NT) + dot(dup, u0_ref[...], NT)
    p1 = dot(dga, g1_ref[...], NT) + dot(dup, u1_ref[...], NT)

    @pl.when(pid == 0)
    def clear():
        acc_ref[which] = p0
        acc_ref[1 - which] = p1

    @pl.when(pid > 0)
    def more():
        acc_ref[which] += p0
        acc_ref[1 - which] += p1

    @pl.when(pid == n - 1)
    def finish():
        sum_ref[...] = jnp.zeros_like(sum_ref)
        gate = jnp.tanh(mod_ref[2:3])

        def body(where):
            dhfm = jnp.concatenate([acc_ref[0, where, :], acc_ref[1, where, :]], axis=1)
            mid = mid_ref[where, :]
            r2 = rms_scale(mid)
            add_row(sum_ref, 0, dhfm)
            add_row(sum_ref, 1, dhfm * (mid * r2 * gain_ref[4:5]))
            dmid, terms = norm_back(dhfm * (1.0 + mod_ref[4:5]), mid, r2, gain_ref[4:5])
            add_row(sum_ref, 2, terms)
            dmid = cot_ref[where, :].astype(jnp.float32) + dmid
            dmid_ref[where, :] = dmid
            o = o_ref[where, :].astype(jnp.float32)
            ro = rms_scale(o)
            add_row(sum_ref, 3, dmid * (o * ro * gain_ref[3:4]))
            do, terms = norm_back(dmid * gate, o, ro, gain_ref[3:4])
            add_row(sum_ref, 4, terms)
            do_ref[where, :] = do.astype(jnp.bfloat16)

        chunks(rows, min(64, rows), body)
        do = do_ref[...]
        q0 = dot(do, w0_ref[...], NT).astype(jnp.bfloat16)
        q1 = dot(do, w1_ref[...], NT).astype(jnp.bfloat16)
        half = q0.shape[1]
        da_ref[:, :half] = jnp.where(which == 0, q0, q1)
        da_ref[:, half:] = jnp.where(which == 0, q1, q0)


def ffn_back(which, dgu, w_gate_up, w_out, middle, cotangent, o, gains, mods, tile=512):
    rows = middle.shape[0]
    n = FF // tile
    half = D // 2
    full = small_spec((rows, D))
    gspec = pl.BlockSpec((half, tile), lambda j, w: (0, j))
    uspec = pl.BlockSpec((half, tile), lambda j, w: (0, j + n))
    return pl.pallas_call(
        ffn_back_kernel,
        grid_spec=pltpu.PrefetchScalarGridSpec(
            num_scalar_prefetch=1,
            grid=(n,),
            in_specs=[
                pl.BlockSpec((2, rows, tile), lambda j, w: (0, 0, j)),
                gspec, gspec, uspec, uspec, full, full, full,
                small_spec(w_out[0].shape), small_spec(w_out[1].shape),
                small_spec(gains.shape), small_spec(mods.shape),
            ],
            out_specs=[full, full, full, small_spec((8, D))],
            scratch_shapes=[pltpu.VMEM((2, rows, half), jnp.float32)],
        ),
        out_shape=[jax.ShapeDtypeStruct((rows, D), jnp.float32)]
        + [jax.ShapeDtypeStruct((rows, D), jnp.bfloat16)] * 2
        + [jax.ShapeDtypeStruct((8, D), jnp.float32)],
        compiler_params=params(60),
        cost_estimate=cost(4 * rows * D * FF + 2 * rows * D * D, 55e6),
    )(
        which, dgu, w_gate_up[0], w_gate_up[1], w_gate_up[0], w_gate_up[1],
        middle, cotangent, o, w_out[0], w_out[1], gains, mods,
    )


def qk_back_kernel(own_blocks, parts, *refs):
    dq_refs, dk_refs, dv_refs = refs[:parts], refs[parts : 2 * parts], refs[2 * parts : 3 * parts]
    qpre_ref, kpre_ref, cos_ref, sin_ref, gain_ref, dqkv_ref, sum_ref = refs[3 * parts :]
    pid = pl.program_id(0)

    @pl.when(pid == 0)
    def clear():
        sum_ref[...] = jnp.zeros_like(sum_ref)

    def back(grad_refs, pre_ref, row):
        pre = pre_ref[...].astype(jnp.float32)
        grad = jnp.concatenate([g[...] for g in grad_refs], axis=1).astype(jnp.float32)
        grad = turn(grad, cos_ref[...], -sin_ref[...])
        d, terms = norm_back(grad, pre, rms_scale(pre), gain_ref[row : row + 1])
        add_row(sum_ref, row, terms)
        return d.astype(jnp.bfloat16)

    dqkv_ref[:, D : 2 * D] = back(dk_refs, kpre_ref, 2)
    width = D // parts
    for i, ref in enumerate(dv_refs):
        dqkv_ref[:, 2 * D + i * width : 2 * D + (i + 1) * width] = ref[...]

    @pl.when(pid < own_blocks)
    def with_query():
        dqkv_ref[:, :D] = back(dq_refs, qpre_ref, 1)

    @pl.when(pid >= own_blocks)
    def no_query():
        dqkv_ref[:, :D] = jnp.zeros((dqkv_ref.shape[0], D), jnp.bfloat16)


def qk_back(dq, dk, dv, qpre, kpre, cosine, sine, gains):
    own, rows = dq[0].shape[0], dk[0].shape[0]
    parts = len(dq)
    step = min(128, own)
    blocks = own // step
    row = lambda n: pl.BlockSpec((step, n), lambda i: (i, 0))
    own_row = lambda n: pl.BlockSpec((step, n), lambda i: (jnp.minimum(i, blocks - 1), 0))
    return pl.pallas_call(
        functools.partial(qk_back_kernel, blocks, parts),
        grid=(rows // step,),
        in_specs=[own_row(D // parts)] * parts + [row(D // parts)] * (2 * parts)
        + [own_row(D), row(D), row(PAIR), row(PAIR), small_spec(gains.shape)],
        out_specs=[row(3 * D), small_spec((8, D))],
        out_shape=[
            jax.ShapeDtypeStruct((rows, 3 * D), jnp.bfloat16),
            jax.ShapeDtypeStruct((8, D), jnp.float32),
        ],
        compiler_params=params(),
        cost_estimate=cost(60 * rows * D, 30e6),
    )(*dq, *dk, *dv, qpre, kpre, cosine, sine, gains)


def project_back_kernel(with_query, dqkv_ref, tok_ref, w_ref, gain_ref, mod_ref, dx_ref, sum_ref):
    @pl.when(pl.program_id(0) == 0)
    def clear():
        sum_ref[...] = jnp.zeros_like(sum_ref)

    first = 0 if with_query else D
    dhm = dot(dqkv_ref[:, first:], w_ref[:, first:], NT)
    x = tok_ref[...].astype(jnp.float32)
    r1 = rms_scale(x)
    add_row(sum_ref, 3, dhm)
    add_row(sum_ref, 4, dhm * (x * r1 * gain_ref[0:1]))
    dx, terms = norm_back(dhm * (1.0 + mod_ref[1:2]), x, r1, gain_ref[0:1])
    add_row(sum_ref, 0, terms)
    dx_ref[...] = dx.astype(jnp.bfloat16)


def project_back(dqkv, first, own, tokens, full_qkv, gains, mods):
    rows = dqkv.shape[0] - own if first else own
    step = min(256, own)
    skip = first // step
    row = pl.BlockSpec((step, D), lambda i: (i, 0))
    return pl.pallas_call(
        functools.partial(project_back_kernel, first == 0),
        grid=(max(rows // step, 1),),
        in_specs=[pl.BlockSpec((step, 3 * D), lambda i: (i + skip, 0)), row]
        + [pl.BlockSpec(full_qkv.shape, lambda i: (0, 0), pipeline_mode=pl.Buffered(1))]
        + [small_spec(gains.shape), small_spec(mods.shape)],
        out_specs=[pl.BlockSpec((step, D), lambda i: (i, 0)), small_spec((8, D))],
        out_shape=[
            jax.ShapeDtypeStruct((rows, D), jnp.bfloat16),
            jax.ShapeDtypeStruct((8, D), jnp.float32),
        ],
        compiler_params=params(),
        cost_estimate=cost(6 * rows * D * D, 30e6),
    )(dqkv, tokens, full_qkv, gains, mods)


def product_kernel(widths, has_received, where_ref, d_ref, a_ref, *refs):
    p = dot(d_ref[0], a_ref[...], TN)
    outs = refs[1:] if has_received else refs
    if has_received:
        p = p + refs[0][0].astype(jnp.float32)
    p = p.astype(jnp.bfloat16)
    start = 0
    for out, width in zip(outs, widths):
        out[0] = p[:, start : start + width]
        start += width


def product(dact, act, starts, lanes, received=None, widths=None):
    parts, tokens, columns = dact.shape
    count = len(starts)
    widths = list(widths or [lanes])
    tile = next(
        t for t in (2048, 1536, 1024, 512, 256, 128) if columns % t == 0 and t * lanes <= 2048 * 512
    )
    each = columns // tile
    spec = lambda w: pl.BlockSpec((1, tile, w), lambda n, k, s: (k, n, 0))
    return pl.pallas_call(
        functools.partial(product_kernel, widths, received is not None),
        grid_spec=pltpu.PrefetchScalarGridSpec(
            num_scalar_prefetch=1,
            grid=(parts * each, count),
            in_specs=[
                pl.BlockSpec((1, tokens, tile), lambda n, k, s: (n // each, 0, n % each)),
                pl.BlockSpec((tokens, lanes), lambda n, k, s: (0, s[k])),
            ]
            + ([] if received is None else [spec(lanes)]),
            out_specs=[spec(w) for w in widths],
        ),
        out_shape=[
            jax.ShapeDtypeStruct((count, parts * columns, w), jnp.bfloat16) for w in widths
        ],
        compiler_params=params(),
        cost_estimate=cost(
            2 * tokens * parts * columns * lanes * count, 4 * parts * columns * lanes * count
        ),
    )(jnp.stack(starts).astype(jnp.int32), dact, act, *([] if received is None else [received]))


def split_product_kernel(portions, count, where_ref, d_ref, *refs):
    acts, received, outs = refs[:count], refs[count], refs[count + 1 :]
    prods = [
        (dot(d_ref[0], acts[f][...], TN) + received[f].astype(jnp.float32)).astype(jnp.bfloat16)
        for f in range(count)
    ]
    half = prods[0].shape[0] // 2
    start = 0
    for i, (width, letter) in enumerate(portions):
        keep, send = outs[2 * i], outs[2 * i + 1]
        lanes = slice(start, start + width)
        start += width
        if letter == "y":
            keep[...] = prods[0][:, lanes]
            send[...] = prods[1][:, lanes]
        elif letter == "x":
            low = where_ref[count] == 0
            for f in range(count):
                a, b = prods[f][:half, lanes], prods[f][half:, lanes]
                keep[f] = jnp.where(low, a, b)
                send[f] = jnp.where(low, b, a)
        else:
            mine = pl.program_id(0) % 2 == where_ref[count + 1]

            @pl.when(mine)
            def to_keep(keep=keep, lanes=lanes):
                for f in range(count):
                    keep[f] = prods[f][:, lanes]

            @pl.when(jnp.logical_not(mine))
            def to_send(send=send, lanes=lanes):
                for f in range(count):
                    send[f] = prods[f][:, lanes]


def split_product(dact, act, starts, lanes, received, portions, bits, nd):
    parts, tokens, columns = dact.shape
    count = len(starts)
    total = parts * columns
    tile = 4 * (total // nd)
    each = columns // tile
    specs, shapes = [], []
    for width, letter in portions:
        if letter == "y":
            spec, shape = pl.BlockSpec((tile, width), lambda n, s: (n, 0)), (total, width)
        elif letter == "x":
            spec = pl.BlockSpec((count, tile // 2, width), lambda n, s: (0, n, 0))
            shape = (count, total // 2, width)
        else:
            spec = pl.BlockSpec((count, tile, width), lambda n, s: (0, n // 2, 0))
            shape = (count, total // 2, width)
        specs += [spec] * 2
        shapes += [jax.ShapeDtypeStruct(shape, jnp.bfloat16)] * 2
    act_spec = lambda f: pl.BlockSpec((tokens, lanes), lambda n, s: (0, s[f]))
    outs = pl.pallas_call(
        functools.partial(split_product_kernel, portions, count),
        grid_spec=pltpu.PrefetchScalarGridSpec(
            num_scalar_prefetch=1,
            grid=(total // tile,),
            in_specs=[pl.BlockSpec((1, tokens, tile), lambda n, s: (n // each, 0, n % each))]
            + [act_spec(f) for f in range(count)]
            + [pl.BlockSpec((count, tile, lanes), lambda n, s: (0, n, 0))],
            out_specs=specs,
        ),
        out_shape=shapes,
        compiler_params=params(),
        cost_estimate=cost(2 * tokens * total * lanes * count, 4 * total * lanes * count),
    )(jnp.stack(list(starts) + list(bits)).astype(jnp.int32), dact, *([act] * count), received)
    return list(zip(outs[::2], outs[1::2]))


ORDERS = ["yxz", "xzy", "zyx"]


def bits_of(size):
    return size.bit_length() - 1


def swap(value, axis, mask, size):
    return lax.ppermute(value, axis, [(i, i ^ mask) for i in range(size)])


def after(value, *earlier):
    return lax.optimization_barrier((value,) + earlier)[0]


def special(env):
    return env[1] == 2 and bits_of(env[0]) >= 3


class Pieces:
    def __init__(self, shard, first, chunk, route, flow):
        nd, nf, me, mine = flow.env
        self.flow, self.route, self.stack = flow, list(enumerate(route)), None
        rows = chunk >> len(route)
        index = sum(((me >> b) & 1) << i for i, b in enumerate(route))
        base = first + (mine ^ 1) * shard.shape[0]
        self.starts = [base + (index ^ rel) * rows for rel in range(1 << len(route))]
        part = lax.dynamic_slice_in_dim(shard, first + index * rows, rows, 0)
        flow.send(part[None], "fsdp", 1, self.land, 0)

    def land(self, got):
        held = [] if self.stack is None else [self.stack]
        if not self.route:
            self.pieces = held + [got]
            return
        self.stack = jnp.concatenate(held + [got]) if held else got
        if self.route:
            _, b = self.route.pop(0)
            self.flow.send(self.stack, "dp", 1 << b, self.land, 0)


def slice_for(shard, env):
    rows = shard.shape[0] // 8
    return lax.dynamic_slice_in_dim(shard, (env[2] & 7) * rows, rows, 0)


def gather_half(shard, got, env):
    nd = env[0]
    if not special(env):
        full = lax.all_gather(shard, "fsdp", axis=0, tiled=True)
        half = full.shape[0] // 2
        return (full[:half], full[half:])
    groups = [list(range(i, i + 8)) for i in range(0, nd, 8)]
    return (shard, lax.all_gather(got, "dp", axis=0, tiled=True, axis_index_groups=groups))


def gather_relative(value, env):
    nf = env[1]
    blocks = [value]
    for b in range(bits_of(nf)):
        blocks = blocks + [swap(p, "fsdp", 1 << b, nf) for p in blocks]
    return jnp.concatenate(blocks, axis=0)


def reduce_relative(value, env):
    nf = env[1]
    total = None
    for b in reversed(range(bits_of(nf))):
        half = value.shape[0] // 2
        got = swap(value[half:], "fsdp", 1 << b, nf)
        total = value[:half].astype(jnp.float32) + got.astype(jnp.float32)
        value = total.astype(jnp.bfloat16)
    return value.astype(jnp.float32) if total is None else total


def sum_fsdp(value, env, anchor=None):
    nf = env[1]
    for b in range(bits_of(nf)):
        got = swap(value.astype(jnp.bfloat16), "fsdp", 1 << b, nf)
        if anchor is not None:
            got = after(got, anchor)
        value = value + got.astype(jnp.float32)
    return value


def side_by_side(own, got, mine):
    first = mine == 0
    return jnp.concatenate([jnp.where(first, own, got), jnp.where(first, got, own)], axis=1)


def stages_of(order, env):
    kinds = {
        "y": [("fsdp", b) for b in range(bits_of(env[1]))],
        "x": [("dp", 1)],
        "z": [("dp", 2)] if bits_of(env[0]) > 2 else [],
    }
    return [stage for letter in order for stage in kinds[letter]]


def add_low(terms):
    total = terms[0].astype(jnp.float32)
    for term in terms[1:]:
        total = total + term.astype(jnp.float32)
    return total.astype(jnp.bfloat16)


class Flow:
    most = 5

    def __init__(self, env):
        self.env, self.pending, self.flying = env, [], []
        self.mark = jnp.zeros((8, 128), jnp.float32)

    def send(self, operand, axis, mask, land, rank, windows=1):
        self.pending.append((operand, axis, mask, land, rank, windows))

    def turn(self, outs, ins):
        nd, nf = self.env[:2]
        landing = [(got, land) for got, land, left in self.flying if left == 1]
        self.flying = [(got, land, left - 1) for got, land, left in self.flying if left > 1]
        if landing:
            gots = tuple(got for got, _ in landing)
            tied = lax.optimization_barrier(gots + tuple(outs) + (self.mark,))
            self.mark = tied[-1]
            for got, (_, land) in zip(tied, landing):
                land(got)
        pending = sorted(self.pending, key=lambda p: p[4])
        pending, self.pending = pending[: self.most - len(self.flying)], pending[self.most - len(self.flying) :]
        sends = tuple(p[0] for p in pending)
        tied = lax.optimization_barrier(sends + tuple(ins) + tuple(outs) + (self.mark,))
        self.mark = tied[-1]
        for operand, (_, axis, mask, land, _, windows) in zip(tied, pending):
            size = nd if axis == "dp" else nf
            self.flying.append((swap(operand, axis, mask, size), land, windows))
        return tied[len(sends) : len(sends) + len(ins)]

    def drain(self, outs):
        while self.flying or self.pending:
            self.turn(outs, ())
            outs = ()


class Ladder:
    def __init__(self, current, alive, stages, env):
        self.current, self.alive, self.stages, self.env = current, alive, stages, env
        self.sent = None

    def split(self, axis, b):
        t = self.current
        if axis == "fsdp":
            pairs = t.reshape((t.shape[0] // 2, 2) + t.shape[1:])
            return pairs[:, 0], pairs[:, 1]
        place = 1 + self.alive.index(b)
        bit = (self.env[2] >> b) & 1
        self.alive = [d for d in self.alive if d != b]
        before, after_dims = t.shape[:place], t.shape[place + 1 :]
        rows = 1
        for n in after_dims[:-1]:
            rows *= n
        count = 1
        for n in before:
            count *= n
        flat = t.reshape(count, 2, rows, t.shape[-1])
        pick = lambda i: lax.dynamic_index_in_dim(flat, i, 1, keepdims=False).reshape(
            before + after_dims
        )
        return pick(bit), pick(bit ^ 1)

    def launch(self, flow, landed, rank, windows=1):
        axis, b = self.stages.pop(0)
        if self.sent is None:
            kept, send = self.split(axis, b)
        else:
            kept, send, self.sent = self.current, self.sent, None

        def land(got):
            self.current = add_low([kept, got.reshape(kept.shape)])
            landed()

        flow.send(send, axis, 1 << b, land, rank, windows)


def join_rows(kept, got, env):
    core = env[2] & 1
    both = jnp.where(
        core == 0,
        jnp.concatenate([kept, got], axis=1),
        jnp.concatenate([got, kept], axis=1),
    )
    return both.T.astype(jnp.float32)


def core_product(dact, act, core, env, rows_only, received=None, widths=None):
    nd, nf, me, mine = env
    count = 1 if rows_only else nf
    lanes = act.shape[1] // (2 * count)
    blocks = [core] if rows_only else [2 * (mine ^ r) + core for r in range(nf)]
    if lanes % 128 == 0:
        outs = product(dact, act, blocks, lanes, received, widths)
        return outs if widths else outs[0]
    wide = jnp.concatenate(list(dact), axis=1)
    parts = [lax.dynamic_slice_in_dim(act, b * lanes, lanes, 1) for b in blocks]
    out = jnp.stack([dot(wide, p, TN) for p in parts])
    if received is not None:
        out = out + received.astype(jnp.float32)
    out = out.astype(jnp.bfloat16)
    if widths is None:
        return out
    cuts = [sum(widths[:i]) for i in range(len(widths))]
    return [out[:, :, a : a + w] for a, w in zip(cuts, widths)]


class Reduction:
    def __init__(self, dact, act, portions, flow, rank, rows_only=False, last_windows=1):
        self.windows, self.last_windows = 1, last_windows
        self.flow, self.env, self.act, self.rank = flow, flow.env, act, rank
        self.portions, self.rows_only = portions, rows_only
        core = self.env[2] & 1
        self.partial = core_product(dact, act, core ^ 1, self.env, rows_only)
        flow.send(self.partial, "dp", 1, self.receive, 0)

    def receive(self, got):
        self.sent = got

    def keep(self, dact):
        nd, nf, me, mine = self.env
        core, bits = me & 1, bits_of(nd)
        alive = list(range(bits - 1, 0, -1))
        tail = (2, self.sent.shape[1] // nd)
        self.ladders = []
        if special(self.env):
            count = 1 if self.rows_only else nf
            blocks = [core] if self.rows_only else [2 * (mine ^ r) + core for r in range(nf)]
            pairs = split_product(
                dact, self.act, blocks, self.act.shape[1] // (2 * count), self.sent,
                [(w, order[0]) for w, order in self.portions], [(me >> 1) & 1, (me >> 2) & 1], nd,
            )
            for (kept, sent), (_, order) in zip(pairs, self.portions):
                stages = stages_of(order, self.env)
                axis, b = stages[0]
                left = [d for d in alive if axis != "dp" or d != b]
                lead = 1 if axis == "fsdp" else count
                shape = (lead,) + (2,) * len(left) + tail + (kept.shape[-1],)
                ladder = Ladder(kept.reshape(shape), left, stages, self.env)
                ladder.sent = sent
                self.ladders.append(ladder)
            first = pairs[0][0]
        else:
            widths = [w for w, _ in self.portions]
            totals = core_product(dact, self.act, core, self.env, self.rows_only, self.sent, widths)
            for total, (_, order) in zip(totals, self.portions):
                shape = (total.shape[0],) + (2,) * (bits - 1) + tail + (total.shape[2],)
                stages = stages_of(order, self.env)
                self.ladders.append(Ladder(total.reshape(shape), alive, stages, self.env))
            first = totals[0]
        self.launch()
        return first

    def launch(self):
        ladders = self.ladders
        if ladders[0].stages:
            self.waiting = len(ladders)
            for ladder in ladders:
                ladder.launch(self.flow, self.landed, self.rank, self.windows)
            return
        if len(ladders) > 1:
            joined = jnp.concatenate([r.current for r in ladders], axis=-1)
            self.ladders = ladders = [Ladder(joined, ladders[0].alive, [], self.env)]
        if ladders[0].alive:
            ladders[0].stages = [("dp", ladders[0].alive[-1])]
            self.windows = self.last_windows
            self.launch()
            return
        core = self.env[2] & 1
        rows = ladders[0].current[0]
        kept = lax.dynamic_index_in_dim(rows, core, 0, keepdims=False)

        def land(got):
            self.result = join_rows(kept, got, self.env)

        sent = lax.dynamic_index_in_dim(rows, core ^ 1, 0, keepdims=False)
        self.flow.send(sent, "dp", 1, land, 3)

    def landed(self):
        self.waiting -= 1
        if not self.waiting:
            self.launch()


class WideSum:
    def __init__(self, value, groups, flow, rank):
        self.value, self.flow, self.rank, self.groups = value, flow, rank, list(groups)
        self.passed = []
        self.launch()

    def launch(self):
        self.passed.append(self.value)
        if self.groups:
            axis, masks = self.groups.pop(0)
            self.waiting, self.total = len(masks), self.value.astype(jnp.float32)
            for mask in masks:
                self.flow.send(self.value, axis, mask, self.land, self.rank)

    def land(self, got):
        self.total = self.total + got.astype(jnp.float32)
        self.waiting -= 1
        if not self.waiting:
            self.value = self.total.astype(got.dtype)
            self.launch()


def hops(axis, size):
    return [(axis, [1 << b]) for b in range(bits_of(size))]


def portion_list(lanes, names):
    units = lanes // 128
    if lanes % 128 or units < len(names):
        return [(lanes, names[-1])]
    cuts = [units * i // len(names) * 128 for i in range(len(names) + 1)]
    return [(b - a, n) for a, b, n in zip(cuts, cuts[1:], names)]


def per_device(
    tokens,
    caption,
    modulation,
    caption_mask,
    positions,
    w_qkv,
    w_out,
    w_caption_kv,
    w_gate_up,
    w_down,
    norm_gains,
    caption_gain,
    cross_gate,
    cotangent,
):
    nd, nf = lax.axis_size("dp"), lax.axis_size("fsdp")
    me, mine = lax.axis_index("dp"), lax.axis_index("fsdp")
    env = (nd, nf, me, mine)
    own_rows = tokens.shape[1]
    heads = cross_gate.shape[0]
    which = (mine if special(env) else jnp.int32(0)).astype(jnp.int32)[None]
    pack = jnp.concatenate(
        [
            norm_gains,
            modulation[0],
            caption_gain[None],
            jnp.pad(cross_gate, (0, caption_gain.shape[0] - heads))[None],
        ]
    )
    flow = Flow(env)
    if special(env):
        landed = {}
        keep_as = lambda name: functools.partial(landed.__setitem__, name)
        half = w_qkv.shape[0] // 2
        gathers = [Pieces(w_qkv, 0, half, (1, 2, 0), flow), Pieces(w_qkv, half, half, (2, 1, 0), flow)]
        flow.send(pack, "fsdp", 1, keep_as("pack"), 0)
        flow.send(positions[0].T, "fsdp", 1, keep_as("places"), 0)
        flow.turn((), ())
        flow.send(slice_for(w_gate_up, env), "fsdp", 1, keep_as("gate_up"), 0)
        (caption_in,) = flow.turn((), (caption[0],))
        pack = side_by_side(pack, landed["pack"], mine)
        places = jnp.concatenate([positions[0].T, landed["places"]])
        partial_kv = dot(caption_in, w_caption_kv)
        flow.send(tokens[0], "fsdp", 1, keep_as("tokens"), 0)
        (places,) = flow.turn((partial_kv,), (places,))
        full_gate_up = gather_half(w_gate_up, landed["gate_up"], env)
        cosine, sine = rope_tables(places)
        flow.turn((cosine, sine), ())
        flow.turn((), ())
        tokens_other = landed["tokens"]
        flow.send(partial_kv.astype(jnp.bfloat16), "fsdp", 1, keep_as("caption"), 0)
        flow.send(slice_for(w_out, env), "fsdp", 1, keep_as("out"), 0)
        pieces = [p for g in gathers for p in g.pieces]
        starts = [mine * w_qkv.shape[0]] + [s for g in gathers for s in g.starts]
        gath_qkv = (w_qkv, pieces, starts)
        (tokens_other,) = flow.turn((), (tokens_other,))
    else:
        pack = lax.all_gather(pack, "fsdp", axis=1, tiled=True)
        cosine, sine = rope_tables(gather_relative(positions[0].T, env))
        full = lax.all_gather(w_qkv, "fsdp", axis=0, tiled=True)
        half = full.shape[0] // 2
        gath_qkv = (full[:half], [full[half:][None]], [jnp.int32(0), jnp.int32(half)])
        tokens_other = gather_relative(tokens[0], env)[own_rows:]
        partial_kv = dot(caption[0], w_caption_kv)
        full_gate_up = gather_half(w_gate_up, None, env)
    pack = pack.astype(jnp.float32)
    gains, mods, cap_gain = pack[:6], pack[6:12], pack[12]
    gate_heads = jnp.tanh(pack[13].reshape(nf, -1)[:, :heads].reshape(HEADS))
    gate_tanh = jnp.repeat(gate_heads, HEAD_DIM)[None]
    bias = jnp.where(caption_mask[0] > 0, 0.0, -1e30).astype(jnp.float32)
    hm, full_qkv, query_b, key_b, value_b, query_pre, key_pre = project(
        tokens[0], tokens_other, gains, mods, cosine, sine, gath_qkv
    )
    if special(env):
        (query_b,) = flow.turn((hm,), (query_b,))
        cap_rows = partial_kv + landed["caption"].astype(jnp.float32)
        full_out = gather_half(w_out, after(landed["out"], full_gate_up[1]), env)
        flow.send(slice_for(w_down, env), "fsdp", 1, keep_as("down"), 0)
        (query_b,) = flow.turn((), (query_b,))
    else:
        cap_rows = sum_fsdp(partial_kv, env)
        full_out = gather_half(w_out, None, env)
    ckey_pre = cap_rows[:, :D]
    ckey_scale = rms_scale(ckey_pre)
    ckey_b = (ckey_pre * ckey_scale * cap_gain).astype(jnp.bfloat16)
    cvalue_b = cap_rows[:, D:].astype(jnp.bfloat16)
    combined, self_out, cross_out, stats = attend(
        query_b, key_b, value_b, ckey_b, cvalue_b, bias[None], gate_tanh
    )
    if special(env):
        (combined,) = flow.turn((stats,), (combined,))
        full_down = gather_half(w_down, landed["down"], env)
    else:
        full_down = gather_half(w_down, None, env)
    projected, middle, ffn_in = output_step(which, combined, full_out, tokens[0], gains, mods)
    gate_part, up_part, ffn_inner = gate_up_step(which, ffn_in, full_gate_up)
    block_out, grad_down, down_sums = down_step(
        which, ffn_inner, full_down, middle, cotangent[0], gains, mods
    )
    lanes_d, lanes_f = D // (2 * nf), FF // (2 * nf)
    red_down = Reduction(grad_down[None], ffn_inner, portion_list(lanes_f, ORDERS), flow, 1)
    (grad_down_b,) = flow.turn((red_down.partial,), (grad_down,))
    dgu = gate_up_back(which, grad_down_b, gate_part, up_part, full_down)
    (grad_down_b,) = flow.turn((dgu,), (grad_down_b,))
    done = red_down.keep(grad_down_b[None])
    (dgu,) = flow.turn((done,), (dgu,))
    red_gate_up = Reduction(dgu, ffn_in, portion_list(lanes_d, ORDERS), flow, 1)
    (dgu_b,) = flow.turn((red_gate_up.partial,), (dgu,))
    grad_mid, grad_proj, grad_comb, ffn_sums = ffn_back(
        which, dgu_b, full_gate_up, full_out, middle, cotangent[0], projected, gains, mods
    )
    grad_comb, grad_proj = flow.turn((ffn_sums,), (grad_comb, grad_proj))
    dq_cross, grad_ckey, grad_cvalue, gate_sums = cross_back(
        query_b, ckey_b, cvalue_b, bias[:, None], gate_tanh, stats, grad_comb, cross_out
    )
    gate_terms = gate_sums[0].reshape(HEADS, HEAD_DIM).sum(axis=-1) * (1.0 - gate_heads**2)
    grad_ckey_pre, cap_gain_terms = norm_back(
        grad_ckey.astype(jnp.float32), ckey_pre, ckey_scale, cap_gain
    )
    grad_cap_kv = jnp.concatenate([grad_ckey_pre, grad_cvalue.astype(jnp.float32)], axis=-1)
    cap_sum = WideSum(grad_cap_kv.astype(jnp.bfloat16), hops("fsdp", nf), flow, 0)
    red_out = Reduction(grad_proj[None], combined, portion_list(lanes_d, ORDERS[2:]), flow, 1.5)
    dgu_b, grad_comb = flow.turn((gate_sums, red_out.partial), (dgu_b, grad_comb))
    done = red_gate_up.keep(dgu_b)
    pairs = D // PAIR
    each = pairs // 4
    parts = []

    def attention_part(grads):
        parts.append(
            self_back(query_b, key_b, value_b, stats, grads, self_out, dq_cross, len(parts) * each, each)
        )
        return parts[-1][0]

    first = attention_part(grad_comb)
    while nf > 2 and cap_sum.groups:
        flow.turn((done,), ())
    grad_comb, grad_proj = flow.turn((done, first), (grad_comb, grad_proj))
    grad_cap_kv = cap_sum.value
    red_caption = Reduction(
        grad_cap_kv[None], caption[0], portion_list(caption.shape[2] // 2, ["xz", "zx"]), flow, 1.2, True, 1
    )
    out_done = red_out.keep(grad_proj[None])
    dones = [attention_part(grad_comb) for _ in range(3)]
    grad_query, grad_key, grad_value = zip(*parts)
    (dq0,) = flow.turn([red_caption.partial, out_done] + dones, (grad_query[0],))
    grad_query = (dq0,) + grad_query[1:]
    grad_mixed, qk_sums = qk_back(
        grad_query, grad_key, grad_value, query_pre, key_pre, cosine, sine, gains
    )
    red_qkv = Reduction(grad_mixed[None], hm, portion_list(lanes_d, ORDERS), flow, 0.5)
    grad_mixed, grad_cap_kv = flow.turn((red_qkv.partial,), (grad_mixed, grad_cap_kv))
    done = red_caption.keep(grad_cap_kv[None])
    dx_other, other_sums = project_back(
        grad_mixed, own_rows, own_rows, tokens_other, full_qkv, gains, mods
    )
    dx_got = []
    if nf == 2:
        flow.send(dx_other, "fsdp", 1, dx_got.append, 0)
    (grad_mixed,) = flow.turn((done, other_sums), (grad_mixed,))
    done = red_qkv.keep(grad_mixed[None])
    dx_own, own_sums = project_back(grad_mixed, 0, own_rows, tokens[0], full_qkv, gains, mods)
    project_sums = own_sums + other_sums if nf > 1 else own_sums
    small = jnp.concatenate(
        [
            project_sums[:1],
            qk_sums[1:3],
            jnp.stack(
                [
                    ffn_sums[4],
                    ffn_sums[2],
                    down_sums[1],
                    jnp.sum(cap_gain_terms, axis=0),
                    jnp.pad(gate_terms, (0, D - HEADS)),
                ]
            ),
        ]
    )
    mod_grads = jnp.stack(
        [
            project_sums[3],
            project_sums[4],
            ffn_sums[3] * (1.0 - jnp.tanh(mods[2]) ** 2),
            ffn_sums[0],
            ffn_sums[1],
            down_sums[0] * (1.0 - jnp.tanh(mods[5]) ** 2),
        ]
    )
    along = hops("dp", nd)
    if special(env):
        along = along[2:] + [("dp", [1, 2, 3])]
    small = jnp.concatenate([small, mod_grads, jnp.zeros((2, D), jnp.float32)])
    small_sum = WideSum(small, hops("fsdp", nf) + along, flow, 1.3)
    (grad_cap_kv,) = flow.turn((done, own_sums), (grad_cap_kv,))
    if nf == 2:
        dx = dx_own.astype(jnp.float32) + dx_got[0].astype(jnp.float32)
    else:
        dx = reduce_relative(jnp.concatenate([dx_own, dx_other]) if nf > 1 else dx_own, env)
    grad_tokens = (grad_mid + dx).astype(jnp.bfloat16)
    grad_caption = dot(grad_cap_kv, w_caption_kv, NT).astype(jnp.bfloat16)
    flow.drain((grad_caption, grad_tokens))
    small, mod_grads = small_sum.value, small_sum.passed[bits_of(nf)][8:14]
    out_down, out_gate_up, out_out, out_caption, out_qkv = (
        r.result for r in (red_down, red_gate_up, red_out, red_caption, red_qkv)
    )
    width = D // nf
    return (
        block_out[None],
        grad_tokens[None],
        grad_caption[None],
        lax.dynamic_slice_in_dim(mod_grads, mine * width, width, 1)[None],
        out_qkv,
        out_out,
        out_caption,
        out_gate_up,
        out_down,
        lax.dynamic_slice_in_dim(small[:6], mine * width, width, 1),
        lax.dynamic_slice_in_dim(small[6], mine * width, width, 0),
        lax.dynamic_slice_in_dim(small[7], mine * heads, heads, 0),
    )


def solution(mesh):
    placed = (
        P("dp", "fsdp", None),
        P("dp", None, "fsdp"),
        P("dp", None, "fsdp"),
        P("dp", None),
        P("dp", None, "fsdp"),
        P("fsdp", None),
        P("fsdp", None),
        P("fsdp", None),
        P("fsdp", None),
        P("fsdp", None),
        P(None, "fsdp"),
        P("fsdp"),
        P("fsdp"),
        P("dp", "fsdp", None),
    )
    return jax.shard_map(
        per_device,
        mesh=mesh,
        in_specs=placed,
        out_specs=(
            P("dp", "fsdp", None),
            P("dp", "fsdp", None),
            P("dp", None, "fsdp"),
            P("dp", None, "fsdp"),
            P("fsdp", "dp"),
            P("fsdp", "dp"),
            P("fsdp", "dp"),
            P("fsdp", "dp"),
            P("fsdp", "dp"),
            P(None, "fsdp"),
            P("fsdp"),
            P("fsdp"),
        ),
        check_vma=False,
    )
```

```python
import functools

import jax
import jax.numpy as jnp
from jax import lax
from jax.experimental import pallas as pl
from jax.experimental.pallas import tpu as pltpu
from jax.sharding import PartitionSpec as P

D = 1536
HEADS = 24
HEAD_DIM = 64
FF = 4096
EPS = 1e-05


def rms_scale(values):
    return lax.rsqrt(jnp.mean(values * values, axis=-1, keepdims=True) + EPS)


def norm_back(grad_normed, values, inv_rms, gain_row):
    scaled_grad = grad_normed * gain_row
    grad_values = inv_rms * scaled_grad - values * inv_rms**3 * jnp.mean(
        scaled_grad * values, axis=-1, keepdims=True
    )
    return (grad_values, grad_normed * values * inv_rms)


def rope_tables(positions):
    lane = jnp.arange(PAIR)
    frequency = 10000.0 ** (-(lane % 16).astype(jnp.float32) / 16)
    places = positions.astype(jnp.float32)
    angles = jnp.where((lane % 64 < 32)[None], places[:, :1], places[:, 1:]) * frequency
    sign = jnp.where(lane % 32 < 16, -1.0, 1.0).astype(jnp.float32)
    return jnp.cos(angles), jnp.sin(angles) * sign


PAIR = 2 * HEAD_DIM
NT = (((1,), (1,)), ((), ()))
TN = (((0,), (0,)), ((), ()))


def head_masks(dtype):
    lane = lax.broadcasted_iota(jnp.int32, (1, PAIR), 1)
    return [(lane < HEAD_DIM).astype(dtype), (lane >= HEAD_DIM).astype(dtype)]


def attend_kernel(q_ref, k_ref, v_ref, ck_ref, cv_ref, bias_ref, gate_ref, a_ref, o_ref, oy_ref, stat_ref):
    masks = head_masks(jnp.float32)
    rows = q_ref.shape[0]
    step = min(rows, 512)
    gate = gate_ref[...]
    for start in range(0, rows, step):
        where = pl.ds(start, step)
        q = q_ref[where, :].astype(jnp.float32) * HEAD_DIM**-0.5
        own, cross, stats = [], [], []
        for mask in masks:
            qm = (q * mask).astype(jnp.bfloat16)
            for keys, values, bias, outs in (
                (k_ref, v_ref, None, own),
                (ck_ref, cv_ref, bias_ref, cross),
            ):
                s = lax.dot_general(qm, keys[...], NT, preferred_element_type=jnp.float32)
                if bias is not None:
                    s = s + bias[...]
                top = jnp.max(s, axis=1, keepdims=True)
                e = jnp.exp(s - top)
                total = jnp.sum(e, axis=1, keepdims=True)
                out = jnp.dot(e.astype(jnp.bfloat16), values[...], preferred_element_type=jnp.float32)
                outs.append(out / total * mask)
                stats.append(top + jnp.log(total))
        o = own[0] + own[1]
        oy = cross[0] + cross[1]
        a_ref[where, :] = (o + gate * oy).astype(jnp.bfloat16)
        o_ref[where, :] = o.astype(jnp.bfloat16)
        oy_ref[where, :] = oy.astype(jnp.bfloat16)
        lane = lax.broadcasted_iota(jnp.int32, (step, PAIR), 1)
        tile = jnp.where(lane == 0, stats[0], jnp.where(lane == 1, stats[1], jnp.where(lane == 2, stats[2], stats[3])))
        stat_ref[0, :, where] = tile.T[:8, :]


def attend(query, key, value, ckey, cvalue, bias_row, gate_lanes):
    rows, keys, slots = query.shape[0], key.shape[0], ckey.shape[0]
    pairs = D // PAIR
    spec = lambda n: pl.BlockSpec((n, PAIR), lambda j: (0, j))
    return pl.pallas_call(
        attend_kernel,
        grid=(pairs,),
        in_specs=[
            spec(rows), spec(keys), spec(keys), spec(slots), spec(slots),
            pl.BlockSpec((1, slots), lambda j: (0, 0)), spec(1),
        ],
        out_specs=[spec(rows)] * 3 + [pl.BlockSpec((1, 8, rows), lambda j: (j, 0, 0))],
        out_shape=[jax.ShapeDtypeStruct((rows, D), jnp.bfloat16)] * 3
        + [jax.ShapeDtypeStruct((pairs, 8, rows), jnp.float32)],
        compiler_params=pltpu.CompilerParams(vmem_limit_bytes=48 * 2**20),
        cost_estimate=cost(16 * rows * (keys + slots) * D, 20e6, HEADS * rows * (keys + slots)),
    )(query, key, value, ckey, cvalue, bias_row, gate_lanes)


def back_part(k_tile, v_tile, bias, qm, grads, deltas, lses):
    masks = head_masks(jnp.bfloat16)
    dk = dv = add = None
    for h in range(2):
        st = dot(k_tile, qm[h], NT)
        if bias is not None:
            st = st + bias
        pt = jnp.exp(st - lses[h])
        dpt = dot(v_tile, grads[h], NT)
        dst = (pt * (dpt - deltas[h])).astype(jnp.bfloat16)
        terms = (
            dot(dst, qm[h]),
            dot(pt.astype(jnp.bfloat16), grads[h]),
            dot(dst, k_tile * masks[h], TN),
        )
        dk, dv, add = terms if h == 0 else (dk + terms[0], dv + terms[1], add + terms[2])
    return dk, dv, add


def head_sums(terms):
    t = terms.T
    return [
        jnp.sum(t[:HEAD_DIM], axis=0, keepdims=True),
        jnp.sum(t[HEAD_DIM:], axis=0, keepdims=True),
    ]


def split_heads(values):
    return [(values * m).astype(jnp.bfloat16) for m in head_masks(jnp.float32)]


def cross_back_kernel(q_ref, ck_ref, cv_ref, bias_ref, gate_ref, stat_ref, da_ref, oy_ref, dq_ref, dck_ref, dcv_ref, gsum_ref):
    qm = split_heads(q_ref[...].astype(jnp.float32) * HEAD_DIM**-0.5)
    da = da_ref[...].astype(jnp.float32)
    doy = (da * gate_ref[...]).astype(jnp.bfloat16).astype(jnp.float32)
    oy = oy_ref[...].astype(jnp.float32)
    gsum_ref[...] = jnp.sum(da * oy, axis=0, keepdims=True)
    stat = stat_ref[0]
    dk, dv, dq = back_part(
        ck_ref[...], cv_ref[...], bias_ref[...], qm, split_heads(doy), head_sums(doy * oy), [stat[1:2], stat[3:4]]
    )
    dck_ref[...] = dk.astype(dck_ref.dtype)
    dcv_ref[...] = dv.astype(dcv_ref.dtype)
    dq_ref[...] = (dq * HEAD_DIM**-0.5).astype(dq_ref.dtype)


def self_back_kernel(q_ref, k_ref, v_ref, stat_ref, da_ref, o_ref, dqc_ref, dq_ref, dk_ref, dv_ref):
    keys = k_ref.shape[0]
    step = min(keys, 256)
    qm = split_heads(q_ref[...].astype(jnp.float32) * HEAD_DIM**-0.5)
    da = da_ref[...].astype(jnp.float32)
    deltas = head_sums(da * o_ref[...].astype(jnp.float32))
    dam = split_heads(da)
    stat = stat_ref[0]
    dq = None
    for start in range(0, keys, step):
        where = pl.ds(start, step)
        dk, dv, add = back_part(k_ref[where, :], v_ref[where, :], None, qm, dam, deltas, [stat[0:1], stat[2:3]])
        dk_ref[where, :] = dk.astype(dk_ref.dtype)
        dv_ref[where, :] = dv.astype(dv_ref.dtype)
        dq = add if dq is None else dq + add
    dq = dq * HEAD_DIM**-0.5 + dqc_ref[...].astype(jnp.float32)
    dq_ref[...] = dq.astype(dq_ref.dtype)


def cross_back(query, ckey, cvalue, bias_col, gate_lanes, stats, grad_a, o_cross):
    rows, slots = query.shape[0], ckey.shape[0]
    pairs = D // PAIR
    spec = lambda n: pl.BlockSpec((n, PAIR), lambda j: (0, j))
    return pl.pallas_call(
        cross_back_kernel,
        grid=(pairs,),
        in_specs=[
            spec(rows), spec(slots), spec(slots),
            pl.BlockSpec((slots, 1), lambda j: (0, 0)), spec(1),
            pl.BlockSpec((1, 8, rows), lambda j: (j, 0, 0)),
            spec(rows), spec(rows),
        ],
        out_specs=[spec(rows), spec(slots), spec(slots), spec(1)],
        out_shape=[jax.ShapeDtypeStruct((n, D), jnp.bfloat16) for n in (rows, slots, slots)]
        + [jax.ShapeDtypeStruct((1, D), jnp.float32)],
        compiler_params=params(48),
        cost_estimate=cost(40 * rows * slots * D, 9e6, HEADS * rows * slots),
    )(query, ckey, cvalue, bias_col, gate_lanes, stats, grad_a, o_cross)


def self_back(query, key, value, stats, grad_a, o_self, dq_cross, first, count):
    rows, keys = query.shape[0], key.shape[0]
    spec = lambda n: pl.BlockSpec((n, PAIR), lambda j: (0, j + first))
    out = lambda n: pl.BlockSpec((n, PAIR), lambda j: (0, j))
    return pl.pallas_call(
        self_back_kernel,
        grid=(count,),
        in_specs=[
            spec(rows), spec(keys), spec(keys),
            pl.BlockSpec((1, 8, rows), lambda j: (j + first, 0, 0)),
            spec(rows), spec(rows), spec(rows),
        ],
        out_specs=[out(rows), out(keys), out(keys)],
        out_shape=[jax.ShapeDtypeStruct((n, count * PAIR), jnp.bfloat16) for n in (rows, keys, keys)],
        compiler_params=params(48),
        cost_estimate=cost(80 * rows * keys * count * PAIR, 1e6 * count, 2 * count * rows * keys),
    )(query, key, value, stats, grad_a, o_self, dq_cross)


NN = (((1,), (0,)), ((), ()))


def dot(a, b, dims=NN):
    return lax.dot_general(a, b, dims, preferred_element_type=jnp.float32)


def chunks(rows, step, body):
    def one(i, carry):
        body(pl.ds(pl.multiple_of(i * step, step), step))
        return carry

    lax.fori_loop(0, rows // step, one, 0)


def add_row(ref, index, terms):
    ref[index : index + 1, :] += jnp.sum(terms, axis=0, keepdims=True)


def partner(values):
    lane = lax.broadcasted_iota(jnp.int32, (values.shape[0], PAIR), 1)
    low = (lane & 31) < 16
    outs = []
    for start in range(0, values.shape[1], PAIR):
        tile = values[:, start : start + PAIR]
        outs.append(jnp.where(low, pltpu.roll(tile, PAIR - 16, 1), pltpu.roll(tile, 16, 1)))
    return jnp.concatenate(outs, axis=1)


def turn(values, cosine, sine):
    count = values.shape[1] // PAIR
    wide = lambda t: jnp.concatenate([t] * count, axis=1)
    return values * wide(cosine) + partner(values) * wide(sine)


def halves(values, which):
    mid = values.shape[1] // 2
    low, high = values[:, :mid], values[:, mid:]
    first = which == 0
    return jnp.where(first, low, high), jnp.where(first, high, low)


def small_spec(shape):
    return pl.BlockSpec(shape, lambda *_: (0,) * len(shape))


def params(mib=56):
    return pltpu.CompilerParams(vmem_limit_bytes=mib * 2**20)


def cost(flops, nbytes, trans=0):
    share = 0.05
    return pl.CostEstimate(
        flops=int(flops * share), bytes_accessed=int(nbytes * share), transcendentals=int(trans * share)
    )


def project_kernel(parts, own_rows, where_ref, tok_ref, other_ref, gain_ref, mod_ref, cos_ref, sin_ref, own_ref, *refs):
    pieces = refs[:parts]
    hm_ref, full_ref, q_ref, k_ref, v_ref, qpre_ref, kpre_ref, pre_ref = refs[parts:]
    pid = pl.program_id(0)
    rows = own_rows + other_ref.shape[0]
    step = min(128, own_rows)
    tile = full_ref.shape[1]
    per = D // tile

    @pl.when(pid == 0)
    def hidden():
        for source, first in ((tok_ref, 0), (other_ref, own_rows)):

            def body(i, carry, source=source, first=first):
                x = source[pl.ds(pl.multiple_of(i * step, step), step), :].astype(jnp.float32)
                hid = x * rms_scale(x) * gain_ref[0:1]
                hid = (hid * (1.0 + mod_ref[1:2]) + mod_ref[0:1]).astype(jnp.bfloat16)
                hm_ref[pl.ds(pl.multiple_of(first + i * step, step), step), :] = hid
                return carry

            lax.fori_loop(0, source.shape[0] // step, body, 0)

    n = own_ref.shape[0]
    full_ref[pl.ds(pl.multiple_of(where_ref[0], n), n), :] = own_ref[...]
    i = 1
    for piece in pieces:
        n = piece.shape[1]
        for k in range(piece.shape[0]):
            full_ref[pl.ds(pl.multiple_of(where_ref[i], n), n), :] = piece[k]
            i += 1

    for j in range(2 * per):
        count = own_rows if j < per else rows

        @pl.when(pid == j)
        def pre(j=j, count=count):
            pre_ref[:count, (j % per) * tile : (j % per + 1) * tile] = dot(
                hm_ref[:count, :], full_ref[...]
            )

    @pl.when(pid >= 2 * per)
    def value():
        v_ref[...] = dot(hm_ref[...], full_ref[...]).astype(jnp.bfloat16)

    for last, count, out, keep, gain in (
        (per - 1, own_rows, q_ref, qpre_ref, 1),
        (2 * per - 1, rows, k_ref, kpre_ref, 2),
    ):

        @pl.when(pid == last)
        def finish(count=count, out=out, keep=keep, gain=gain):
            def body(where):
                p = pre_ref[where, :]
                n = p * rms_scale(p) * gain_ref[gain : gain + 1]
                out[where, :] = turn(n, cos_ref[where, :], sin_ref[where, :]).astype(jnp.bfloat16)
                keep[where, :] = p.astype(jnp.bfloat16)

            chunks(count, min(step, count), body)


def project(tokens, others, gains, mods, cosine, sine, weight, tile=512):
    own, pieces, starts = weight
    own_rows = tokens.shape[0]
    rows = own_rows + others.shape[0]
    n = 3 * D // tile
    vtile = 2 * D // tile
    outs = [
        ((rows, D), jnp.bfloat16, None),
        ((D, 3 * D), jnp.bfloat16, pl.BlockSpec((D, tile), lambda j, w: (0, j))),
        ((own_rows, D), jnp.bfloat16, None),
        ((rows, D), jnp.bfloat16, None),
        ((rows, D), jnp.bfloat16, pl.BlockSpec((rows, tile), lambda j, w: (0, jnp.maximum(j - vtile, 0)))),
        ((own_rows, D), jnp.bfloat16, None),
        ((rows, D), jnp.bfloat16, None),
    ]
    return pl.pallas_call(
        functools.partial(project_kernel, len(pieces), own_rows),
        grid_spec=pltpu.PrefetchScalarGridSpec(
            num_scalar_prefetch=1,
            grid=(n,),
            in_specs=[small_spec(a.shape) for a in (tokens, others, gains, mods, cosine, sine)]
            + [pl.BlockSpec((own.shape[0], tile), lambda j, w: (0, j))]
            + [pl.BlockSpec(p.shape[:2] + (tile,), lambda j, w: (0, 0, j)) for p in pieces],
            out_specs=[s if s is not None else small_spec(shape) for shape, _, s in outs],
            scratch_shapes=[pltpu.VMEM((rows, D), jnp.float32)],
        ),
        out_shape=[jax.ShapeDtypeStruct(shape, d) for shape, d, _ in outs],
        compiler_params=params(58),
        cost_estimate=cost(2 * D * D * (own_rows + 2 * rows), 60e6),
    )(jnp.stack(starts).astype(jnp.int32), tokens, others, gains, mods, cosine, sine, own, *pieces)


def output_kernel(which_ref, a_ref, w0_ref, w1_ref, x_ref, gain_ref, mod_ref, o_ref, mid_ref, hfm_ref):
    a0, a1 = halves(a_ref[...], which_ref[0])
    o = dot(a0, w0_ref[...]) + dot(a1, w1_ref[...])
    o_ref[...] = o.astype(jnp.bfloat16)
    on = o * rms_scale(o) * gain_ref[3:4]
    mid = x_ref[...].astype(jnp.float32) + jnp.tanh(mod_ref[2:3]) * on
    mid_ref[...] = mid
    hf = mid * rms_scale(mid) * gain_ref[4:5]
    hfm_ref[...] = (hf * (1.0 + mod_ref[4:5]) + mod_ref[3:4]).astype(jnp.bfloat16)


def output_step(which, combined, weight, tokens, gains, mods):
    rows = combined.shape[0]
    step = min(rows, 256)
    row_spec = pl.BlockSpec((step, D), lambda i, w: (i, 0))
    return pl.pallas_call(
        output_kernel,
        grid_spec=pltpu.PrefetchScalarGridSpec(
            num_scalar_prefetch=1,
            grid=(rows // step,),
            in_specs=[row_spec, small_spec(weight[0].shape), small_spec(weight[1].shape), row_spec]
            + [small_spec(gains.shape), small_spec(mods.shape)],
            out_specs=[row_spec] * 3,
        ),
        out_shape=[
            jax.ShapeDtypeStruct((rows, D), jnp.bfloat16),
            jax.ShapeDtypeStruct((rows, D), jnp.float32),
            jax.ShapeDtypeStruct((rows, D), jnp.bfloat16),
        ],
        compiler_params=params(),
        cost_estimate=cost(2 * rows * D * D, 15e6),
    )(which, combined, weight[0], weight[1], tokens, gains, mods)


def gate_up_kernel(which_ref, h_ref, g0_ref, g1_ref, u0_ref, u1_ref, ga_ref, up_ref, ff_ref, hs_ref):
    @pl.when(pl.program_id(0) == 0)
    def split():
        hs_ref[0], hs_ref[1] = halves(h_ref[...], which_ref[0])

    ga = dot(hs_ref[0], g0_ref[...]) + dot(hs_ref[1], g1_ref[...])
    up = dot(hs_ref[0], u0_ref[...]) + dot(hs_ref[1], u1_ref[...])
    ga_ref[...] = ga.astype(jnp.bfloat16)
    up_ref[...] = up.astype(jnp.bfloat16)
    ff_ref[...] = (ga / (1.0 + jnp.exp(-ga)) * up).astype(jnp.bfloat16)


def gate_up_step(which, hfm, weight, tile=512):
    rows = hfm.shape[0]
    n = FF // tile
    half = D // 2
    spec = lambda off: pl.BlockSpec((half, tile), lambda j, w: (0, j + off))
    out = pl.BlockSpec((rows, tile), lambda j, w: (0, j))
    return pl.pallas_call(
        gate_up_kernel,
        grid_spec=pltpu.PrefetchScalarGridSpec(
            num_scalar_prefetch=1,
            grid=(n,),
            in_specs=[small_spec(hfm.shape), spec(0), spec(0), spec(n), spec(n)],
            out_specs=[out] * 3,
            scratch_shapes=[pltpu.VMEM((2, rows, half), jnp.bfloat16)],
        ),
        out_shape=[jax.ShapeDtypeStruct((rows, FF), jnp.bfloat16)] * 3,
        compiler_params=params(),
        cost_estimate=cost(4 * rows * D * FF, 40e6, rows * FF),
    )(which, hfm, weight[0], weight[1], weight[0], weight[1])


def down_kernel(which_ref, ff_ref, w0_ref, w1_ref, mid_ref, cot_ref, gain_ref, mod_ref, out_ref, df_ref, sum_ref, f_ref, hs_ref):
    pid = pl.program_id(0)
    tile = w0_ref.shape[1]
    rows = ff_ref.shape[0]

    @pl.when(pid == 0)
    def split():
        hs_ref[0], hs_ref[1] = halves(ff_ref[...], which_ref[0])

    f_ref[pid] = dot(hs_ref[0], w0_ref[...]) + dot(hs_ref[1], w1_ref[...])

    @pl.when(pid == pl.num_programs(0) - 1)
    def finish():
        gate = jnp.tanh(mod_ref[5:6])
        sum_ref[...] = jnp.zeros_like(sum_ref)

        def body(where):
            f = jnp.concatenate([f_ref[j, where, :] for j in range(D // tile)], axis=1)
            rf = rms_scale(f)
            fn = f * rf * gain_ref[5:6]
            dy = cot_ref[where, :].astype(jnp.float32)
            out_ref[where, :] = (mid_ref[where, :] + gate * fn).astype(jnp.bfloat16)
            dfn = dy * gate
            add_row(sum_ref, 0, dy * fn)
            df, terms = norm_back(dfn, f, rf, gain_ref[5:6])
            add_row(sum_ref, 1, terms)
            df_ref[where, :] = df.astype(jnp.bfloat16)

        chunks(rows, min(64, rows), body)


def down_step(which, ffh, weight, middle, cotangent, gains, mods, tile=256):
    rows = ffh.shape[0]
    half = FF // 2
    spec = pl.BlockSpec((half, tile), lambda j, w: (0, j))
    full = small_spec((rows, D))
    return pl.pallas_call(
        down_kernel,
        grid_spec=pltpu.PrefetchScalarGridSpec(
            num_scalar_prefetch=1,
            grid=(D // tile,),
            in_specs=[small_spec(ffh.shape), spec, spec, full, full, small_spec(gains.shape), small_spec(mods.shape)],
            out_specs=[full, full, small_spec((8, D))],
            scratch_shapes=[
                pltpu.VMEM((D // tile, rows, tile), jnp.float32),
                pltpu.VMEM((2, rows, half), jnp.bfloat16),
            ],
        ),
        out_shape=[jax.ShapeDtypeStruct((rows, D), jnp.bfloat16)] * 2
        + [jax.ShapeDtypeStruct((8, D), jnp.float32)],
        compiler_params=params(),
        cost_estimate=cost(2 * rows * D * FF, 24e6),
    )(which, ffh, weight[0], weight[1], middle, cotangent, gains, mods)


def gate_up_back_kernel(which_ref, df_ref, ga_ref, up_ref, d0_ref, d1_ref, dgu_ref):
    pid = pl.program_id(0)
    n = pl.num_programs(0)

    def work(w_ref):
        dffh = dot(df_ref[...], w_ref[...], NT)
        ga = ga_ref[...].astype(jnp.float32)
        up = up_ref[...].astype(jnp.float32)
        s = 1.0 / (1.0 + jnp.exp(-ga))
        dgu_ref[0] = (dffh * up * (s * (1.0 + ga * (1.0 - s)))).astype(jnp.bfloat16)
        dgu_ref[1] = (dffh * (ga * s)).astype(jnp.bfloat16)

    @pl.when(pid < n // 2)
    def first():
        work(d0_ref)

    @pl.when(pid >= n // 2)
    def second():
        work(d1_ref)


def gate_up_back(which, df, ga, up, w_down, tile=512):
    rows = df.shape[0]
    n = FF // tile
    h = n // 2
    cols = pl.BlockSpec((rows, tile), lambda j, w: (0, (j + w[0] * h) % n))
    return pl.pallas_call(
        gate_up_back_kernel,
        grid_spec=pltpu.PrefetchScalarGridSpec(
            num_scalar_prefetch=1,
            grid=(n,),
            in_specs=[
                small_spec((rows, D)), cols, cols,
                pl.BlockSpec((tile, D), lambda j, w: (jnp.minimum(j, h - 1), 0)),
                pl.BlockSpec((tile, D), lambda j, w: (jnp.maximum(j - h, 0), 0)),
            ],
            out_specs=pl.BlockSpec((2, rows, tile), lambda j, w: (0, 0, (j + w[0] * h) % n)),
        ),
        out_shape=jax.ShapeDtypeStruct((2, rows, FF), jnp.bfloat16),
        compiler_params=params(),
        cost_estimate=cost(2 * rows * D * FF, 30e6, rows * FF),
    )(which, df, ga, up, w_down[0], w_down[1])


def ffn_back_kernel(
    which_ref, dgu_ref, g0_ref, g1_ref, u0_ref, u1_ref,
    mid_ref, cot_ref, o_ref, w0_ref, w1_ref, gain_ref, mod_ref,
    dmid_ref, do_ref, da_ref, sum_ref, acc_ref,
):
    pid = pl.program_id(0)
    n = pl.num_programs(0)
    rows = mid_ref.shape[0]
    which = which_ref[0]
    dga, dup = dgu_ref[0], dgu_ref[1]
    p0 = dot(dga, g0_ref[...], NT) + dot(dup, u0_ref[...], NT)
    p1 = dot(dga, g1_ref[...], NT) + dot(dup, u1_ref[...], NT)

    @pl.when(pid == 0)
    def clear():
        acc_ref[which] = p0
        acc_ref[1 - which] = p1

    @pl.when(pid > 0)
    def more():
        acc_ref[which] += p0
        acc_ref[1 - which] += p1

    @pl.when(pid == n - 1)
    def finish():
        sum_ref[...] = jnp.zeros_like(sum_ref)
        gate = jnp.tanh(mod_ref[2:3])

        def body(where):
            dhfm = jnp.concatenate([acc_ref[0, where, :], acc_ref[1, where, :]], axis=1)
            mid = mid_ref[where, :]
            r2 = rms_scale(mid)
            add_row(sum_ref, 0, dhfm)
            add_row(sum_ref, 1, dhfm * (mid * r2 * gain_ref[4:5]))
            dmid, terms = norm_back(dhfm * (1.0 + mod_ref[4:5]), mid, r2, gain_ref[4:5])
            add_row(sum_ref, 2, terms)
            dmid = cot_ref[where, :].astype(jnp.float32) + dmid
            dmid_ref[where, :] = dmid
            o = o_ref[where, :].astype(jnp.float32)
            ro = rms_scale(o)
            add_row(sum_ref, 3, dmid * (o * ro * gain_ref[3:4]))
            do, terms = norm_back(dmid * gate, o, ro, gain_ref[3:4])
            add_row(sum_ref, 4, terms)
            do_ref[where, :] = do.astype(jnp.bfloat16)

        chunks(rows, min(64, rows), body)
        do = do_ref[...]
        q0 = dot(do, w0_ref[...], NT).astype(jnp.bfloat16)
        q1 = dot(do, w1_ref[...], NT).astype(jnp.bfloat16)
        half = q0.shape[1]
        da_ref[:, :half] = jnp.where(which == 0, q0, q1)
        da_ref[:, half:] = jnp.where(which == 0, q1, q0)


def ffn_back(which, dgu, w_gate_up, w_out, middle, cotangent, o, gains, mods, tile=512):
    rows = middle.shape[0]
    n = FF // tile
    half = D // 2
    full = small_spec((rows, D))
    gspec = pl.BlockSpec((half, tile), lambda j, w: (0, j))
    uspec = pl.BlockSpec((half, tile), lambda j, w: (0, j + n))
    return pl.pallas_call(
        ffn_back_kernel,
        grid_spec=pltpu.PrefetchScalarGridSpec(
            num_scalar_prefetch=1,
            grid=(n,),
            in_specs=[
                pl.BlockSpec((2, rows, tile), lambda j, w: (0, 0, j)),
                gspec, gspec, uspec, uspec, full, full, full,
                small_spec(w_out[0].shape), small_spec(w_out[1].shape),
                small_spec(gains.shape), small_spec(mods.shape),
            ],
            out_specs=[full, full, full, small_spec((8, D))],
            scratch_shapes=[pltpu.VMEM((2, rows, half), jnp.float32)],
        ),
        out_shape=[jax.ShapeDtypeStruct((rows, D), jnp.float32)]
        + [jax.ShapeDtypeStruct((rows, D), jnp.bfloat16)] * 2
        + [jax.ShapeDtypeStruct((8, D), jnp.float32)],
        compiler_params=params(60),
        cost_estimate=cost(4 * rows * D * FF + 2 * rows * D * D, 55e6),
    )(
        which, dgu, w_gate_up[0], w_gate_up[1], w_gate_up[0], w_gate_up[1],
        middle, cotangent, o, w_out[0], w_out[1], gains, mods,
    )


def qk_back_kernel(own_blocks, parts, *refs):
    dq_refs, dk_refs, dv_refs = refs[:parts], refs[parts : 2 * parts], refs[2 * parts : 3 * parts]
    qpre_ref, kpre_ref, cos_ref, sin_ref, gain_ref, dqkv_ref, sum_ref = refs[3 * parts :]
    pid = pl.program_id(0)

    @pl.when(pid == 0)
    def clear():
        sum_ref[...] = jnp.zeros_like(sum_ref)

    def back(grad_refs, pre_ref, row):
        pre = pre_ref[...].astype(jnp.float32)
        grad = jnp.concatenate([g[...] for g in grad_refs], axis=1).astype(jnp.float32)
        grad = turn(grad, cos_ref[...], -sin_ref[...])
        d, terms = norm_back(grad, pre, rms_scale(pre), gain_ref[row : row + 1])
        add_row(sum_ref, row, terms)
        return d.astype(jnp.bfloat16)

    dqkv_ref[:, D : 2 * D] = back(dk_refs, kpre_ref, 2)
    width = D // parts
    for i, ref in enumerate(dv_refs):
        dqkv_ref[:, 2 * D + i * width : 2 * D + (i + 1) * width] = ref[...]

    @pl.when(pid < own_blocks)
    def with_query():
        dqkv_ref[:, :D] = back(dq_refs, qpre_ref, 1)

    @pl.when(pid >= own_blocks)
    def no_query():
        dqkv_ref[:, :D] = jnp.zeros((dqkv_ref.shape[0], D), jnp.bfloat16)


def qk_back(dq, dk, dv, qpre, kpre, cosine, sine, gains):
    own, rows = dq[0].shape[0], dk[0].shape[0]
    parts = len(dq)
    step = min(128, own)
    blocks = own // step
    row = lambda n: pl.BlockSpec((step, n), lambda i: (i, 0))
    own_row = lambda n: pl.BlockSpec((step, n), lambda i: (jnp.minimum(i, blocks - 1), 0))
    return pl.pallas_call(
        functools.partial(qk_back_kernel, blocks, parts),
        grid=(rows // step,),
        in_specs=[own_row(D // parts)] * parts + [row(D // parts)] * (2 * parts)
        + [own_row(D), row(D), row(PAIR), row(PAIR), small_spec(gains.shape)],
        out_specs=[row(3 * D), small_spec((8, D))],
        out_shape=[
            jax.ShapeDtypeStruct((rows, 3 * D), jnp.bfloat16),
            jax.ShapeDtypeStruct((8, D), jnp.float32),
        ],
        compiler_params=params(),
        cost_estimate=cost(60 * rows * D, 30e6),
    )(*dq, *dk, *dv, qpre, kpre, cosine, sine, gains)


def project_back_kernel(with_query, dqkv_ref, tok_ref, w_ref, gain_ref, mod_ref, dx_ref, sum_ref):
    @pl.when(pl.program_id(0) == 0)
    def clear():
        sum_ref[...] = jnp.zeros_like(sum_ref)

    first = 0 if with_query else D
    dhm = dot(dqkv_ref[:, first:], w_ref[:, first:], NT)
    x = tok_ref[...].astype(jnp.float32)
    r1 = rms_scale(x)
    add_row(sum_ref, 3, dhm)
    add_row(sum_ref, 4, dhm * (x * r1 * gain_ref[0:1]))
    dx, terms = norm_back(dhm * (1.0 + mod_ref[1:2]), x, r1, gain_ref[0:1])
    add_row(sum_ref, 0, terms)
    dx_ref[...] = dx.astype(jnp.bfloat16)


def project_back(dqkv, first, own, tokens, full_qkv, gains, mods):
    rows = dqkv.shape[0] - own if first else own
    step = min(256, own)
    skip = first // step
    row = pl.BlockSpec((step, D), lambda i: (i, 0))
    return pl.pallas_call(
        functools.partial(project_back_kernel, first == 0),
        grid=(max(rows // step, 1),),
        in_specs=[pl.BlockSpec((step, 3 * D), lambda i: (i + skip, 0)), row]
        + [pl.BlockSpec(full_qkv.shape, lambda i: (0, 0), pipeline_mode=pl.Buffered(1))]
        + [small_spec(gains.shape), small_spec(mods.shape)],
        out_specs=[pl.BlockSpec((step, D), lambda i: (i, 0)), small_spec((8, D))],
        out_shape=[
            jax.ShapeDtypeStruct((rows, D), jnp.bfloat16),
            jax.ShapeDtypeStruct((8, D), jnp.float32),
        ],
        compiler_params=params(),
        cost_estimate=cost(6 * rows * D * D, 30e6),
    )(dqkv, tokens, full_qkv, gains, mods)


def product_kernel(widths, has_received, where_ref, d_ref, a_ref, *refs):
    p = dot(d_ref[0], a_ref[...], TN)
    outs = refs[1:] if has_received else refs
    if has_received:
        p = p + refs[0][0].astype(jnp.float32)
    p = p.astype(jnp.bfloat16)
    start = 0
    for out, width in zip(outs, widths):
        out[0] = p[:, start : start + width]
        start += width


def product(dact, act, starts, lanes, received=None, widths=None):
    parts, tokens, columns = dact.shape
    count = len(starts)
    widths = list(widths or [lanes])
    tile = next(
        t for t in (2048, 1536, 1024, 512, 256, 128) if columns % t == 0 and t * lanes <= 2048 * 512
    )
    each = columns // tile
    spec = lambda w: pl.BlockSpec((1, tile, w), lambda n, k, s: (k, n, 0))
    return pl.pallas_call(
        functools.partial(product_kernel, widths, received is not None),
        grid_spec=pltpu.PrefetchScalarGridSpec(
            num_scalar_prefetch=1,
            grid=(parts * each, count),
            in_specs=[
                pl.BlockSpec((1, tokens, tile), lambda n, k, s: (n // each, 0, n % each)),
                pl.BlockSpec((tokens, lanes), lambda n, k, s: (0, s[k])),
            ]
            + ([] if received is None else [spec(lanes)]),
            out_specs=[spec(w) for w in widths],
        ),
        out_shape=[
            jax.ShapeDtypeStruct((count, parts * columns, w), jnp.bfloat16) for w in widths
        ],
        compiler_params=params(),
        cost_estimate=cost(
            2 * tokens * parts * columns * lanes * count, 4 * parts * columns * lanes * count
        ),
    )(jnp.stack(starts).astype(jnp.int32), dact, act, *([] if received is None else [received]))


def split_product_kernel(portions, count, where_ref, d_ref, *refs):
    acts, received, outs = refs[:count], refs[count], refs[count + 1 :]
    prods = [
        (dot(d_ref[0], acts[f][...], TN) + received[f].astype(jnp.float32)).astype(jnp.bfloat16)
        for f in range(count)
    ]
    half = prods[0].shape[0] // 2
    start = 0
    for i, (width, letter) in enumerate(portions):
        keep, send = outs[2 * i], outs[2 * i + 1]
        lanes = slice(start, start + width)
        start += width
        if letter == "y":
            keep[...] = prods[0][:, lanes]
            send[...] = prods[1][:, lanes]
        elif letter == "x":
            low = where_ref[count] == 0
            for f in range(count):
                a, b = prods[f][:half, lanes], prods[f][half:, lanes]
                keep[f] = jnp.where(low, a, b)
                send[f] = jnp.where(low, b, a)
        else:
            mine = pl.program_id(0) % 2 == where_ref[count + 1]

            @pl.when(mine)
            def to_keep(keep=keep, lanes=lanes):
                for f in range(count):
                    keep[f] = prods[f][:, lanes]

            @pl.when(jnp.logical_not(mine))
            def to_send(send=send, lanes=lanes):
                for f in range(count):
                    send[f] = prods[f][:, lanes]


def split_product(dact, act, starts, lanes, received, portions, bits, nd):
    parts, tokens, columns = dact.shape
    count = len(starts)
    total = parts * columns
    tile = 4 * (total // nd)
    each = columns // tile
    specs, shapes = [], []
    for width, letter in portions:
        if letter == "y":
            spec, shape = pl.BlockSpec((tile, width), lambda n, s: (n, 0)), (total, width)
        elif letter == "x":
            spec = pl.BlockSpec((count, tile // 2, width), lambda n, s: (0, n, 0))
            shape = (count, total // 2, width)
        else:
            spec = pl.BlockSpec((count, tile, width), lambda n, s: (0, n // 2, 0))
            shape = (count, total // 2, width)
        specs += [spec] * 2
        shapes += [jax.ShapeDtypeStruct(shape, jnp.bfloat16)] * 2
    act_spec = lambda f: pl.BlockSpec((tokens, lanes), lambda n, s: (0, s[f]))
    outs = pl.pallas_call(
        functools.partial(split_product_kernel, portions, count),
        grid_spec=pltpu.PrefetchScalarGridSpec(
            num_scalar_prefetch=1,
            grid=(total // tile,),
            in_specs=[pl.BlockSpec((1, tokens, tile), lambda n, s: (n // each, 0, n % each))]
            + [act_spec(f) for f in range(count)]
            + [pl.BlockSpec((count, tile, lanes), lambda n, s: (0, n, 0))],
            out_specs=specs,
        ),
        out_shape=shapes,
        compiler_params=params(),
        cost_estimate=cost(2 * tokens * total * lanes * count, 4 * total * lanes * count),
    )(jnp.stack(list(starts) + list(bits)).astype(jnp.int32), dact, *([act] * count), received)
    return list(zip(outs[::2], outs[1::2]))


ORDERS = ["yxz", "xzy", "zyx"]


def bits_of(size):
    return size.bit_length() - 1


def swap(value, axis, mask, size):
    return lax.ppermute(value, axis, [(i, i ^ mask) for i in range(size)])


def after(value, *earlier):
    return lax.optimization_barrier((value,) + earlier)[0]


def special(env):
    return env[1] == 2 and bits_of(env[0]) >= 3


class Pieces:
    def __init__(self, shard, first, chunk, route, flow):
        nd, nf, me, mine = flow.env
        self.flow, self.route, self.stack = flow, list(enumerate(route)), None
        rows = chunk >> len(route)
        index = sum(((me >> b) & 1) << i for i, b in enumerate(route))
        base = first + (mine ^ 1) * shard.shape[0]
        self.starts = [base + (index ^ rel) * rows for rel in range(1 << len(route))]
        part = lax.dynamic_slice_in_dim(shard, first + index * rows, rows, 0)
        flow.send(part[None], "fsdp", 1, self.land, 0)

    def land(self, got):
        held = [] if self.stack is None else [self.stack]
        if not self.route:
            self.pieces = held + [got]
            return
        self.stack = jnp.concatenate(held + [got]) if held else got
        if self.route:
            _, b = self.route.pop(0)
            self.flow.send(self.stack, "dp", 1 << b, self.land, 0)


def slice_for(shard, env):
    rows = shard.shape[0] // 8
    return lax.dynamic_slice_in_dim(shard, (env[2] & 7) * rows, rows, 0)


def gather_half(shard, got, env):
    nd = env[0]
    if not special(env):
        full = lax.all_gather(shard, "fsdp", axis=0, tiled=True)
        half = full.shape[0] // 2
        return (full[:half], full[half:])
    groups = [list(range(i, i + 8)) for i in range(0, nd, 8)]
    return (shard, lax.all_gather(got, "dp", axis=0, tiled=True, axis_index_groups=groups))


def gather_relative(value, env):
    nf = env[1]
    blocks = [value]
    for b in range(bits_of(nf)):
        blocks = blocks + [swap(p, "fsdp", 1 << b, nf) for p in blocks]
    return jnp.concatenate(blocks, axis=0)


def reduce_relative(value, env):
    nf = env[1]
    total = None
    for b in reversed(range(bits_of(nf))):
        half = value.shape[0] // 2
        got = swap(value[half:], "fsdp", 1 << b, nf)
        total = value[:half].astype(jnp.float32) + got.astype(jnp.float32)
        value = total.astype(jnp.bfloat16)
    return value.astype(jnp.float32) if total is None else total


def sum_fsdp(value, env, anchor=None):
    nf = env[1]
    for b in range(bits_of(nf)):
        got = swap(value.astype(jnp.bfloat16), "fsdp", 1 << b, nf)
        if anchor is not None:
            got = after(got, anchor)
        value = value + got.astype(jnp.float32)
    return value


def side_by_side(own, got, mine):
    first = mine == 0
    return jnp.concatenate([jnp.where(first, own, got), jnp.where(first, got, own)], axis=1)


def stages_of(order, env):
    kinds = {
        "y": [("fsdp", b) for b in range(bits_of(env[1]))],
        "x": [("dp", 1)],
        "z": [("dp", 2)] if bits_of(env[0]) > 2 else [],
    }
    return [stage for letter in order for stage in kinds[letter]]


def add_low(terms):
    total = terms[0].astype(jnp.float32)
    for term in terms[1:]:
        total = total + term.astype(jnp.float32)
    return total.astype(jnp.bfloat16)


class Flow:
    most = 5

    def __init__(self, env):
        self.env, self.pending, self.flying = env, [], []
        self.mark = jnp.zeros((8, 128), jnp.float32)

    def send(self, operand, axis, mask, land, rank, windows=1):
        self.pending.append((operand, axis, mask, land, rank, windows))

    def turn(self, outs, ins):
        nd, nf = self.env[:2]
        landing = [(got, land) for got, land, left in self.flying if left == 1]
        self.flying = [(got, land, left - 1) for got, land, left in self.flying if left > 1]
        if landing:
            gots = tuple(got for got, _ in landing)
            tied = lax.optimization_barrier(gots + tuple(outs) + (self.mark,))
            self.mark = tied[-1]
            for got, (_, land) in zip(tied, landing):
                land(got)
        pending = sorted(self.pending, key=lambda p: p[4])
        pending, self.pending = pending[: self.most - len(self.flying)], pending[self.most - len(self.flying) :]
        sends = tuple(p[0] for p in pending)
        tied = lax.optimization_barrier(sends + tuple(ins) + tuple(outs) + (self.mark,))
        self.mark = tied[-1]
        for operand, (_, axis, mask, land, _, windows) in zip(tied, pending):
            size = nd if axis == "dp" else nf
            self.flying.append((swap(operand, axis, mask, size), land, windows))
        return tied[len(sends) : len(sends) + len(ins)]

    def drain(self, outs):
        while self.flying or self.pending:
            self.turn(outs, ())
            outs = ()


class Ladder:
    def __init__(self, current, alive, stages, env):
        self.current, self.alive, self.stages, self.env = current, alive, stages, env
        self.sent = None

    def split(self, axis, b):
        t = self.current
        if axis == "fsdp":
            pairs = t.reshape((t.shape[0] // 2, 2) + t.shape[1:])
            return pairs[:, 0], pairs[:, 1]
        place = 1 + self.alive.index(b)
        bit = (self.env[2] >> b) & 1
        self.alive = [d for d in self.alive if d != b]
        before, after_dims = t.shape[:place], t.shape[place + 1 :]
        rows = 1
        for n in after_dims[:-1]:
            rows *= n
        count = 1
        for n in before:
            count *= n
        flat = t.reshape(count, 2, rows, t.shape[-1])
        pick = lambda i: lax.dynamic_index_in_dim(flat, i, 1, keepdims=False).reshape(
            before + after_dims
        )
        return pick(bit), pick(bit ^ 1)

    def launch(self, flow, landed, rank, windows=1):
        axis, b = self.stages.pop(0)
        if self.sent is None:
            kept, send = self.split(axis, b)
        else:
            kept, send, self.sent = self.current, self.sent, None

        def land(got):
            self.current = add_low([kept, got.reshape(kept.shape)])
            landed()

        flow.send(send, axis, 1 << b, land, rank, windows)


def join_rows(kept, got, env):
    core = env[2] & 1
    both = jnp.where(
        core == 0,
        jnp.concatenate([kept, got], axis=1),
        jnp.concatenate([got, kept], axis=1),
    )
    return both.T.astype(jnp.float32)


def core_product(dact, act, core, env, rows_only, received=None, widths=None):
    nd, nf, me, mine = env
    count = 1 if rows_only else nf
    lanes = act.shape[1] // (2 * count)
    blocks = [core] if rows_only else [2 * (mine ^ r) + core for r in range(nf)]
    if lanes % 128 == 0:
        outs = product(dact, act, blocks, lanes, received, widths)
        return outs if widths else outs[0]
    wide = jnp.concatenate(list(dact), axis=1)
    parts = [lax.dynamic_slice_in_dim(act, b * lanes, lanes, 1) for b in blocks]
    out = jnp.stack([dot(wide, p, TN) for p in parts])
    if received is not None:
        out = out + received.astype(jnp.float32)
    out = out.astype(jnp.bfloat16)
    if widths is None:
        return out
    cuts = [sum(widths[:i]) for i in range(len(widths))]
    return [out[:, :, a : a + w] for a, w in zip(cuts, widths)]


class Reduction:
    def __init__(self, dact, act, portions, flow, rank, rows_only=False, last_windows=1):
        self.windows, self.last_windows = 1, last_windows
        self.flow, self.env, self.act, self.rank = flow, flow.env, act, rank
        self.portions, self.rows_only = portions, rows_only
        core = self.env[2] & 1
        self.partial = core_product(dact, act, core ^ 1, self.env, rows_only)
        flow.send(self.partial, "dp", 1, self.receive, 0)

    def receive(self, got):
        self.sent = got

    def keep(self, dact):
        nd, nf, me, mine = self.env
        core, bits = me & 1, bits_of(nd)
        alive = list(range(bits - 1, 0, -1))
        tail = (2, self.sent.shape[1] // nd)
        self.ladders = []
        if special(self.env):
            count = 1 if self.rows_only else nf
            blocks = [core] if self.rows_only else [2 * (mine ^ r) + core for r in range(nf)]
            pairs = split_product(
                dact, self.act, blocks, self.act.shape[1] // (2 * count), self.sent,
                [(w, order[0]) for w, order in self.portions], [(me >> 1) & 1, (me >> 2) & 1], nd,
            )
            for (kept, sent), (_, order) in zip(pairs, self.portions):
                stages = stages_of(order, self.env)
                axis, b = stages[0]
                left = [d for d in alive if axis != "dp" or d != b]
                lead = 1 if axis == "fsdp" else count
                shape = (lead,) + (2,) * len(left) + tail + (kept.shape[-1],)
                ladder = Ladder(kept.reshape(shape), left, stages, self.env)
                ladder.sent = sent
                self.ladders.append(ladder)
            first = pairs[0][0]
        else:
            widths = [w for w, _ in self.portions]
            totals = core_product(dact, self.act, core, self.env, self.rows_only, self.sent, widths)
            for total, (_, order) in zip(totals, self.portions):
                shape = (total.shape[0],) + (2,) * (bits - 1) + tail + (total.shape[2],)
                stages = stages_of(order, self.env)
                self.ladders.append(Ladder(total.reshape(shape), alive, stages, self.env))
            first = totals[0]
        self.launch()
        return first

    def launch(self):
        ladders = self.ladders
        if ladders[0].stages:
            self.waiting = len(ladders)
            for ladder in ladders:
                ladder.launch(self.flow, self.landed, self.rank, self.windows)
            return
        if len(ladders) > 1:
            joined = jnp.concatenate([r.current for r in ladders], axis=-1)
            self.ladders = ladders = [Ladder(joined, ladders[0].alive, [], self.env)]
        if ladders[0].alive:
            ladders[0].stages = [("dp", ladders[0].alive[-1])]
            self.windows = self.last_windows
            self.launch()
            return
        core = self.env[2] & 1
        rows = ladders[0].current[0]
        kept = lax.dynamic_index_in_dim(rows, core, 0, keepdims=False)

        def land(got):
            self.result = join_rows(kept, got, self.env)

        sent = lax.dynamic_index_in_dim(rows, core ^ 1, 0, keepdims=False)
        self.flow.send(sent, "dp", 1, land, 3)

    def landed(self):
        self.waiting -= 1
        if not self.waiting:
            self.launch()


class WideSum:
    def __init__(self, value, groups, flow, rank):
        self.value, self.flow, self.rank, self.groups = value, flow, rank, list(groups)
        self.passed = []
        self.launch()

    def launch(self):
        self.passed.append(self.value)
        if self.groups:
            axis, masks = self.groups.pop(0)
            self.waiting, self.total = len(masks), self.value.astype(jnp.float32)
            for mask in masks:
                self.flow.send(self.value, axis, mask, self.land, self.rank)

    def land(self, got):
        self.total = self.total + got.astype(jnp.float32)
        self.waiting -= 1
        if not self.waiting:
            self.value = self.total.astype(got.dtype)
            self.launch()


def hops(axis, size):
    return [(axis, [1 << b]) for b in range(bits_of(size))]


def portion_list(lanes, names):
    units = lanes // 128
    if lanes % 128 or units < len(names):
        return [(lanes, names[-1])]
    cuts = [units * i // len(names) * 128 for i in range(len(names) + 1)]
    return [(b - a, n) for a, b, n in zip(cuts, cuts[1:], names)]


def per_device(
    tokens,
    caption,
    modulation,
    caption_mask,
    positions,
    w_qkv,
    w_out,
    w_caption_kv,
    w_gate_up,
    w_down,
    norm_gains,
    caption_gain,
    cross_gate,
    cotangent,
):
    nd, nf = lax.axis_size("dp"), lax.axis_size("fsdp")
    me, mine = lax.axis_index("dp"), lax.axis_index("fsdp")
    env = (nd, nf, me, mine)
    own_rows = tokens.shape[1]
    heads = cross_gate.shape[0]
    which = (mine if special(env) else jnp.int32(0)).astype(jnp.int32)[None]
    pack = jnp.concatenate(
        [
            norm_gains,
            modulation[0],
            caption_gain[None],
            jnp.pad(cross_gate, (0, caption_gain.shape[0] - heads))[None],
        ]
    )
    flow = Flow(env)
    if special(env):
        landed = {}
        keep_as = lambda name: functools.partial(landed.__setitem__, name)
        half = w_qkv.shape[0] // 2
        gathers = [Pieces(w_qkv, 0, half, (1, 2, 0), flow), Pieces(w_qkv, half, half, (2, 1, 0), flow)]
        flow.send(pack, "fsdp", 1, keep_as("pack"), 0)
        flow.send(positions[0].T, "fsdp", 1, keep_as("places"), 0)
        flow.turn((), ())
        flow.send(slice_for(w_gate_up, env), "fsdp", 1, keep_as("gate_up"), 0)
        (caption_in,) = flow.turn((), (caption[0],))
        pack = side_by_side(pack, landed["pack"], mine)
        places = jnp.concatenate([positions[0].T, landed["places"]])
        partial_kv = dot(caption_in, w_caption_kv)
        flow.send(tokens[0], "fsdp", 1, keep_as("tokens"), 0)
        (places,) = flow.turn((partial_kv,), (places,))
        full_gate_up = gather_half(w_gate_up, landed["gate_up"], env)
        cosine, sine = rope_tables(places)
        flow.turn((cosine, sine), ())
        flow.turn((), ())
        tokens_other = landed["tokens"]
        flow.send(partial_kv.astype(jnp.bfloat16), "fsdp", 1, keep_as("caption"), 0)
        flow.send(slice_for(w_out, env), "fsdp", 1, keep_as("out"), 0)
        pieces = [p for g in gathers for p in g.pieces]
        starts = [mine * w_qkv.shape[0]] + [s for g in gathers for s in g.starts]
        gath_qkv = (w_qkv, pieces, starts)
        (tokens_other,) = flow.turn((), (tokens_other,))
    else:
        pack = lax.all_gather(pack, "fsdp", axis=1, tiled=True)
        cosine, sine = rope_tables(gather_relative(positions[0].T, env))
        full = lax.all_gather(w_qkv, "fsdp", axis=0, tiled=True)
        half = full.shape[0] // 2
        gath_qkv = (full[:half], [full[half:][None]], [jnp.int32(0), jnp.int32(half)])
        tokens_other = gather_relative(tokens[0], env)[own_rows:]
        partial_kv = dot(caption[0], w_caption_kv)
        full_gate_up = gather_half(w_gate_up, None, env)
    pack = pack.astype(jnp.float32)
    gains, mods, cap_gain = pack[:6], pack[6:12], pack[12]
    gate_heads = jnp.tanh(pack[13].reshape(nf, -1)[:, :heads].reshape(HEADS))
    gate_tanh = jnp.repeat(gate_heads, HEAD_DIM)[None]
    bias = jnp.where(caption_mask[0] > 0, 0.0, -1e30).astype(jnp.float32)
    hm, full_qkv, query_b, key_b, value_b, query_pre, key_pre = project(
        tokens[0], tokens_other, gains, mods, cosine, sine, gath_qkv
    )
    if special(env):
        (query_b,) = flow.turn((hm,), (query_b,))
        cap_rows = partial_kv + landed["caption"].astype(jnp.float32)
        full_out = gather_half(w_out, after(landed["out"], full_gate_up[1]), env)
        flow.send(slice_for(w_down, env), "fsdp", 1, keep_as("down"), 0)
        (query_b,) = flow.turn((), (query_b,))
    else:
        cap_rows = sum_fsdp(partial_kv, env)
        full_out = gather_half(w_out, None, env)
    ckey_pre = cap_rows[:, :D]
    ckey_scale = rms_scale(ckey_pre)
    ckey_b = (ckey_pre * ckey_scale * cap_gain).astype(jnp.bfloat16)
    cvalue_b = cap_rows[:, D:].astype(jnp.bfloat16)
    combined, self_out, cross_out, stats = attend(
        query_b, key_b, value_b, ckey_b, cvalue_b, bias[None], gate_tanh
    )
    if special(env):
        (combined,) = flow.turn((stats,), (combined,))
        full_down = gather_half(w_down, landed["down"], env)
    else:
        full_down = gather_half(w_down, None, env)
    projected, middle, ffn_in = output_step(which, combined, full_out, tokens[0], gains, mods)
    gate_part, up_part, ffn_inner = gate_up_step(which, ffn_in, full_gate_up)
    block_out, grad_down, down_sums = down_step(
        which, ffn_inner, full_down, middle, cotangent[0], gains, mods
    )
    lanes_d, lanes_f = D // (2 * nf), FF // (2 * nf)
    red_down = Reduction(grad_down[None], ffn_inner, portion_list(lanes_f, ORDERS), flow, 1)
    (grad_down_b,) = flow.turn((red_down.partial,), (grad_down,))
    dgu = gate_up_back(which, grad_down_b, gate_part, up_part, full_down)
    (grad_down_b,) = flow.turn((dgu,), (grad_down_b,))
    done = red_down.keep(grad_down_b[None])
    (dgu,) = flow.turn((done,), (dgu,))
    red_gate_up = Reduction(dgu, ffn_in, portion_list(lanes_d, ORDERS), flow, 1)
    (dgu_b,) = flow.turn((red_gate_up.partial,), (dgu,))
    grad_mid, grad_proj, grad_comb, ffn_sums = ffn_back(
        which, dgu_b, full_gate_up, full_out, middle, cotangent[0], projected, gains, mods
    )
    grad_comb, grad_proj = flow.turn((ffn_sums,), (grad_comb, grad_proj))
    dq_cross, grad_ckey, grad_cvalue, gate_sums = cross_back(
        query_b, ckey_b, cvalue_b, bias[:, None], gate_tanh, stats, grad_comb, cross_out
    )
    gate_terms = gate_sums[0].reshape(HEADS, HEAD_DIM).sum(axis=-1) * (1.0 - gate_heads**2)
    grad_ckey_pre, cap_gain_terms = norm_back(
        grad_ckey.astype(jnp.float32), ckey_pre, ckey_scale, cap_gain
    )
    grad_cap_kv = jnp.concatenate([grad_ckey_pre, grad_cvalue.astype(jnp.float32)], axis=-1)
    cap_sum = WideSum(grad_cap_kv.astype(jnp.bfloat16), hops("fsdp", nf), flow, 0)
    red_out = Reduction(grad_proj[None], combined, portion_list(lanes_d, ORDERS[2:]), flow, 1.5)
    dgu_b, grad_comb = flow.turn((gate_sums, red_out.partial), (dgu_b, grad_comb))
    done = red_gate_up.keep(dgu_b)
    pairs = D // PAIR
    each = pairs // 4
    parts = []

    def attention_part(grads):
        parts.append(
            self_back(query_b, key_b, value_b, stats, grads, self_out, dq_cross, len(parts) * each, each)
        )
        return parts[-1][0]

    first = attention_part(grad_comb)
    while nf > 2 and cap_sum.groups:
        flow.turn((done,), ())
    grad_comb, grad_proj = flow.turn((done, first), (grad_comb, grad_proj))
    grad_cap_kv = cap_sum.value
    red_caption = Reduction(
        grad_cap_kv[None], caption[0], portion_list(caption.shape[2] // 2, ["xz", "zx"]), flow, 1.2, True, 1
    )
    out_done = red_out.keep(grad_proj[None])
    dones = [attention_part(grad_comb) for _ in range(3)]
    grad_query, grad_key, grad_value = zip(*parts)
    (dq0,) = flow.turn([red_caption.partial, out_done] + dones, (grad_query[0],))
    grad_query = (dq0,) + grad_query[1:]
    grad_mixed, qk_sums = qk_back(
        grad_query, grad_key, grad_value, query_pre, key_pre, cosine, sine, gains
    )
    red_qkv = Reduction(grad_mixed[None], hm, portion_list(lanes_d, ORDERS), flow, 0.5)
    dx_other, other_sums = project_back(
        after(grad_mixed, red_qkv.partial), own_rows, own_rows, tokens_other, full_qkv, gains, mods
    )
    grad_mixed, grad_cap_kv = flow.turn((red_qkv.partial, other_sums), (grad_mixed, grad_cap_kv))
    done = red_caption.keep(grad_cap_kv[None])
    dx_got = []
    if nf == 2:
        flow.send(dx_other, "fsdp", 1, dx_got.append, 0)
    (grad_mixed,) = flow.turn((done,), (grad_mixed,))
    done = red_qkv.keep(grad_mixed[None])
    dx_own, own_sums = project_back(grad_mixed, 0, own_rows, tokens[0], full_qkv, gains, mods)
    project_sums = own_sums + other_sums if nf > 1 else own_sums
    small = jnp.concatenate(
        [
            project_sums[:1],
            qk_sums[1:3],
            jnp.stack(
                [
                    ffn_sums[4],
                    ffn_sums[2],
                    down_sums[1],
                    jnp.sum(cap_gain_terms, axis=0),
                    jnp.pad(gate_terms, (0, D - HEADS)),
                ]
            ),
        ]
    )
    mod_grads = jnp.stack(
        [
            project_sums[3],
            project_sums[4],
            ffn_sums[3] * (1.0 - jnp.tanh(mods[2]) ** 2),
            ffn_sums[0],
            ffn_sums[1],
            down_sums[0] * (1.0 - jnp.tanh(mods[5]) ** 2),
        ]
    )
    along = hops("dp", nd)
    if special(env):
        along = along[2:] + [("dp", [1, 2, 3])]
    small = jnp.concatenate([small, mod_grads, jnp.zeros((2, D), jnp.float32)])
    small_sum = WideSum(small, hops("fsdp", nf) + along, flow, 1.3)
    (grad_cap_kv,) = flow.turn((done, own_sums), (grad_cap_kv,))
    if nf == 2:
        dx = dx_own.astype(jnp.float32) + dx_got[0].astype(jnp.float32)
    else:
        dx = reduce_relative(jnp.concatenate([dx_own, dx_other]) if nf > 1 else dx_own, env)
    grad_tokens = (grad_mid + dx).astype(jnp.bfloat16)
    grad_caption = dot(grad_cap_kv, w_caption_kv, NT).astype(jnp.bfloat16)
    flow.drain((grad_caption, grad_tokens))
    small, mod_grads = small_sum.value, small_sum.passed[bits_of(nf)][8:14]
    out_down, out_gate_up, out_out, out_caption, out_qkv = (
        r.result for r in (red_down, red_gate_up, red_out, red_caption, red_qkv)
    )
    width = D // nf
    return (
        block_out[None],
        grad_tokens[None],
        grad_caption[None],
        lax.dynamic_slice_in_dim(mod_grads, mine * width, width, 1)[None],
        out_qkv,
        out_out,
        out_caption,
        out_gate_up,
        out_down,
        lax.dynamic_slice_in_dim(small[:6], mine * width, width, 1),
        lax.dynamic_slice_in_dim(small[6], mine * width, width, 0),
        lax.dynamic_slice_in_dim(small[7], mine * heads, heads, 0),
    )


def solution(mesh):
    placed = (
        P("dp", "fsdp", None),
        P("dp", None, "fsdp"),
        P("dp", None, "fsdp"),
        P("dp", None),
        P("dp", None, "fsdp"),
        P("fsdp", None),
        P("fsdp", None),
        P("fsdp", None),
        P("fsdp", None),
        P("fsdp", None),
        P(None, "fsdp"),
        P("fsdp"),
        P("fsdp"),
        P("dp", "fsdp", None),
    )
    return jax.shard_map(
        per_device,
        mesh=mesh,
        in_specs=placed,
        out_specs=(
            P("dp", "fsdp", None),
            P("dp", "fsdp", None),
            P("dp", None, "fsdp"),
            P("dp", None, "fsdp"),
            P("fsdp", "dp"),
            P("fsdp", "dp"),
            P("fsdp", "dp"),
            P("fsdp", "dp"),
            P("fsdp", "dp"),
            P(None, "fsdp"),
            P("fsdp"),
            P("fsdp"),
        ),
        check_vma=False,
    )
```
